32 devices in a mesh: dp: 8 (over y, x, core), seq: 4 (over z).
Axes of the slice: x: 2, y: 2, z: 4, core: 2. Of those that a mesh axis runs over, the one named last changes fastest.
Arguments:
- clips: float32 [24, 512, 1024], P('dp', 'seq'), may hold values from -6 to 6
- counts: int32 [8], P('dp'), may hold values from 1 to 3, as said below
- out_cotangent: float32 [24, 512, 1024], P('dp', 'seq'), may hold values from -6 to 6
- norm1_gain: float32 [1024], P(('dp', 'seq')), may hold values from 0.5 to 1.5
- norm1_shift: float32 [1024], P(('dp', 'seq')), may hold values from -1 to 1
- qkv_weight: float32 [3145728], P(('dp', 'seq')), may hold values from -0.1875 to 0.1875
- query_bias: float32 [1024], P(('dp', 'seq')), may hold values from -3 to 3
- value_bias: float32 [1024], P(('dp', 'seq')), may hold values from -0.26516503 to 0.26516503
- proj_weight: float32 [1048576], P(('dp', 'seq')), may hold values from -2.5 to 2.5
- proj_bias: float32 [1024], P(('dp', 'seq')), may hold values from -1 to 1
- norm2_gain: float32 [1024], P(('dp', 'seq')), may hold values from 0.5 to 1.5
- norm2_shift: float32 [1024], P(('dp', 'seq')), may hold values from -1 to 1
- up_weight: float32 [4194304], P(('dp', 'seq')), may hold values from -0.1875 to 0.1875
- up_bias: float32 [4096], P(('dp', 'seq')), may hold values from -3 to 3
- down_weight: float32 [4194304], P(('dp', 'seq')), may hold values from -0.09375 to 0.09375
- down_bias: float32 [1024], P(('dp', 'seq')), may hold values from -1 to 1
Outputs:
- block_out: float32 [24, 512, 1024], P('dp', 'seq')
- input_grad: float32 [24, 512, 1024], P('dp', 'seq')
- norm1_gain_grad: float32 [1024], P(('dp', 'seq'))
- norm1_shift_grad: float32 [1024], P(('dp', 'seq'))
- qkv_weight_grad: float32 [3145728], P(('dp', 'seq'))
- query_bias_grad: float32 [1024], P(('dp', 'seq'))
- value_bias_grad: float32 [1024], P(('dp', 'seq'))
- proj_weight_grad: float32 [1048576], P(('dp', 'seq'))
- proj_bias_grad: float32 [1024], P(('dp', 'seq'))
- norm2_gain_grad: float32 [1024], P(('dp', 'seq'))
- norm2_shift_grad: float32 [1024], P(('dp', 'seq'))
- up_weight_grad: float32 [4194304], P(('dp', 'seq'))
- up_bias_grad: float32 [4096], P(('dp', 'seq'))
- down_weight_grad: float32 [4194304], P(('dp', 'seq'))
- down_bias_grad: float32 [1024], P(('dp', 'seq'))
The draws below stay inside these ranges and needn't reach their ends.
Inputs may be any that keep to these rules, and one draw needn't show every extreme that they name: `counts`: some data group holds 3 clips and another holds 1.
All inputs are finite; a program needn't handle non-finite values.
Results may differ from the reference program's by a relative error of at most 0.03.
Values may be sent and summed in bfloat16 or wider, within the bound.
A program may use at most 256 MiB of HBM per device.

```python
import jax
import jax.numpy as jnp
from jax import lax

D = 1024
FF = 4096
HEADS = 16
HEAD_DIM = 64
MB = 3
CLIP = 512
SLOTS = 24
N_DP = 8


def draw_counts(key, part):
    key = jax.random.fold_in(key, 7)
    first_key, second_key, third_key = jax.random.split(key, 3)
    counts = jax.random.randint(first_key, (N_DP,), 1, MB + 1)
    busiest = jax.random.randint(second_key, (), 0, N_DP)
    lightest = (busiest + jax.random.randint(third_key, (), 1, N_DP)) % N_DP
    counts = counts.at[busiest].set(MB).at[lightest].set(1)
    return counts.astype(jnp.int32)


def levels(rng, dims, pieces, least, largest):
    level = 1.0
    for axis_at, blocks in pieces:
        steps = jax.random.uniform(jax.random.fold_in(jax.random.fold_in(rng, 6), axis_at), (blocks,), jnp.float32, least / len(pieces), largest / len(pieces))
        level = level * jnp.repeat(jnp.exp(steps), dims[axis_at] // blocks).reshape((-1,) + (1,) * (len(dims) - 1 - axis_at))
    return level


def bell_draw(own_key, dims, width, reach, pieces=(), kind=jnp.bfloat16):
    values = width * jax.random.normal(own_key, dims, jnp.float32)
    if pieces:
        values = values * levels(own_key, dims, pieces, -0.22, 0.18)
    return jnp.clip(values, -reach, reach).astype(kind)


def setup_inputs(seed: int = 0) -> dict:
    streams_of = jax.random.split(jax.random.key(seed), 17)
    clips = bell_draw(streams_of[0], (SLOTS, CLIP, D), 1.0, 6.0, ((0, 8), (1, 4)), jnp.float32)
    counts = draw_counts(jax.random.fold_in(streams_of[16], 71), 0)
    out_cotangent = bell_draw(streams_of[2], (SLOTS, CLIP, D), 1.0, 6.0, ((0, 8), (1, 4)), jnp.float32)
    norm1_gain = jnp.clip(1.0 + 0.1 * jax.random.normal(streams_of[3], (D,), jnp.float32), 0.5, 1.5)
    norm1_shift = bell_draw(streams_of[4], (D,), 0.2, 1.0, ((0, 32),), jnp.float32)
    qkv_weight = bell_draw(streams_of[5], (3 * D * D,), D ** -0.5, 0.1875, ((0, 32),), jnp.float32)
    query_bias = bell_draw(streams_of[6], (D,), 0.5, 3.0, ((0, 32),), jnp.float32)
    value_bias = bell_draw(streams_of[7], (D,), (CLIP ** -0.5), 0.26516503, ((0, 32),), jnp.float32)
    proj_weight = bell_draw(streams_of[8], (D * D,), (max(1, 3 * D // CLIP)) ** -0.5, 2.5, ((0, 32),), jnp.float32)
    proj_bias = bell_draw(streams_of[9], (D,), 0.2, 1.0, ((0, 32),), jnp.float32)
    norm2_gain = jnp.clip(1.0 + 0.1 * jax.random.normal(streams_of[10], (D,), jnp.float32), 0.5, 1.5)
    norm2_shift = bell_draw(streams_of[11], (D,), 0.2, 1.0, ((0, 32),), jnp.float32)
    up_weight = bell_draw(streams_of[12], (D * FF,), D ** -0.5, 0.1875, ((0, 32),), jnp.float32)
    up_bias = bell_draw(streams_of[13], (FF,), 0.5, 3.0, ((0, 32),), jnp.float32)
    down_weight = bell_draw(streams_of[14], (FF * D,), FF ** -0.5, 0.09375, ((0, 32),), jnp.float32)
    down_bias = bell_draw(streams_of[15], (D,), 0.2, 1.0, ((0, 32),), jnp.float32)
    return {"clips": clips, "counts": counts, "out_cotangent": out_cotangent, "norm1_gain": norm1_gain, "norm1_shift": norm1_shift, "qkv_weight": qkv_weight, "query_bias": query_bias, "value_bias": value_bias, "proj_weight": proj_weight, "proj_bias": proj_bias, "norm2_gain": norm2_gain, "norm2_shift": norm2_shift, "up_weight": up_weight, "up_bias": up_bias, "down_weight": down_weight, "down_bias": down_bias}


EPSILON = 1e-05
HIGH = lax.Precision.HIGHEST

@jax.custom_vjp
def low(v):
    return lax.optimization_barrier(v.astype(jnp.bfloat16)).astype(jnp.float32)

@jax.custom_vjp
def low_back(v):
    return v

def low_keep(v):
    return (low(v), None)

def low_pass(kept, grad):
    return (grad,)

def back_keep(v):
    return (v, None)

def back_low(kept, grad):
    return (low(grad),)
low.defvjp(low_keep, low_pass)
low_back.defvjp(back_keep, back_low)

def layer_norm(values, gain_vec, shift_vec):
    center = values - lax.optimization_barrier(jnp.mean(values, axis=-1, keepdims=True))
    spread = lax.optimization_barrier(jnp.mean(center * center, axis=-1, keepdims=True))
    return center * lax.rsqrt(spread + EPSILON) * gain_vec + shift_vec

def shaped_weights(flat_list):
    return (flat_list[0], flat_list[1], flat_list[2].reshape(D, 3 * D), flat_list[3], flat_list[4], flat_list[5].reshape(D, D), flat_list[6], flat_list[7], flat_list[8], flat_list[9].reshape(D, FF), flat_list[10], flat_list[11].reshape(FF, D), flat_list[12])

def clip_forward(inputs, weights):
    gain_first, shift_first, qkv_matrix, query_shift, value_shift, proj_matrix, proj_shift, gain_second, shift_second, up_matrix, up_shift, down_matrix, down_shift = weights
    length = inputs.shape[0]
    normed_first = low(layer_norm(inputs, gain_first, shift_first))
    projected = jnp.dot(normed_first, qkv_matrix, precision=HIGH)
    queries = low(low_back(projected[:, :D] + query_shift))
    keys_all = low(low_back(projected[:, D:2 * D]))
    values_all = low(low_back(projected[:, 2 * D:] + value_shift))
    query_heads = queries.reshape(length, HEADS, HEAD_DIM)
    key_heads = keys_all.reshape(length, HEADS, HEAD_DIM)
    value_heads = values_all.reshape(length, HEADS, HEAD_DIM)
    scores = low_back(jnp.einsum('qhd,khd->hqk', query_heads, key_heads, precision=HIGH) * HEAD_DIM ** (-0.5))
    softened = low(jax.nn.softmax(scores, axis=-1))
    mixed_heads = jnp.einsum('hqk,khd->qhd', softened, value_heads, precision=HIGH)
    attended = low(low_back(mixed_heads.reshape(length, D)))
    middle = inputs + low_back(jnp.dot(attended, proj_matrix, precision=HIGH) + proj_shift)
    normed_second = low(layer_norm(middle, gain_second, shift_second))
    upper_part = low_back(jnp.dot(normed_second, up_matrix, precision=HIGH) + up_shift)
    hidden = low(jax.nn.gelu(upper_part, approximate=False))
    return middle + low_back(jnp.dot(hidden, down_matrix, precision=HIGH) + down_shift)

def reference(clips, counts, out_cotangent, norm1_gain, norm1_shift, qkv_weight, query_bias, value_bias, proj_weight, proj_bias, norm2_gain, norm2_shift, up_weight, up_bias, down_weight, down_bias):
    slot_index = jnp.arange(SLOTS, dtype=jnp.int32)
    living = (slot_index % MB < counts[slot_index // MB]).astype(jnp.float32)[:, None, None]
    params = (norm1_gain, norm1_shift, qkv_weight, query_bias, value_bias, proj_weight, proj_bias, norm2_gain, norm2_shift, up_weight, up_bias, down_weight, down_bias)
    params = tuple((parameter.astype(jnp.float32) for parameter in params))

    def forward(inputs, flat_list):
        weights = shaped_weights(tuple((low(parameter) for parameter in flat_list)))

        def one_clip(carry, single):
            return (carry, clip_forward(single, weights))
        unused, results = lax.scan(jax.checkpoint(one_clip), jnp.float32(0.0), inputs)
        return results
    block_out, backward = jax.vjp(forward, clips.astype(jnp.float32), params)
    input_grad, grads = backward(out_cotangent.astype(jnp.float32) * living)
    return (block_out * living, input_grad, grads[0], grads[1], grads[2], grads[3], grads[4], grads[5], grads[6], grads[7], grads[8], grads[9], grads[10], grads[11], grads[12])
```

```python
import functools

import jax
import jax.numpy as jnp
from jax import lax
from jax.experimental import pallas as pl
from jax.experimental.pallas import tpu as pltpu
from jax.sharding import PartitionSpec as P

D = 1024
FF = 4096
HEADS = 16
HEAD_DIM = 64
EPSILON = 1e-05
LANES = 128
BF = jnp.bfloat16
F32 = jnp.float32
AXES = ("dp", "seq")
RING = (0, 1, 3, 2)


def dot(a, b):
    return jnp.dot(a, b, preferred_element_type=F32)


def dot_nt(a, b):
    return lax.dot_general(a, b, (((1,), (1,)), ((), ())), preferred_element_type=F32)


def dot_tn(a, b):
    return lax.dot_general(a, b, (((0,), (0,)), ((), ())), preferred_element_type=F32)


def soft_t(q2, k_half):
    scores = dot_nt(k_half, q2) * (HEAD_DIM**-0.5)
    top = jnp.max(scores, axis=0, keepdims=True)
    e = jnp.exp(scores - top)
    return e * (1.0 / jnp.sum(e, axis=0, keepdims=True))


def attend_kernel(q_ref, k_ref, v_ref, o_ref):
    q2, k2, v2 = q_ref[...], k_ref[...], v_ref[...]
    low = lax.broadcasted_iota(jnp.int32, k2.shape, 1) < HEAD_DIM
    v_t = v2.T
    zero = jnp.zeros_like(k2)
    parts = []
    for h in range(2):
        k_half = jnp.where(low == (h == 0), k2, zero)
        p_t = soft_t(q2, k_half).astype(BF)
        parts.append(dot(v_t[h * HEAD_DIM : (h + 1) * HEAD_DIM], p_t))
    o_ref[...] = jnp.concatenate(parts, axis=0).T.astype(BF)


def attend(qkv):
    t = qkv.shape[0]
    n = D // LANES
    spec = lambda off: pl.BlockSpec((t, LANES), lambda h: (0, off + h))
    return pl.pallas_call(
        attend_kernel,
        grid=(n,),
        out_shape=jax.ShapeDtypeStruct((t, D), BF),
        in_specs=[spec(0), spec(n), spec(2 * n)],
        out_specs=spec(0),
        compiler_params=pltpu.CompilerParams(vmem_limit_bytes=48 * 2**20),
        cost_estimate=pl.CostEstimate(
            flops=16 * 4 * t * t * HEAD_DIM, bytes_accessed=8 * t * D, transcendentals=16 * t * t
        ),
    )(qkv, qkv, qkv)


def attend_back_kernel(q_ref, k_ref, v_ref, do_ref, dq_ref, dk_ref, dv_ref):
    q2, k2, v2, do2 = q_ref[...], k_ref[...], v_ref[...], do_ref[...]
    low = lax.broadcasted_iota(jnp.int32, k2.shape, 1) < HEAD_DIM
    k_t = k2.T
    zero = jnp.zeros_like(k2)
    dq, dk, dv = [], [], []
    for h in range(2):
        mine = low == (h == 0)
        p = soft_t(q2, jnp.where(mine, k2, zero))
        dp = dot_nt(jnp.where(mine, v2, zero), do2)
        total = jnp.sum(p * dp, axis=0, keepdims=True)
        ds = (p * (dp - total)).astype(BF)
        dv.append(dot(p.astype(BF), do2))
        dk.append(dot(ds, q2))
        dq.append(dot(k_t[h * HEAD_DIM : (h + 1) * HEAD_DIM], ds))
    scale = HEAD_DIM**-0.5
    dq_ref[...] = (jnp.concatenate(dq, axis=0).T * scale).astype(BF)
    dk_ref[...] = (jnp.where(low, dk[0], dk[1]) * scale).astype(BF)
    dv_ref[...] = jnp.where(low, dv[0], dv[1]).astype(BF)


def attend_back(qkv, do):
    t = qkv.shape[0]
    n = D // LANES
    spec = lambda off: pl.BlockSpec((t, LANES), lambda h: (0, off + h))
    return pl.pallas_call(
        attend_back_kernel,
        grid=(n,),
        out_shape=[jax.ShapeDtypeStruct((t, D), BF)] * 3,
        in_specs=[spec(0), spec(n), spec(2 * n), spec(0)],
        out_specs=[spec(0)] * 3,
        compiler_params=pltpu.CompilerParams(vmem_limit_bytes=48 * 2**20),
        cost_estimate=pl.CostEstimate(
            flops=16 * 10 * t * t * HEAD_DIM, bytes_accessed=14 * t * D, transcendentals=16 * t * t
        ),
    )(qkv, qkv, qkv, do)


class Links:
    def __init__(self, n_dp, n_seq):
        self.n_dp, self.n_seq = n_dp, n_seq
        self.short = n_dp == 8 and n_seq == len(RING)
        self.dp = lax.axis_index("dp")
        self.z = lax.axis_index("seq")

    def cross(self, x, bit):
        s = self.n_seq
        pairs = [(d * s + z, (d ^ bit) * s + z) for d in range(self.n_dp) for z in range(s)]
        return lax.ppermute(x, AXES, pairs)

    def ring(self, x):
        s = self.n_seq
        step = {RING[i]: RING[(i + 1) % s] for i in range(s)}
        pairs = [(d * s + z, d * s + step[z]) for d in range(self.n_dp) for z in range(s)]
        return lax.ppermute(x, AXES, pairs)

    def place(self):
        return jnp.array(RING, jnp.int32)[self.z]

    def gather(self, shard):
        if not self.short:
            whole = lax.all_gather(shard, AXES, axis=0, tiled=True)
            return list(jnp.split(whole, self.n_dp, axis=0))
        rows = shard.shape[0]
        held = [shard]
        for _ in range(3):
            held.append(self.ring(held[-1]))
        held = jnp.stack(held)
        place = self.place()
        own = jnp.concatenate(
            [lax.dynamic_index_in_dim(held, (place - RING[k]) % 4, 0, False) for k in range(4)]
        )
        half = 2 * rows
        from_x = self.cross(own, 2)
        from_y = self.cross(own, 4)
        far = jnp.concatenate([self.cross(from_x[:half], 4), self.cross(from_y[half:], 2)])
        blocks = []
        for b in (own, from_x, from_y, far):
            blocks += [b, self.cross(b, 1)]
        return blocks

    def reduce(self, blocks):
        if not self.short:
            whole = jnp.concatenate(blocks).astype(BF)
            return lax.psum_scatter(whole, AXES, scatter_dimension=0, tiled=True).astype(F32)
        sums = []
        for j in (3, 1, 2, 0):
            theirs = self.cross(blocks[2 * j + 1].astype(BF), 1)
            sums.append(blocks[2 * j].astype(F32) + theirs.astype(F32))
        far, to_x, to_y, own = sums
        half = far.shape[0] // 2
        far = far.astype(BF)
        low = self.cross(far[:half], 2).astype(F32)
        high = self.cross(far[half:], 4).astype(F32)
        to_y = jnp.concatenate([to_y[:half] + low, to_y[half:]])
        to_x = jnp.concatenate([to_x[:half], to_x[half:] + high])
        own = own + self.cross(to_x.astype(BF), 2).astype(F32) + self.cross(to_y.astype(BF), 4).astype(F32)
        rows = own.shape[0] // 4
        place = self.place()
        order = jnp.array(RING, jnp.int32)

        def piece(back):
            return lax.dynamic_slice_in_dim(own, order[(place - back) % 4] * rows, rows, 0)

        moving = self.ring(piece(1).astype(BF))
        for back in (2, 3):
            moving = self.ring((piece(back) + moving.astype(F32)).astype(BF))
        return piece(4) + moving.astype(F32)

    def blocks_of(self, x, axis):
        width = x.shape[axis] // self.n_dp
        if not self.short:
            return jnp.split(x, self.n_dp, axis=axis)
        return [
            lax.dynamic_slice_in_dim(x, (self.dp ^ m) * width, width, axis) for m in range(self.n_dp)
        ]

    def ordered(self, x, axis):
        return jnp.concatenate(self.blocks_of(x, axis), axis=axis)


    def lead(self, d, slots):
        return d % 2 if self.n_seq > slots else 0

    def shift_pairs(self, s, slots):
        n = self.n_seq
        pairs = []
        for d in range(self.n_dp):
            for z in range(n):
                to = (z + s) % n
                if 0 <= to - self.lead(d, slots) < slots:
                    pairs.append((d * n + z, d * n + to))
        return pairs

    def my_clip(self, slots):
        lead = self.dp % 2 if self.n_seq > slots else 0
        return self.z - lead

    def collect(self, x):
        slots, n = x.shape[0], self.n_seq
        clip = self.my_clip(slots)
        parts = []
        for s in range(n):
            lead = self.z - clip
            index = jnp.clip((self.z + s) % n - lead, 0, slots - 1)
            part = lax.dynamic_index_in_dim(x, index, 0, False)
            parts.append(part if s == 0 else lax.ppermute(part, AXES, self.shift_pairs(s, slots)))
        return jnp.concatenate(parts)

    def hand_back(self, y, slots):
        n = self.n_seq
        rows = y.shape[0] // n
        lead = self.z - self.my_clip(slots)
        back = []
        for s in range(n):
            part = y[s * rows : (s + 1) * rows]
            pairs = [(b, a) for a, b in self.shift_pairs(s, slots)]
            back.append(part if s == 0 else lax.ppermute(part, AXES, pairs))
        back = jnp.stack(back)
        return jnp.stack(
            [lax.dynamic_index_in_dim(back, (c + lead - self.z) % n, 0, False) for c in range(slots)]
        )


def norm_parts(v):
    center = v - jnp.mean(v, axis=-1, keepdims=True)
    r = lax.rsqrt(jnp.mean(center * center, axis=-1, keepdims=True) + EPSILON)
    return center * r, r


def norm_back(vhat, r, gain, e):
    t = e * gain
    grad = r * (
        t - jnp.mean(t, axis=-1, keepdims=True) - vhat * jnp.mean(t * vhat, axis=-1, keepdims=True)
    )
    return grad, jnp.sum(e * vhat, axis=0), jnp.sum(e, axis=0)


def gelu_both(u):
    cdf = 0.5 * (1.0 + lax.erf(u * 0.7071067811865476))
    pdf = 0.3989422804014327 * jnp.exp(-0.5 * u * u)
    return u * cdf, cdf + u * pdf


SMALL = (D, D, D, D, D, D, D, FF, D)


def per_device(
    n_dp,
    n_seq,
    clips,
    counts,
    out_cotangent,
    norm1_gain,
    norm1_shift,
    qkv_weight,
    query_bias,
    value_bias,
    proj_weight,
    proj_bias,
    norm2_gain,
    norm2_shift,
    up_weight,
    up_bias,
    down_weight,
    down_bias,
):
    links = Links(n_dp, n_seq)
    n = n_dp * n_seq
    slots = clips.shape[0]
    rows = D // n
    small = (
        norm1_gain,
        norm1_shift,
        query_bias,
        value_bias,
        proj_bias,
        norm2_gain,
        norm2_shift,
        up_bias,
        down_bias,
    )
    packed = jnp.concatenate(small)
    packed = jnp.pad(packed, (0, rows * LANES - packed.shape[0])).reshape(rows, LANES)
    shard_a = jnp.concatenate(
        [qkv_weight.reshape(rows, 3 * D), proj_weight.reshape(rows, D), packed], axis=1
    ).astype(BF)
    shard_u = up_weight.reshape(rows, FF).astype(BF)
    shard_d = down_weight.reshape(FF // n, D).astype(BF)

    x = links.collect(clips.astype(BF)).astype(F32)
    blocks_a = links.gather(shard_a)
    blocks_u = links.gather(shard_u)
    out_grad = links.collect(out_cotangent.astype(BF))
    blocks_d = links.gather(shard_d)

    clip = links.my_clip(slots)
    alive = (clip >= 0) & (clip < slots) & (clip < counts[0])
    out_grad = jnp.where(alive, out_grad, jnp.zeros_like(out_grad))

    a_mat = jnp.concatenate(blocks_a)
    table = a_mat[:, 4 * D :].reshape(n_dp, n_seq, rows * LANES)
    table = links.ordered(table, 0).reshape(n, rows * LANES).astype(F32)
    vectors, at = [], 0
    for size in SMALL:
        vectors.append(table[:, at : at + size // n].reshape(size))
        at += size // n
    gain1, shift1, q_bias, v_bias, p_bias, gain2, shift2, u_bias, d_bias = vectors

    vhat1, r1 = norm_parts(x)
    normed1 = (vhat1 * gain1 + shift1).astype(BF)
    normed1_b = links.ordered(normed1, 1)
    qkv_bias = jnp.concatenate([q_bias, jnp.zeros_like(q_bias), v_bias])
    qkv_mat, proj_mat = a_mat[:, : 3 * D], a_mat[:, 3 * D : 4 * D]
    qkv = (dot(normed1_b, qkv_mat) + qkv_bias).astype(BF)
    attended = attend(qkv)
    attended_b = links.ordered(attended, 1)
    branch = dot(attended_b, proj_mat) + p_bias
    middle = x + branch
    vhat2, r2 = norm_parts(middle)
    normed2_b = links.ordered((vhat2 * gain2 + shift2).astype(BF), 1)
    u_mat = jnp.concatenate(blocks_u)
    hidden, slope = gelu_both(dot(normed2_b, u_mat) + u_bias)
    hidden_b = links.ordered(hidden.astype(BF), 1)
    slope = slope.astype(BF)
    d_mat = jnp.concatenate(blocks_d)
    out_part = branch + dot(hidden_b, d_mat) + d_bias
    living = (jnp.arange(slots) < counts[0]).astype(F32)[:, None, None]
    block_out = living * (clips + links.hand_back(out_part.astype(BF), slots).astype(F32))

    d_down = dot_tn(hidden_b, out_grad).astype(BF)
    down_grad = links.reduce(jnp.split(d_down, n_dp, axis=0))
    hidden_grad = links.ordered(dot_nt(out_grad, d_mat), 1)
    upper_grad = (hidden_grad * slope).astype(BF)
    d_up = dot_tn(normed2_b, upper_grad).astype(BF)
    up_grad = links.reduce(jnp.split(d_up, n_dp, axis=0))
    normed_grad = links.ordered(dot_nt(upper_grad, u_mat), 1)
    part, gain2_grad, shift2_grad = norm_back(vhat2, r2, gain2, normed_grad)
    middle_part = out_grad.astype(F32) + part
    branch_grad = middle_part.astype(BF)
    attended_grad = links.ordered(dot_nt(branch_grad, proj_mat).astype(BF), 1)
    dq, dk, dv = attend_back(qkv, attended_grad)
    joined = jnp.concatenate([dq, dk, dv], axis=1)
    first_grad = links.ordered(dot_nt(joined, qkv_mat), 1)
    first_part, gain1_grad, shift1_grad = norm_back(vhat1, r1, gain1, first_grad)
    living_cot = living * out_cotangent
    input_grad = living_cot + links.hand_back((part + first_part).astype(BF), slots).astype(F32)

    total = lambda g: jnp.sum(g.astype(F32), axis=0)
    small_grads = (
        gain1_grad,
        shift1_grad,
        total(dq),
        total(dv),
        total(branch_grad),
        gain2_grad,
        shift2_grad,
        total(upper_grad),
        total(out_grad),
    )
    grad_table = jnp.concatenate([g.reshape(n, -1) for g in small_grads], axis=1)
    width = grad_table.shape[1]
    grad_table = jnp.pad(grad_table, ((0, 0), (0, rows * LANES - width)))
    grad_table = links.ordered(grad_table.reshape(n_dp, n_seq, rows * LANES), 0)
    d_a = jnp.concatenate(
        [
            dot_tn(normed1_b, joined).astype(BF),
            dot_tn(attended_b, branch_grad).astype(BF),
            grad_table.reshape(n * rows, LANES).astype(BF),
        ],
        axis=1,
    )
    a_grad = links.reduce(jnp.split(d_a, n_dp, axis=0))
    small_out = a_grad[:, 4 * D :].reshape(-1)
    pieces, at = [], 0
    for size in SMALL:
        pieces.append(small_out[at : at + size // n])
        at += size // n
    g1, s1, qb, vb, pb, g2, s2, ub, db = pieces
    return (
        block_out,
        input_grad,
        g1,
        s1,
        a_grad[:, : 3 * D].reshape(-1),
        qb,
        vb,
        a_grad[:, 3 * D : 4 * D].reshape(-1),
        pb,
        g2,
        s2,
        up_grad.reshape(-1),
        ub,
        down_grad.reshape(-1),
        db,
    )


def solution(mesh):
    flat = P(AXES)
    tokens = P("dp", "seq", None)
    return jax.shard_map(
        functools.partial(per_device, mesh.shape["dp"], mesh.shape["seq"]),
        mesh=mesh,
        in_specs=(tokens, P("dp"), tokens) + (flat,) * 13,
        out_specs=(tokens, tokens) + (flat,) * 13,
        check_vma=False,
    )
```

```python
import functools

import jax
import jax.numpy as jnp
from jax import lax
from jax.experimental import pallas as pl
from jax.experimental.pallas import tpu as pltpu
from jax.sharding import PartitionSpec as P

D = 1024
FF = 4096
HEADS = 16
HEAD_DIM = 64
EPSILON = 1e-05
LANES = 128
BF = jnp.bfloat16
F32 = jnp.float32
AXES = ("dp", "seq")
MESH = pl.DeviceIdType.MESH
RING = (0, 1, 3, 2)


def dot(a, b):
    return jnp.dot(a, b, preferred_element_type=F32)


def dot_nt(a, b):
    return lax.dot_general(a, b, (((1,), (1,)), ((), ())), preferred_element_type=F32)


def dot_tn(a, b):
    return lax.dot_general(a, b, (((0,), (0,)), ((), ())), preferred_element_type=F32)


def soft_t(q2, k_half):
    scores = dot_nt(k_half, q2) * (HEAD_DIM**-0.5)
    top = jnp.max(scores, axis=0, keepdims=True)
    e = jnp.exp(scores - top)
    return e * (1.0 / jnp.sum(e, axis=0, keepdims=True))


def attend_kernel(q_ref, k_ref, v_ref, o_ref):
    q2, k2, v2 = q_ref[...], k_ref[...], v_ref[...]
    low = lax.broadcasted_iota(jnp.int32, k2.shape, 1) < HEAD_DIM
    v_t = v2.T
    zero = jnp.zeros_like(k2)
    parts = []
    for h in range(2):
        k_half = jnp.where(low == (h == 0), k2, zero)
        p_t = soft_t(q2, k_half).astype(BF)
        parts.append(dot(v_t[h * HEAD_DIM : (h + 1) * HEAD_DIM], p_t))
    o_ref[...] = jnp.concatenate(parts, axis=0).T.astype(BF)


def attend(qkv):
    t = qkv.shape[0]
    n = D // LANES
    spec = lambda off: pl.BlockSpec((t, LANES), lambda h: (0, off + h))
    return pl.pallas_call(
        attend_kernel,
        grid=(n,),
        out_shape=jax.ShapeDtypeStruct((t, D), BF),
        in_specs=[spec(0), spec(n), spec(2 * n)],
        out_specs=spec(0),
        compiler_params=pltpu.CompilerParams(vmem_limit_bytes=48 * 2**20),
        cost_estimate=pl.CostEstimate(
            flops=16 * 4 * t * t * HEAD_DIM, bytes_accessed=8 * t * D, transcendentals=16 * t * t
        ),
    )(qkv, qkv, qkv)


def attend_back_kernel(q_ref, k_ref, v_ref, do_ref, dq_ref, dk_ref, dv_ref):
    q2, k2, v2, do2 = q_ref[...], k_ref[...], v_ref[...], do_ref[...]
    low = lax.broadcasted_iota(jnp.int32, k2.shape, 1) < HEAD_DIM
    k_t = k2.T
    zero = jnp.zeros_like(k2)
    dq, dk, dv = [], [], []
    for h in range(2):
        mine = low == (h == 0)
        p = soft_t(q2, jnp.where(mine, k2, zero))
        dp = dot_nt(jnp.where(mine, v2, zero), do2)
        total = jnp.sum(p * dp, axis=0, keepdims=True)
        ds = (p * (dp - total)).astype(BF)
        dv.append(dot(p.astype(BF), do2))
        dk.append(dot(ds, q2))
        dq.append(dot(k_t[h * HEAD_DIM : (h + 1) * HEAD_DIM], ds))
    scale = HEAD_DIM**-0.5
    dq_ref[...] = (jnp.concatenate(dq, axis=0).T * scale).astype(BF)
    dk_ref[...] = (jnp.where(low, dk[0], dk[1]) * scale).astype(BF)
    dv_ref[...] = jnp.where(low, dv[0], dv[1]).astype(BF)


def attend_back(qkv, do):
    t = qkv.shape[0]
    n = D // LANES
    spec = lambda off: pl.BlockSpec((t, LANES), lambda h: (0, off + h))
    return pl.pallas_call(
        attend_back_kernel,
        grid=(n,),
        out_shape=[jax.ShapeDtypeStruct((t, D), BF)] * 3,
        in_specs=[spec(0), spec(n), spec(2 * n), spec(0)],
        out_specs=[spec(0)] * 3,
        compiler_params=pltpu.CompilerParams(vmem_limit_bytes=48 * 2**20),
        cost_estimate=pl.CostEstimate(
            flops=16 * 10 * t * t * HEAD_DIM, bytes_accessed=14 * t * D, transcendentals=16 * t * t
        ),
    )(qkv, qkv, qkv, do)


class Links:
    def __init__(self, n_dp, n_seq):
        self.n_dp, self.n_seq = n_dp, n_seq
        self.short = n_dp == 8 and n_seq == len(RING)
        self.dp = lax.axis_index("dp")
        self.z = lax.axis_index("seq")

    def cross(self, x, bit):
        s = self.n_seq
        pairs = [(d * s + z, (d ^ bit) * s + z) for d in range(self.n_dp) for z in range(s)]
        return lax.ppermute(x, AXES, pairs)

    def ring(self, x):
        s = self.n_seq
        step = {RING[i]: RING[(i + 1) % s] for i in range(s)}
        pairs = [(d * s + z, d * s + step[z]) for d in range(self.n_dp) for z in range(s)]
        return lax.ppermute(x, AXES, pairs)

    def place(self):
        return jnp.array(RING, jnp.int32)[self.z]

    def gather(self, shard):
        return lax.all_gather(shard, AXES, axis=0, tiled=True)

    def reduce(self, blocks):
        if not self.short:
            whole = jnp.concatenate(blocks).astype(BF)
            return lax.psum_scatter(whole, AXES, scatter_dimension=0, tiled=True).astype(F32)
        sums = []
        for j in (3, 1, 2, 0):
            theirs = self.cross(blocks[2 * j + 1].astype(BF), 1)
            sums.append(blocks[2 * j].astype(F32) + theirs.astype(F32))
        far, to_x, to_y, own = sums
        half = far.shape[0] // 2
        far = far.astype(BF)
        low = self.cross(far[:half], 2).astype(F32)
        high = self.cross(far[half:], 4).astype(F32)
        to_y = jnp.concatenate([to_y[:half] + low, to_y[half:]])
        to_x = jnp.concatenate([to_x[:half], to_x[half:] + high])
        own = own + self.cross(to_x.astype(BF), 2).astype(F32) + self.cross(to_y.astype(BF), 4).astype(F32)
        rows = own.shape[0] // 4
        place = self.place()
        order = jnp.array(RING, jnp.int32)

        def piece(back):
            return lax.dynamic_slice_in_dim(own, order[(place - back) % 4] * rows, rows, 0)

        moving = self.ring(piece(1).astype(BF))
        for back in (2, 3):
            moving = self.ring((piece(back) + moving.astype(F32)).astype(BF))
        return piece(4) + moving.astype(F32)

    def blocks_of(self, x, axis):
        width = x.shape[axis] // self.n_dp
        if not self.short:
            return jnp.split(x, self.n_dp, axis=axis)
        return [
            lax.dynamic_slice_in_dim(x, (self.dp ^ m) * width, width, axis) for m in range(self.n_dp)
        ]


    def lead(self, d, slots):
        return d % 2 if self.n_seq > slots else 0

    def shift_pairs(self, s, slots):
        n = self.n_seq
        pairs = []
        for d in range(self.n_dp):
            for z in range(n):
                to = (z + s) % n
                if 0 <= to - self.lead(d, slots) < slots:
                    pairs.append((d * n + z, d * n + to))
        return pairs

    def my_clip(self, slots):
        lead = self.dp % 2 if self.n_seq > slots else 0
        return self.z - lead

    def collect(self, x):
        slots, n = x.shape[0], self.n_seq
        clip = self.my_clip(slots)
        parts = []
        for s in range(n):
            lead = self.z - clip
            index = jnp.clip((self.z + s) % n - lead, 0, slots - 1)
            part = lax.dynamic_index_in_dim(x, index, 0, False)
            parts.append(part if s == 0 else lax.ppermute(part, AXES, self.shift_pairs(s, slots)))
        host = (clip >= 0) & (clip < slots)
        return jnp.where(host, jnp.concatenate(parts), jnp.zeros((), x.dtype))

    def hand_back(self, y, slots):
        n = self.n_seq
        rows = y.shape[0] // n
        lead = self.z - self.my_clip(slots)
        back = []
        for s in range(n):
            part = y[s * rows : (s + 1) * rows]
            pairs = [(b, a) for a, b in self.shift_pairs(s, slots)]
            back.append(part if s == 0 else lax.ppermute(part, AXES, pairs))
        back = jnp.stack(back)
        return jnp.stack(
            [lax.dynamic_index_in_dim(back, (c + lead - self.z) % n, 0, False) for c in range(slots)]
        )


def guarded(cond, f):
    if cond is None: f()
    else: pl.when(cond)(f)

class Copies:
    def __init__(self, send, recv):
        self.send, self.recv, self.n, self.sent = send, recv, 0, []
        self.dp, self.z = lax.axis_index("dp"), lax.axis_index("seq")
    def slots(self, k):
        self.n += k
        return list(range(self.n - k, self.n))
    def remote(self, slot, src, dst, dev):
        return pltpu.make_async_remote_copy(src_ref=src, dst_ref=dst, send_sem=self.send.at[slot], recv_sem=self.recv.at[slot], device_id=dev, device_id_type=MESH)
    def start(self, slot, src, dst, dev, cond=None):
        guarded(cond, lambda: self.remote(slot, src(), dst(), dev).start())
        self.sent.append((slot, src, dst, dev, cond))
    def arrived(self, slot, dst, cond=None):
        guarded(cond, lambda: self.remote(slot, dst(), dst(), (self.dp ^ 1, self.z)).wait_recv())
    def finish(self):
        for slot, src, dst, dev, cond in self.sent:
            guarded(cond, lambda: self.remote(slot, src(), dst(), dev).wait_send())
        self.sent = []

class Gather:
    def __init__(self, io, shard, out, fine, local):
        self.io, self.shard, self.out, self.fine = io, shard, out, fine
        self.r = shard.shape[0]
        self.local = pltpu.make_async_copy(shard, self.at(0, 0), local)
        self.keys = (0, -1, 1, -2, 2, -3, 3) if fine else (None,)
        self.z_slot = {(e * s): io.slots(1)[0] for e in (1, 2, 3) for s in (-1, 1)}
        self.slot = {k: dict(x=io.slots(1), y=io.slots(1), d=io.slots(2), own=io.slots(1), cx=io.slots(1), cy=io.slots(1), cd=io.slots(2)) for k in self.keys}
    def at(self, m, k, part=None):
        io, r = self.io, self.r
        if k is None: base, n = (io.dp ^ m) * 4 * r, 4 * r
        else: base, n = ((io.dp ^ m) * 4 + io.z + k) * r, r
        if part is not None: n = n // 2; base = base + part * n
        return self.out.at[pl.ds(pl.multiple_of(base, 16), n)]
    def ok(self, k):
        if not k: return None
        return (self.io.z + k >= 0) & (self.io.z + k <= 3)
    def move(self, name, i, m, k, bit, part=None, src=None):
        ref = lambda: self.at(m, k, part)
        io = self.io
        io.start(self.slot[k][name][i], src or ref, ref, (io.dp ^ bit, io.z), self.ok(k))
    def got(self, name, i, m, k, part=None):
        self.io.arrived(self.slot[k][name][i], lambda: self.at(m, k, part), self.ok(k))
    def start_z(self):
        io = self.io
        self.local.start()
        mine = lambda: self.shard
        to = lambda: self.at(0, 0)
        io.start(self.z_slot[-1], mine, to, (io.dp, io.z + 1), io.z < 3)
        io.start(self.z_slot[1], mine, to, (io.dp, io.z - 1), io.z > 0)
    def pass_z(self, e):
        io = self.io
        for s in (-1, 1):
            k = s * e
            ref = lambda k=k: self.at(0, k)
            io.arrived(self.z_slot[k], ref, self.ok(k))
            if e < 3:
                to = io.z - s
                io.start(self.z_slot[s * (e + 1)], ref, ref, (io.dp, to), self.ok(k) & (to >= 0) & (to <= 3))
    def spread(self, k):
        src = (lambda: self.shard) if k == 0 else None
        self.move("x", 0, 0, k, 2, src=src)
        self.move("y", 0, 0, k, 4, src=src)
        self.move("own", 0, 0, k, 1, src=src)
    def pass_on(self, k):
        self.got("x", 0, 2, k)
        self.move("d", 0, 2, k, 4, 0)
        self.got("y", 0, 4, k)
        self.move("d", 1, 4, k, 2, 1)
        self.move("cx", 0, 2, k, 1)
        self.move("cy", 0, 4, k, 1)
    def far(self, k):
        for h in range(2):
            self.got("d", h, 6, k, h)
            self.move("cd", h, 6, k, 1, h)
    def done(self, k):
        self.got("own", 0, 1, k)
        self.got("cx", 0, 3, k)
        self.got("cy", 0, 5, k)
        for h in range(2): self.got("cd", h, 7, k, h)

class Collect:
    def __init__(self, io, src, dst, local):
        self.io, self.src, self.dst = io, src, dst
        self.slots = io.slots(4)
        self.local = local
        self.rows = src.shape[1]
        self.host = self.valid(io.z)
    def part(self, s): return self.dst.at[pl.ds(s * self.rows, self.rows)]
    def valid(self, z):
        clip = z - self.io.dp % 2
        return (clip >= 0) & (clip < 3)
    def start(self):
        io = self.io
        for s in range(4):
            to = (io.z + s) % 4
            src = lambda to=to: self.src.at[jnp.clip(to - io.dp % 2, 0, 2)]
            if s == 0:
                guarded(self.host, lambda: pltpu.make_async_copy(src(), self.part(0), self.local).start())
            else:
                io.start(self.slots[s], src, lambda s=s: self.part(s), (io.dp, to), self.valid(to))
    def wait(self):
        guarded(self.host, lambda: pltpu.make_async_copy(self.part(0), self.part(0), self.local).wait())
        for s in range(1, 4):
            self.io.arrived(self.slots[s], lambda s=s: self.part(s), self.host)

N_SLOTS = 140
def gather_kernel(a, u, d, x, c, wa, wu, wd, xb, cb, zero, send, recv, local):
    io = Copies(send, recv)
    ga, gu, gd = Gather(io, a, wa, True, local.at[0]), Gather(io, u, wu, False, local.at[1]), Gather(io, d, wd, False, local.at[2])
    cx, cc = Collect(io, x, xb, local.at[3]), Collect(io, c, cb, local.at[4])
    assert io.n <= N_SLOTS, io.n
    bar = pltpu.get_barrier_semaphore()
    partners = [(io.dp, io.z ^ k) for k in (1, 2, 3)] + [(io.dp ^ b, io.z) for b in (1, 2, 4)]
    for p in partners: pl.semaphore_signal(bar, inc=1, device_id=p, device_id_type=MESH)
    zero[...] = jnp.zeros_like(zero)
    pl.semaphore_wait(bar, len(partners))
    ga.start_z(); ga.spread(0)
    ga.local.wait()
    ga.pass_z(1); ga.spread(-1); ga.spread(1)
    ga.pass_on(0)
    ga.pass_z(2); ga.spread(-2); ga.spread(2)
    gu.start_z()
    ga.far(0)
    ga.pass_on(-1); ga.pass_on(1)
    ga.pass_z(3); ga.spread(-3); ga.spread(3)
    gu.pass_z(1)
    ga.far(-1); ga.far(1)
    gu.pass_z(2)
    cx.start()
    ga.pass_on(-2); ga.pass_on(2)
    gu.pass_z(3)
    gu.local.wait()
    gu.spread(None)
    ga.far(-2); ga.far(2)
    gd.start_z()
    ga.pass_on(-3); ga.pass_on(3)
    ga.far(-3); ga.far(3)
    for i in ga.keys: ga.done(i)
    gd.pass_z(1)
    cx.wait()
    gd.pass_z(2)
    gd.pass_z(3)
    gd.local.wait()
    gd.spread(None)
    cc.start()
    gu.pass_on(None)
    gu.far(None)
    gu.done(None)
    cc.wait()
    gd.pass_on(None)
    gd.far(None)
    gd.done(None)
    for col in (cx, cc):
        def fill():
            cp = pltpu.make_async_copy(zero, col.dst, local.at[5])
            cp.start(); cp.wait()
        guarded(jnp.logical_not(col.host), fill)
    io.finish()

def gather_all(a, u, d, x, c):
    t = x.shape[1]*4
    any_ = pl.BlockSpec(memory_space=pl.ANY)
    sh = lambda r, c_: jax.ShapeDtypeStruct((r, c_), BF)
    return pl.pallas_call(gather_kernel,
        out_shape=[sh(32*a.shape[0], a.shape[1]), sh(32*u.shape[0], u.shape[1]), sh(32*d.shape[0], d.shape[1]), sh(t,1024), sh(t,1024)],
        in_specs=[any_]*5, out_specs=[any_]*5,
        scratch_shapes=[pltpu.VMEM((t,1024),BF), pltpu.SemaphoreType.DMA((N_SLOTS,)), pltpu.SemaphoreType.DMA((N_SLOTS,)), pltpu.SemaphoreType.DMA((8,))],
        compiler_params=pltpu.CompilerParams(collective_id=0, has_side_effects=True, vmem_limit_bytes=56*2**20))(a,u,d,x,c)


def norm_parts(v):
    center = v - jnp.mean(v, axis=-1, keepdims=True)
    r = lax.rsqrt(jnp.mean(center * center, axis=-1, keepdims=True) + EPSILON)
    return center * r, r


def norm_back(vhat, r, gain, e):
    t = e * gain
    grad = r * (
        t - jnp.mean(t, axis=-1, keepdims=True) - vhat * jnp.mean(t * vhat, axis=-1, keepdims=True)
    )
    return grad, jnp.sum(e * vhat, axis=0), jnp.sum(e, axis=0)


def gelu_both(u):
    cdf = 0.5 * (1.0 + lax.erf(u * 0.7071067811865476))
    pdf = 0.3989422804014327 * jnp.exp(-0.5 * u * u)
    return u * cdf, cdf + u * pdf


SMALL = (D, D, D, D, D, D, D, FF, D)


def per_device(
    n_dp,
    n_seq,
    clips,
    counts,
    out_cotangent,
    norm1_gain,
    norm1_shift,
    qkv_weight,
    query_bias,
    value_bias,
    proj_weight,
    proj_bias,
    norm2_gain,
    norm2_shift,
    up_weight,
    up_bias,
    down_weight,
    down_bias,
):
    links = Links(n_dp, n_seq)
    n = n_dp * n_seq
    slots = clips.shape[0]
    rows = D // n
    small = (
        norm1_gain,
        norm1_shift,
        query_bias,
        value_bias,
        proj_bias,
        norm2_gain,
        norm2_shift,
        up_bias,
        down_bias,
    )
    packed = jnp.concatenate(small)
    packed = jnp.pad(packed, (0, rows * LANES - packed.shape[0])).reshape(rows, LANES)
    shard_a = jnp.concatenate(
        [qkv_weight.reshape(rows, 3 * D), proj_weight.reshape(rows, D), packed], axis=1
    ).astype(BF)
    shard_u = up_weight.reshape(rows, FF).astype(BF)
    shard_d = down_weight.reshape(FF // n, D).astype(BF)

    living = (jnp.arange(slots) < counts[0]).astype(F32)[:, None, None]
    living_cot = living * out_cotangent
    tokens = (clips.astype(BF), living_cot.astype(BF))
    if links.short:
        a_mat, u_mat, d_mat, x, out_grad = gather_all(shard_a, shard_u, shard_d, *tokens)
    else:
        a_mat, u_mat, d_mat = (links.gather(shard) for shard in (shard_a, shard_u, shard_d))
        x, out_grad = (links.collect(t) for t in tokens)
    x = x.astype(F32)

    table = a_mat[:, 4 * D :].reshape(n_dp, n_seq, rows * LANES)
    table = table.reshape(n, rows * LANES).astype(F32)
    vectors, at = [], 0
    for size in SMALL:
        vectors.append(table[:, at : at + size // n].reshape(size))
        at += size // n
    gain1, shift1, q_bias, v_bias, p_bias, gain2, shift2, u_bias, d_bias = vectors

    vhat1, r1 = norm_parts(x)
    normed1 = (vhat1 * gain1 + shift1).astype(BF)
    qkv_bias = jnp.concatenate([q_bias, jnp.zeros_like(q_bias), v_bias])
    qkv_mat, proj_mat = a_mat[:, : 3 * D], a_mat[:, 3 * D : 4 * D]
    qkv = (dot(normed1, qkv_mat) + qkv_bias).astype(BF)
    attended = attend(qkv)
    branch = dot(attended, proj_mat) + p_bias
    middle = x + branch
    vhat2, r2 = norm_parts(middle)
    normed2 = (vhat2 * gain2 + shift2).astype(BF)
    hidden, slope = gelu_both(dot(normed2, u_mat) + u_bias)
    hidden = hidden.astype(BF)
    slope = slope.astype(BF)
    out_part = branch + dot(hidden, d_mat) + d_bias
    block_out = living * (clips + links.hand_back(out_part.astype(BF), slots).astype(F32))

    d_down = dot_tn(hidden, out_grad).astype(BF)
    down_grad = links.reduce(links.blocks_of(d_down, 0))
    hidden_grad = dot_nt(out_grad, d_mat)
    upper_grad = (hidden_grad * slope).astype(BF)
    d_up = dot_tn(normed2, upper_grad).astype(BF)
    up_grad = links.reduce(links.blocks_of(d_up, 0))
    normed_grad = dot_nt(upper_grad, u_mat)
    part, gain2_grad, shift2_grad = norm_back(vhat2, r2, gain2, normed_grad)
    middle_part = out_grad.astype(F32) + part
    branch_grad = middle_part.astype(BF)
    attended_grad = dot_nt(branch_grad, proj_mat).astype(BF)
    dq, dk, dv = attend_back(qkv, attended_grad)
    joined = jnp.concatenate([dq, dk, dv], axis=1)
    first_grad = dot_nt(joined, qkv_mat)
    first_part, gain1_grad, shift1_grad = norm_back(vhat1, r1, gain1, first_grad)
    input_grad = living_cot + links.hand_back((part + first_part).astype(BF), slots).astype(F32)

    total = lambda g: jnp.sum(g.astype(F32), axis=0)
    small_grads = (
        gain1_grad,
        shift1_grad,
        total(dq),
        total(dv),
        total(branch_grad),
        gain2_grad,
        shift2_grad,
        total(upper_grad),
        total(out_grad),
    )
    grad_table = jnp.concatenate([g.reshape(n, -1) for g in small_grads], axis=1)
    width = grad_table.shape[1]
    grad_table = jnp.pad(grad_table, ((0, 0), (0, rows * LANES - width)))
    d_a = jnp.concatenate(
        [
            dot_tn(normed1, joined).astype(BF),
            dot_tn(attended, branch_grad).astype(BF),
            grad_table.reshape(n * rows, LANES).astype(BF),
        ],
        axis=1,
    )
    a_grad = links.reduce(links.blocks_of(d_a, 0))
    small_out = a_grad[:, 4 * D :].reshape(-1)
    pieces, at = [], 0
    for size in SMALL:
        pieces.append(small_out[at : at + size // n])
        at += size // n
    g1, s1, qb, vb, pb, g2, s2, ub, db = pieces
    return (
        block_out,
        input_grad,
        g1,
        s1,
        a_grad[:, : 3 * D].reshape(-1),
        qb,
        vb,
        a_grad[:, 3 * D : 4 * D].reshape(-1),
        pb,
        g2,
        s2,
        up_grad.reshape(-1),
        ub,
        down_grad.reshape(-1),
        db,
    )


def solution(mesh):
    flat = P(AXES)
    tokens = P("dp", "seq", None)
    return jax.shard_map(
        functools.partial(per_device, mesh.shape["dp"], mesh.shape["seq"]),
        mesh=mesh,
        in_specs=(tokens, P("dp"), tokens) + (flat,) * 13,
        out_specs=(tokens, tokens) + (flat,) * 13,
        check_vma=False,
    )
```

```python
import functools

import jax
import jax.numpy as jnp
from jax import lax
from jax.experimental import pallas as pl
from jax.experimental.pallas import tpu as pltpu
from jax.sharding import PartitionSpec as P

D = 1024
FF = 4096
HEADS = 16
HEAD_DIM = 64
EPSILON = 1e-05
LANES = 128
BF = jnp.bfloat16
F32 = jnp.float32
AXES = ("dp", "seq")
MESH = pl.DeviceIdType.MESH


def dot(a, b):
    return jnp.dot(a, b, preferred_element_type=F32)


def dot_nt(a, b):
    return lax.dot_general(a, b, (((1,), (1,)), ((), ())), preferred_element_type=F32)


def dot_tn(a, b):
    return lax.dot_general(a, b, (((0,), (0,)), ((), ())), preferred_element_type=F32)


def soft_t(q2, k_half):
    scores = dot_nt(k_half, q2) * (HEAD_DIM**-0.5)
    top = jnp.max(scores, axis=0, keepdims=True)
    e = jnp.exp(scores - top)
    return e * (1.0 / jnp.sum(e, axis=0, keepdims=True))


def attend_kernel(q_ref, k_ref, v_ref, o_ref):
    q2, k2, v2 = q_ref[...], k_ref[...], v_ref[...]
    low = lax.broadcasted_iota(jnp.int32, k2.shape, 1) < HEAD_DIM
    v_t = v2.T
    zero = jnp.zeros_like(k2)
    parts = []
    for h in range(2):
        k_half = jnp.where(low == (h == 0), k2, zero)
        p_t = soft_t(q2, k_half).astype(BF)
        parts.append(dot(v_t[h * HEAD_DIM : (h + 1) * HEAD_DIM], p_t))
    o_ref[...] = jnp.concatenate(parts, axis=0).T.astype(BF)


def attend(qkv):
    t = qkv.shape[0]
    n = D // LANES
    spec = lambda off: pl.BlockSpec((t, LANES), lambda h: (0, off + h))
    return pl.pallas_call(
        attend_kernel,
        grid=(n,),
        out_shape=jax.ShapeDtypeStruct((t, D), BF),
        in_specs=[spec(0), spec(n), spec(2 * n)],
        out_specs=spec(0),
        compiler_params=pltpu.CompilerParams(vmem_limit_bytes=48 * 2**20),
        cost_estimate=pl.CostEstimate(
            flops=16 * 4 * t * t * HEAD_DIM, bytes_accessed=8 * t * D, transcendentals=16 * t * t
        ),
    )(qkv, qkv, qkv)


def attend_back_pair(q2, k2, v2, do2):
    low = lax.broadcasted_iota(jnp.int32, k2.shape, 1) < HEAD_DIM
    k_t = k2.T
    zero = jnp.zeros_like(k2)
    dq, dk, dv = [], [], []
    for h in range(2):
        mine = low == (h == 0)
        p = soft_t(q2, jnp.where(mine, k2, zero))
        dp = dot_nt(jnp.where(mine, v2, zero), do2)
        total = jnp.sum(p * dp, axis=0, keepdims=True)
        ds = (p * (dp - total)).astype(BF)
        dv.append(dot(p.astype(BF), do2))
        dk.append(dot(ds, q2))
        dq.append(dot(k_t[h * HEAD_DIM : (h + 1) * HEAD_DIM], ds))
    scale = HEAD_DIM**-0.5
    return (
        (jnp.concatenate(dq, axis=0).T * scale).astype(BF),
        (jnp.where(low, dk[0], dk[1]) * scale).astype(BF),
        jnp.where(low, dv[0], dv[1]).astype(BF),
    )


def attend_back_kernel(q_ref, k_ref, v_ref, do_ref, dq_ref, dk_ref, dv_ref):
    grads = attend_back_pair(q_ref[...], k_ref[...], v_ref[...], do_ref[...])
    dq_ref[...], dk_ref[...], dv_ref[...] = grads


def attend_back(qkv, do):
    t = qkv.shape[0]
    n = D // LANES
    spec = lambda off: pl.BlockSpec((t, LANES), lambda h: (0, off + h))
    return pl.pallas_call(
        attend_back_kernel,
        grid=(n,),
        out_shape=[jax.ShapeDtypeStruct((t, D), BF)] * 3,
        in_specs=[spec(0), spec(n), spec(2 * n), spec(0)],
        out_specs=[spec(0)] * 3,
        compiler_params=pltpu.CompilerParams(vmem_limit_bytes=48 * 2**20),
        cost_estimate=pl.CostEstimate(
            flops=16 * 10 * t * t * HEAD_DIM, bytes_accessed=14 * t * D, transcendentals=16 * t * t
        ),
    )(qkv, qkv, qkv, do)


class Links:
    def __init__(self, n_dp, n_seq):
        self.n_dp, self.n_seq = n_dp, n_seq
        self.short = n_dp == 8 and n_seq == 4
        self.dp = lax.axis_index("dp")
        self.z = lax.axis_index("seq")

    def gather(self, shard):
        return lax.all_gather(shard, AXES, axis=0, tiled=True)

    def reduce(self, grad):
        return lax.psum_scatter(grad.astype(BF), AXES, scatter_dimension=0, tiled=True).astype(F32)


    def lead(self, d, slots):
        return d % 2 if self.n_seq > slots else 0

    def shift_pairs(self, s, slots):
        n = self.n_seq
        pairs = []
        for d in range(self.n_dp):
            for z in range(n):
                to = (z + s) % n
                if 0 <= to - self.lead(d, slots) < slots:
                    pairs.append((d * n + z, d * n + to))
        return pairs

    def my_clip(self, slots):
        lead = self.dp % 2 if self.n_seq > slots else 0
        return self.z - lead

    def collect(self, x):
        slots, n = x.shape[0], self.n_seq
        clip = self.my_clip(slots)
        parts = []
        for s in range(n):
            lead = self.z - clip
            index = jnp.clip((self.z + s) % n - lead, 0, slots - 1)
            part = lax.dynamic_index_in_dim(x, index, 0, False)
            parts.append(part if s == 0 else lax.ppermute(part, AXES, self.shift_pairs(s, slots)))
        host = (clip >= 0) & (clip < slots)
        return jnp.where(host, jnp.concatenate(parts), jnp.zeros((), x.dtype))

    def hand_back(self, y, slots):
        n = self.n_seq
        rows = y.shape[0] // n
        back = []
        for s in range(n):
            part = y[s * rows : (s + 1) * rows]
            pairs = [(b, a) for a, b in self.shift_pairs(s, slots)]
            back.append(part if s == 0 else lax.ppermute(part, AXES, pairs))
        return self.by_clip(jnp.stack(back), slots)

    def by_clip(self, back, slots):
        n = self.n_seq
        lead = self.z - self.my_clip(slots)
        return jnp.stack(
            [lax.dynamic_index_in_dim(back, (c + lead - self.z) % n, 0, False) for c in range(slots)]
        )


def guarded(cond, f):
    if cond is None: f()
    else: pl.when(cond)(f)

class Copies:
    def __init__(self, send, recv, local=None):
        self.send, self.recv, self.n, self.sent = send, recv, 0, []
        self.local, self.n_local = local, 0
        self.dp, self.z = lax.axis_index("dp"), lax.axis_index("seq")
    def slots(self, k):
        self.n += k
        return list(range(self.n - k, self.n))
    def remote(self, slot, src, dst, dev):
        return pltpu.make_async_remote_copy(src_ref=src, dst_ref=dst, send_sem=self.send.at[slot], recv_sem=self.recv.at[slot], device_id=dev, device_id_type=MESH)
    def start(self, slot, src, dst, dev, cond=None):
        guarded(cond, lambda: self.remote(slot, src(), dst(), dev).start())
        self.sent.append((slot, src, dst, dev, cond))
    def arrived(self, slot, dst, cond=None):
        guarded(cond, lambda: self.remote(slot, dst(), dst(), (self.dp ^ 1, self.z)).wait_recv())
    def sent_wait(self, which=None):
        rest = []
        for slot, src, dst, dev, cond in self.sent:
            if which is None or slot == which:
                guarded(cond, lambda: self.remote(slot, src(), dst(), dev).wait_send())
            else:
                rest.append((slot, src, dst, dev, cond))
        self.sent = rest
    def finish(self):
        self.sent_wait()
    def locals(self, k):
        self.n_local += k
        return self.n_local - k
    def load(self, src, dst):
        copy = pltpu.make_async_copy(src, dst, self.local.at[self.locals(1)])
        copy.start()
        return copy

class Gather:
    def __init__(self, io, shard, out, fine, local):
        self.io, self.shard, self.out, self.fine = io, shard, out, fine
        self.r = shard.shape[0]
        self.local = pltpu.make_async_copy(shard, self.at(0, 0), local)
        self.keys = (0, -1, 1, -2, 2, -3, 3) if fine else (None,)
        self.z_slot = {(e * s): io.slots(1)[0] for e in (1, 2, 3) for s in (-1, 1)}
        self.slot = {k: dict(x=io.slots(1), y=io.slots(1), d=io.slots(2), own=io.slots(1), cx=io.slots(1), cy=io.slots(1), cd=io.slots(2)) for k in self.keys}
    def at(self, m, k, part=None):
        io, r = self.io, self.r
        if k is None: base, n = (io.dp ^ m) * 4 * r, 4 * r
        else: base, n = ((io.dp ^ m) * 4 + io.z + k) * r, r
        if part is not None: n = n // 2; base = base + part * n
        return self.out.at[pl.ds(pl.multiple_of(base, 16), n)]
    def ok(self, k):
        if not k: return None
        return (self.io.z + k >= 0) & (self.io.z + k <= 3)
    def move(self, name, i, m, k, bit, part=None, src=None):
        ref = lambda: self.at(m, k, part)
        io = self.io
        io.start(self.slot[k][name][i], src or ref, ref, (io.dp ^ bit, io.z), self.ok(k))
    def got(self, name, i, m, k, part=None):
        self.io.arrived(self.slot[k][name][i], lambda: self.at(m, k, part), self.ok(k))
    def start_z(self):
        io = self.io
        self.local.start()
        mine = lambda: self.shard
        to = lambda: self.at(0, 0)
        io.start(self.z_slot[-1], mine, to, (io.dp, io.z + 1), io.z < 3)
        io.start(self.z_slot[1], mine, to, (io.dp, io.z - 1), io.z > 0)
    def pass_z(self, e):
        io = self.io
        for s in (-1, 1):
            k = s * e
            ref = lambda k=k: self.at(0, k)
            io.arrived(self.z_slot[k], ref, self.ok(k))
            if e < 3:
                to = io.z - s
                io.start(self.z_slot[s * (e + 1)], ref, ref, (io.dp, to), self.ok(k) & (to >= 0) & (to <= 3))
    def spread(self, k):
        src = (lambda: self.shard) if k == 0 else None
        self.move("x", 0, 0, k, 2, src=src)
        self.move("y", 0, 0, k, 4, src=src)
        self.move("own", 0, 0, k, 1, src=src)
    def pass_on(self, k):
        self.got("x", 0, 2, k)
        self.move("d", 0, 2, k, 4, 0)
        self.got("y", 0, 4, k)
        self.move("d", 1, 4, k, 2, 1)
        self.move("cx", 0, 2, k, 1)
        self.move("cy", 0, 4, k, 1)
    def far(self, k):
        for h in range(2):
            self.got("d", h, 6, k, h)
            self.move("cd", h, 6, k, 1, h)
    def done(self, k):
        self.got("own", 0, 1, k)
        self.got("cx", 0, 3, k)
        self.got("cy", 0, 5, k)
        for h in range(2): self.got("cd", h, 7, k, h)

class Collect:
    def __init__(self, io, src, dst, local):
        self.io, self.src, self.dst = io, src, dst
        self.slots = io.slots(4)
        self.local = local
        self.rows = src.shape[1]
        self.host = self.valid(io.z)
    def part(self, s): return self.dst.at[pl.ds(s * self.rows, self.rows)]
    def valid(self, z):
        clip = z - self.io.dp % 2
        return (clip >= 0) & (clip < 3)
    def start(self):
        io = self.io
        for s in range(4):
            to = (io.z + s) % 4
            src = lambda to=to: self.src.at[jnp.clip(to - io.dp % 2, 0, 2)]
            if s == 0:
                guarded(self.host, lambda: pltpu.make_async_copy(src(), self.part(0), self.local).start())
            else:
                io.start(self.slots[s], src, lambda s=s: self.part(s), (io.dp, to), self.valid(to))
    def wait(self):
        guarded(self.host, lambda: pltpu.make_async_copy(self.part(0), self.part(0), self.local).wait())
        for s in range(1, 4):
            self.io.arrived(self.slots[s], lambda s=s: self.part(s), self.host)

N_SLOTS = 140
def gather_kernel(a, u, d, x, c, wa, wu, wd, xb, cb, zero, send, recv, local):
    io = Copies(send, recv)
    ga, gu, gd = Gather(io, a, wa, True, local.at[0]), Gather(io, u, wu, False, local.at[1]), Gather(io, d, wd, False, local.at[2])
    cx, cc = Collect(io, x, xb, local.at[3]), Collect(io, c, cb, local.at[4])
    assert io.n <= N_SLOTS, io.n
    bar = pltpu.get_barrier_semaphore()
    partners = [(io.dp, io.z ^ k) for k in (1, 2, 3)] + [(io.dp ^ b, io.z) for b in (1, 2, 4)]
    for p in partners: pl.semaphore_signal(bar, inc=1, device_id=p, device_id_type=MESH)
    zero[...] = jnp.zeros_like(zero)
    pl.semaphore_wait(bar, len(partners))
    ga.start_z(); ga.spread(0)
    ga.local.wait()
    ga.pass_z(1); ga.spread(-1); ga.spread(1)
    ga.pass_on(0)
    ga.pass_z(2); ga.spread(-2); ga.spread(2)
    gu.start_z()
    ga.far(0)
    ga.pass_on(-1); ga.pass_on(1)
    ga.pass_z(3); ga.spread(-3); ga.spread(3)
    gu.pass_z(1)
    ga.far(-1); ga.far(1)
    gu.pass_z(2)
    cx.start()
    ga.pass_on(-2); ga.pass_on(2)
    gu.pass_z(3)
    gu.local.wait()
    gu.spread(None)
    ga.far(-2); ga.far(2)
    gd.start_z()
    ga.pass_on(-3); ga.pass_on(3)
    ga.far(-3); ga.far(3)
    for i in ga.keys: ga.done(i)
    gd.pass_z(1)
    cx.wait()
    gd.pass_z(2)
    gd.pass_z(3)
    gd.local.wait()
    gd.spread(None)
    cc.start()
    gu.pass_on(None)
    gu.far(None)
    gu.done(None)
    cc.wait()
    gd.pass_on(None)
    gd.far(None)
    gd.done(None)
    for col in (cx, cc):
        def fill():
            cp = pltpu.make_async_copy(zero, col.dst, local.at[5])
            cp.start(); cp.wait()
        guarded(jnp.logical_not(col.host), fill)
    io.finish()

def gather_all(a, u, d, x, c):
    t = x.shape[1]*4
    any_ = pl.BlockSpec(memory_space=pl.ANY)
    sh = lambda r, c_: jax.ShapeDtypeStruct((r, c_), BF)
    return pl.pallas_call(gather_kernel,
        out_shape=[sh(32*a.shape[0], a.shape[1]), sh(32*u.shape[0], u.shape[1]), sh(32*d.shape[0], d.shape[1]), sh(t,1024), sh(t,1024)],
        in_specs=[any_]*5, out_specs=[any_]*5,
        scratch_shapes=[pltpu.VMEM((t,1024),BF), pltpu.SemaphoreType.DMA((N_SLOTS,)), pltpu.SemaphoreType.DMA((N_SLOTS,)), pltpu.SemaphoreType.DMA((8,))],
        compiler_params=pltpu.CompilerParams(collective_id=0, has_side_effects=True, vmem_limit_bytes=56*2**20))(a,u,d,x,c)


class Reduce:
    def __init__(self, io, r, s, land, pieces, stage, out):
        self.io, self.r, self.s, self.land, self.pieces = io, r, s, land, pieces
        self.stage, self.out = stage, out
        self.slot = io.slots(6)
        self.z_slot = io.slots(4)

    def half(self, j, h):
        return self.s(j).at[pl.ds(h * 2 * self.r, 2 * self.r)]

    def send(self, i, j, h, bit):
        io = self.io
        io.start(self.slot[i], lambda: self.half(j, h), lambda: self.land.at[i], (io.dp ^ bit, io.z))

    def start(self):
        self.send(0, 3, 0, 2)
        self.send(1, 3, 1, 4)
        self.send(2, 1, 0, 2)
        self.send(3, 2, 1, 4)

    def load(self, i, at):
        self.io.arrived(self.slot[i], lambda: self.land.at[i])
        return self.io.load(self.land.at[i], self.stage.at[at])

    def relay(self):
        for i, j, h, bit in ((0, 2, 0, 4), (1, 1, 1, 2)):
            self.load(i, i).wait()
            ref = self.half(j, h)
            ref[...] = (ref[...].astype(F32) + self.stage[i].astype(F32)).astype(ref.dtype)
            self.send(5 - i, j, h, bit)

    def fold(self):
        io, r = self.io, self.r
        for i in (0, 1):
            io.sent_wait(self.slot[i])
        for h, (a, b) in enumerate(((2, 5), (4, 3))):
            one, two = self.load(a, 0), self.load(b, 1)
            one.wait()
            two.wait()
            own = self.half(0, h)[...]
            total = own.astype(F32) + self.stage[0].astype(F32) + self.stage[1].astype(F32)
            self.half(3, h)[...] = total.astype(own.dtype)
        for k in (1, 2, 3):
            io.start(
                self.z_slot[k],
                lambda k=k: self.piece(io.z ^ k),
                lambda k=k: self.pieces.at[k],
                (io.dp, io.z ^ k),
            )

    def piece(self, z):
        return self.s(3).at[pl.ds(pl.multiple_of(z * self.r, self.r), self.r)]

    def finish(self):
        io, r = self.io, self.r
        spots = [self.stage.at[i, pl.ds(h * r, r)] for i, h in ((0, 0), (0, 1), (1, 0))]
        loads = []
        for k in (1, 2, 3):
            io.arrived(self.z_slot[k], lambda k=k: self.pieces.at[k])
            loads.append(io.load(self.pieces.at[k], spots[k - 1]))
        total = self.piece(io.z)[...].astype(F32)
        for copy, spot in zip(loads, spots):
            copy.wait()
            total = total + spot[...].astype(F32)
        self.out[...] = total


class HandBack:
    def __init__(self, io, src, dst):
        self.io, self.src, self.dst = io, src, dst
        self.slots = io.slots(4)
        self.rows = dst.shape[1]

    def host(self, z):
        clip = z - self.io.dp % 2
        return (clip >= 0) & (clip < 3)

    def part(self, s):
        return self.src.at[pl.ds(s * self.rows, self.rows)]

    def start(self):
        io = self.io
        for s in range(1, 4):
            to = (io.z + 4 - s) % 4
            io.start(
                self.slots[s], lambda s=s: self.part(s), lambda s=s: self.dst.at[s], (io.dp, to), self.host(io.z)
            )
        copy = io.load(self.part(0), self.dst.at[0])
        copy.wait()

    def wait(self):
        io = self.io
        for s in range(1, 4):
            io.arrived(self.slots[s], lambda s=s: self.dst.at[s], self.host((io.z + s) % 4))


N_BACK = 120
N_LOCAL = 112


def norm_rows(v):
    center = v - jnp.mean(v, axis=-1, keepdims=True)
    r = lax.rsqrt(jnp.mean(center * center, axis=-1, keepdims=True) + EPSILON)
    return center * r, r


def backward_kernel(
    wa, wu, wd, og, x, middle, normed1, normed2, qkv_in, attended, hidden, slope, gain1, gain2, d_bias,
    a_out, u_out, d_out, s_out, ret_out, ret_in, a_land, u_land, d_land, s_land, a_pieces, u_pieces, d_pieces, s_pieces,
    og2, ug2, bg2, hj2, np2, n1p2, atp2, flip, qkv, ag, xv, part, wdb, wb, tiles, acc, s_d, s_u, stage_d, stage_u,
    table, table_sib, s_s, stage_s, vec, ub,
    send, recv, local, ready,
):
    io = Copies(send, recv, local)
    dp, z = io.dp, io.z
    t = og.shape[0]
    own, sib = pl.ds(0, t), pl.ds(t, t)
    core = (dp ^ 1, z)

    red_d = Reduce(io, d_out.shape[0], lambda j: s_d.at[j], d_land, d_pieces, stage_d, d_out)
    red_u = Reduce(io, u_out.shape[0], lambda j: s_u.at[j], u_land, u_pieces, stage_u, u_out)
    n_a = a_out.shape[0]
    red_a = Reduce(io, n_a, lambda j: ug2.at[pl.ds(j * 4 * n_a, 4 * n_a)], a_land, a_pieces, stage_u, a_out)
    red_s = Reduce(io, s_out.shape[0], lambda j: s_s.at[j], s_land, s_pieces, stage_s, s_out)
    back_in = HandBack(io, qkv.at[:, pl.ds(D, D)], ret_in)
    back_out = HandBack(io, qkv.at[:, pl.ds(0, D)], ret_out)

    bar = pltpu.get_barrier_semaphore()
    partners = [(dp, z ^ k) for k in (1, 2, 3)] + [(dp ^ b, z) for b in (1, 2, 4)]
    for p in partners:
        pl.semaphore_signal(bar, inc=1, device_id=p, device_id_type=MESH)

    def planes(src, dst):
        width = dst.shape[1] // 4
        return [
            io.load(
                src.at[:, pl.ds(pl.multiple_of((dp ^ (2 * j)) * width, LANES), width)],
                dst.at[own, pl.ds(j * width, width)],
            )
            for j in range(4)
        ]

    first = [io.load(og, og2.at[own])] + planes(hidden, hj2.at[:, pl.ds(0, FF // 2)])
    pl.semaphore_wait(bar, len(partners))

    def swap_planes(src, dst):
        width = dst.shape[1] // 4
        slots = io.slots(4)
        for j in range(4):
            io.start(
                slots[j],
                lambda j=j: src.at[:, pl.ds(pl.multiple_of((dp ^ (2 * j + 1)) * width, LANES), width)],
                lambda j=j: dst.at[sib, pl.ds(j * width, width)],
                core,
            )
        return [(slots[j], lambda j=j: dst.at[sib, pl.ds(j * width, width)]) for j in range(4)]

    og_slot = io.slots(1)[0]
    io.start(og_slot, lambda: og, lambda: og2.at[sib], core)
    swapped_h = swap_planes(hidden, hj2.at[:, pl.ds(0, FF // 2)])
    swapped_2 = swap_planes(normed2, np2)
    swapped_1 = swap_planes(normed1, n1p2) + swap_planes(attended, atp2)
    second = planes(normed2, np2)
    second_half = t
    d_rows = wdb.shape[1]
    w_rows = wb.shape[1]

    def stream(n, copies, body):
        base = io.locals(2 * len(copies(0, 0)))

        def make(i, slot):
            pairs = copies(i, slot)
            return [
                pltpu.make_async_copy(a, b, io.local.at[base + 2 * c + slot]) for c, (a, b) in enumerate(pairs)
            ]

        for c in make(0, 0):
            c.start()

        def step(i, _):
            slot = i % 2

            @pl.when(i + 1 < n)
            def _():
                for c in make(i + 1, (i + 1) % 2):
                    c.start()

            for c in make(i, slot):
                c.wait()
            body(i, slot)
            return 0

        lax.fori_loop(0, n, step, 0)

    def lanes(i, width):
        return pl.ds(pl.multiple_of(i * width, LANES), width)

    for c in first:
        c.wait()
    io.arrived(og_slot, lambda: og2.at[sib])
    for slot, ref in swapped_h:
        io.arrived(slot, ref)
    third = planes(normed1, n1p2) + planes(attended, atp2)
    third += [io.load(qkv_in, qkv), io.load(x, xv), io.load(middle, part)]
    width = FF // 8
    for j in (3, 1, 2, 0):
        s_d[j] = dot_tn(hj2[:, j * width : (j + 1) * width], og2[...]).astype(BF)
        if j == 3:
            red_d.send(0, 3, 0, 2)
            red_d.send(1, 3, 1, 4)
        elif j == 1:
            red_d.send(2, 1, 0, 2)
        elif j == 2:
            red_d.send(3, 2, 1, 4)
    pl.semaphore_signal(ready, inc=1, device_id=core, device_id_type=MESH)
    vec[7:8] = jnp.sum(og2[own].astype(F32), axis=0, keepdims=True)

    ug_slots = io.slots(FF // d_rows)

    def ug_copy(i):
        return io.remote(ug_slots[0] + i, ug2.at[own, lanes(i, d_rows)], ug2.at[sib, lanes(i, d_rows)], core)

    def hidden_step(i, slot):
        grad = dot_nt(og2[own], wdb[slot]) * tiles[slot].astype(F32)
        low = grad.astype(BF)
        ug2[own, lanes(i, d_rows)] = low
        ub[:, lanes(i, d_rows)] = jnp.sum(low.astype(F32), axis=0, keepdims=True)
        ug_copy(i).start()

    stream(
        FF // d_rows,
        lambda i, slot: [
            (wd.at[pl.ds(pl.multiple_of(i * d_rows, d_rows), d_rows)], wdb.at[slot]),
            (slope.at[:, lanes(i, d_rows)], tiles.at[slot]),
        ],
        hidden_step,
    )

    for c in second:
        c.wait()
    for slot, ref in swapped_2:
        io.arrived(slot, ref)
    flip[...] = np2[...].T
    for i in range(FF // d_rows):
        ug_copy(i).wait_recv()

    def up_step(i, _):
        block = dot(flip[...], ug2[:, lanes(i, 512)]).astype(BF)
        for j in range(4):
            s_u[j, :, lanes(i, 512)] = block[j * LANES : (j + 1) * LANES]
        return 0

    lax.fori_loop(0, FF // 512, up_step, 0)
    red_u.start()
    red_d.relay()

    def up_back(i, slot):
        acc[:, lanes(i, w_rows)] = dot_nt(ug2[own], wb[slot, :, 0:FF])

    w_tile = lambda ref, lo, n: lambda i, slot: [
        (ref.at[pl.ds(pl.multiple_of(i * w_rows, w_rows), w_rows), pl.ds(lo, n)], wb.at[slot, :, pl.ds(0, n)])
    ]
    stream(D // w_rows, w_tile(wu, 0, FF), up_back)
    for c in third:
        c.wait()
    for i in (0, 1, 4, 5, 6):
        vec[i : i + 1] = jnp.zeros((1, D), F32)
    chunk = 128

    def second_norm(i, _):
        rows = pl.ds(pl.multiple_of(i * chunk, chunk), chunk)
        e = acc[rows]
        vhat, r = norm_rows(part[rows])
        g = e * gain2[...]
        grad = r * (
            g - jnp.mean(g, axis=-1, keepdims=True) - vhat * jnp.mean(g * vhat, axis=-1, keepdims=True)
        )
        vec[5:6] += jnp.sum(e * vhat, axis=0, keepdims=True)
        vec[6:7] += jnp.sum(e, axis=0, keepdims=True)
        part[rows] = grad
        low = (og2[rows].astype(F32) + grad).astype(BF)
        bg2[rows] = low
        vec[4:5] += jnp.sum(low.astype(F32), axis=0, keepdims=True)
        return 0

    lax.fori_loop(0, t // chunk, second_norm, 0)
    bg_slot = io.slots(1)[0]
    io.start(bg_slot, lambda: bg2.at[own], lambda: bg2.at[sib], core)

    def proj_back(i, slot):
        ag[:, lanes(i, w_rows)] = dot_nt(bg2[own], wb[slot, :, 0:D]).astype(BF)

    stream(D // w_rows, w_tile(wa, 3 * D, D), proj_back)

    def heads(i, _):
        def at(k):
            return lanes(k * (D // LANES) + i, LANES)

        dq, dk, dv = attend_back_pair(qkv[:, at(0)], qkv[:, at(1)], qkv[:, at(2)], ag[:, at(0)])
        for k, grad in enumerate((dq, dk, dv)):
            hj2[own, at(k)] = grad
        vec[2:3, at(0)] = jnp.sum(dq.astype(F32), axis=0, keepdims=True)
        vec[3:4, at(0)] = jnp.sum(dv.astype(F32), axis=0, keepdims=True)
        return 0

    lax.fori_loop(0, D // LANES, heads, 0)
    jn_slot = io.slots(1)[0]
    pl.semaphore_wait(ready, 1)
    io.start(jn_slot, lambda: hj2.at[own], lambda: hj2.at[sib], core)
    red_u.relay()
    red_d.fold()

    def qkv_back(i, slot):
        acc[:, lanes(i, w_rows)] = dot_nt(hj2[own], wb[slot, :, 0 : 3 * D])

    stream(D // w_rows, w_tile(wa, 0, 3 * D), qkv_back)

    def first_norm(i, _):
        rows = pl.ds(pl.multiple_of(i * chunk, chunk), chunk)
        e = acc[rows]
        vhat, r = norm_rows(xv[rows].astype(F32))
        g = e * gain1[...]
        grad = r * (
            g - jnp.mean(g, axis=-1, keepdims=True) - vhat * jnp.mean(g * vhat, axis=-1, keepdims=True)
        )
        vec[0:1] += jnp.sum(e * vhat, axis=0, keepdims=True)
        vec[1:2] += jnp.sum(e, axis=0, keepdims=True)
        qkv[rows, D : 2 * D] = (part[rows] + grad).astype(BF)
        return 0

    lax.fori_loop(0, t // chunk, first_norm, 0)
    back_in.start()

    spread_n = lax.broadcasted_iota(jnp.int32, (32, D), 0)
    spread_c = lax.broadcasted_iota(jnp.int32, (32, D), 1)
    mine = (spread_c // 32) == spread_n
    pick_c = lax.broadcasted_iota(jnp.int32, (D, LANES), 0)
    pick_l = lax.broadcasted_iota(jnp.int32, (D, LANES), 1)
    table[...] = jnp.zeros_like(table)
    for k in range(2):
        rows = jnp.zeros((32, LANES), F32)
        for q in range(4):
            spread = jnp.where(mine, vec[4 * k + q : 4 * k + q + 1], 0.0)
            pick = jnp.where(pick_l == 32 * q + pick_c % 32, 1.0, 0.0)
            rows = rows + jnp.dot(spread, pick, preferred_element_type=F32, precision=lax.Precision.HIGHEST)
        for n in range(32):
            table[8 * n + k : 8 * n + k + 1] = rows[n : n + 1]
    for n in range(32):
        table[8 * n + 2 : 8 * n + 3] = ub[:, n * LANES : (n + 1) * LANES]
    table_slot = io.slots(1)[0]
    io.start(table_slot, lambda: table, lambda: table_sib, core)

    for slot in range(FF // d_rows):
        ug_copy(slot).wait_send()
    for slot, ref in swapped_1:
        io.arrived(slot, ref)
    flip[...] = atp2[...].T
    io.arrived(bg_slot, lambda: bg2.at[sib])

    def proj_step(i, _):
        block = dot(flip[...], bg2[:, lanes(i, 512)]).astype(BF)
        ug2[own, lanes(6 + i, 512)] = block
        return 0

    lax.fori_loop(0, D // 512, proj_step, 0)
    flip[...] = n1p2[...].T
    io.arrived(jn_slot, lambda: hj2.at[sib])

    def qkv_step(i, _):
        block = dot(flip[...], hj2[:, lanes(i, 512)]).astype(BF)
        ug2[own, lanes(i, 512)] = block
        return 0

    lax.fori_loop(0, 3 * D // 512, qkv_step, 0)
    red_a.start()
    io.arrived(table_slot, lambda: table_sib)
    for j in range(4):
        rows = pl.ds(pl.multiple_of((dp ^ (2 * j)) * 32, 32), 32)
        s_s[j] = table[rows] + table_sib[rows]
    red_s.start()
    red_d.finish()

    load_middle = io.load(middle, part)
    acc[...] = jnp.zeros_like(acc)

    def down_step(i, slot):
        acc[...] += dot(tiles[slot], wdb[slot])

    stream(
        FF // d_rows,
        lambda i, slot: [
            (wd.at[pl.ds(pl.multiple_of(i * d_rows, d_rows), d_rows)], wdb.at[slot]),
            (hidden.at[:, lanes(i, d_rows)], tiles.at[slot]),
        ],
        down_step,
    )
    load_middle.wait()
    qkv[:, 0:D] = (acc[...] + (part[...] - xv[...].astype(F32)) + d_bias[...]).astype(BF)
    back_out.start()

    red_u.fold()
    red_s.relay()
    red_a.relay()
    red_u.finish()
    red_s.fold()
    red_a.fold()
    red_s.finish()
    back_in.wait()
    back_out.wait()
    red_a.finish()
    io.finish()


def backward(wa, wu, wd, og, x, middle, normed1, normed2, qkv, attended, hidden, slope, gain1, gain2, d_bias):
    t = og.shape[0]
    any_ = pl.BlockSpec(memory_space=pl.ANY)
    vmem = pl.BlockSpec(memory_space=pltpu.VMEM)
    sh = jax.ShapeDtypeStruct
    ra, rd, rs = D // 32, FF // 32, 8
    outs = [
        (sh((ra, FF), F32), vmem),
        (sh((ra, FF), F32), vmem),
        (sh((rd, D), F32), vmem),
        (sh((rs, LANES), F32), vmem),
        (sh((4, t // 4, D), BF), any_),
        (sh((4, t // 4, D), BF), any_),
    ]
    for count, k in ((6, 2), (4, 1)):
        outs += [
            (sh((count, k * ra, FF), BF), any_),
            (sh((count, k * ra, FF), BF), any_),
            (sh((count, k * rd, D), BF), any_),
            (sh((count, k * rs, LANES), F32), any_),
        ]
    v = pltpu.VMEM
    results = pl.pallas_call(
        backward_kernel,
        out_shape=[o for o, _ in outs],
        in_specs=[any_] * 12 + [vmem] * 3,
        out_specs=[o for _, o in outs],
        scratch_shapes=[
            v((2 * t, D), BF),
            v((2 * t, FF), BF),
            v((2 * t, D), BF),
            v((2 * t, 3 * D), BF),
            v((2 * t, D // 2), BF),
            v((2 * t, D // 2), BF),
            v((2 * t, D // 2), BF),
            v((D // 2, 2 * t), BF),
            v((t, 3 * D), BF),
            v((t, D), BF),
            v((t, D), BF),
            v((t, D), F32),
            v((2, 512, D), BF),
            v((2, 256, FF), BF),
            v((2, t, 512), BF),
            v((t, D), F32),
            v((4, 4 * rd, D), BF),
            v((4, 4 * ra, FF), BF),
            v((2, 2 * rd, D), BF),
            v((2, 2 * ra, FF), BF),
            v((32 * rs, LANES), F32),
            v((32 * rs, LANES), F32),
            v((4, 4 * rs, LANES), F32),
            v((2, 2 * rs, LANES), F32),
            v((8, D), F32),
            v((1, FF), F32),
            pltpu.SemaphoreType.DMA((N_BACK,)),
            pltpu.SemaphoreType.DMA((N_BACK,)),
            pltpu.SemaphoreType.DMA((N_LOCAL,)),
            pltpu.SemaphoreType.REGULAR,
        ],
        compiler_params=pltpu.CompilerParams(
            collective_id=1, has_side_effects=True, vmem_limit_bytes=60 * 2**20
        ),
    )(wa, wu, wd, og, x, middle, normed1, normed2, qkv, attended, hidden, slope, gain1, gain2, d_bias)
    return results[:6]


def norm_parts(v):
    center = v - jnp.mean(v, axis=-1, keepdims=True)
    r = lax.rsqrt(jnp.mean(center * center, axis=-1, keepdims=True) + EPSILON)
    return center * r, r


def norm_back(vhat, r, gain, e):
    t = e * gain
    grad = r * (
        t - jnp.mean(t, axis=-1, keepdims=True) - vhat * jnp.mean(t * vhat, axis=-1, keepdims=True)
    )
    return grad, jnp.sum(e * vhat, axis=0), jnp.sum(e, axis=0)


def gelu_both(u):
    cdf = 0.5 * (1.0 + lax.erf(u * 0.7071067811865476))
    pdf = 0.3989422804014327 * jnp.exp(-0.5 * u * u)
    return u * cdf, cdf + u * pdf


SMALL = (D, D, D, D, D, D, D, D, FF)


def per_device(
    n_dp,
    n_seq,
    clips,
    counts,
    out_cotangent,
    norm1_gain,
    norm1_shift,
    qkv_weight,
    query_bias,
    value_bias,
    proj_weight,
    proj_bias,
    norm2_gain,
    norm2_shift,
    up_weight,
    up_bias,
    down_weight,
    down_bias,
):
    links = Links(n_dp, n_seq)
    n = n_dp * n_seq
    slots = clips.shape[0]
    rows = D // n
    small = (
        norm1_gain,
        norm1_shift,
        query_bias,
        value_bias,
        proj_bias,
        norm2_gain,
        norm2_shift,
        down_bias,
        up_bias,
    )
    packed = jnp.concatenate(small)
    packed = jnp.pad(packed, (0, rows * LANES - packed.shape[0])).reshape(rows, LANES)
    shard_a = jnp.concatenate(
        [qkv_weight.reshape(rows, 3 * D), proj_weight.reshape(rows, D), packed], axis=1
    ).astype(BF)
    shard_u = up_weight.reshape(rows, FF).astype(BF)
    shard_d = down_weight.reshape(FF // n, D).astype(BF)

    living = (jnp.arange(slots) < counts[0]).astype(F32)[:, None, None]
    living_cot = living * out_cotangent
    tokens = (clips.astype(BF), living_cot.astype(BF))
    if links.short:
        a_mat, u_mat, d_mat, x, out_grad = gather_all(shard_a, shard_u, shard_d, *tokens)
    else:
        a_mat, u_mat, d_mat = (links.gather(shard) for shard in (shard_a, shard_u, shard_d))
        x, out_grad = (links.collect(t) for t in tokens)
    x = x.astype(F32)

    table = a_mat[:, 4 * D :].reshape(n_dp, n_seq, rows * LANES)
    table = table.reshape(n, rows * LANES).astype(F32)
    vectors, at = [], 0
    for size in SMALL:
        vectors.append(table[:, at : at + size // n].reshape(size))
        at += size // n
    gain1, shift1, q_bias, v_bias, p_bias, gain2, shift2, d_bias, u_bias = vectors

    vhat1, r1 = norm_parts(x)
    normed1 = (vhat1 * gain1 + shift1).astype(BF)
    qkv_bias = jnp.concatenate([q_bias, jnp.zeros_like(q_bias), v_bias])
    qkv_mat, proj_mat = a_mat[:, : 3 * D], a_mat[:, 3 * D : 4 * D]
    qkv = (dot(normed1, qkv_mat) + qkv_bias).astype(BF)
    attended = attend(qkv)
    branch = dot(attended, proj_mat) + p_bias
    middle = x + branch
    vhat2, r2 = norm_parts(middle)
    normed2 = (vhat2 * gain2 + shift2).astype(BF)
    hidden, slope = gelu_both(dot(normed2, u_mat) + u_bias)
    hidden = hidden.astype(BF)
    slope = slope.astype(BF)
    if links.short:
        row = lambda v: v.reshape(1, -1)
        qkv_proj_grad, up_grad, down_grad, small_grad, out_back, in_back = backward(
            a_mat,
            u_mat,
            d_mat,
            out_grad,
            x.astype(BF),
            middle,
            normed1,
            normed2,
            qkv,
            attended,
            hidden,
            slope,
            row(gain1),
            row(gain2),
            row(d_bias),
        )
        out_home, in_home = links.by_clip(out_back, slots), links.by_clip(in_back, slots)
        small_out = small_grad[:3].reshape(-1)
    else:
        out_part = branch + dot(hidden, d_mat) + d_bias
        out_home = links.hand_back(out_part.astype(BF), slots)
        down_grad = links.reduce(dot_tn(hidden, out_grad))
        upper_grad = (dot_nt(out_grad, d_mat) * slope).astype(BF)
        up_grad = links.reduce(dot_tn(normed2, upper_grad))
        part, gain2_grad, shift2_grad = norm_back(vhat2, r2, gain2, dot_nt(upper_grad, u_mat))
        branch_grad = (out_grad.astype(F32) + part).astype(BF)
        dq, dk, dv = attend_back(qkv, dot_nt(branch_grad, proj_mat).astype(BF))
        joined = jnp.concatenate([dq, dk, dv], axis=1)
        first_part, gain1_grad, shift1_grad = norm_back(vhat1, r1, gain1, dot_nt(joined, qkv_mat))
        in_home = links.hand_back((part + first_part).astype(BF), slots)
        total = lambda g: jnp.sum(g.astype(F32), axis=0)
        small_grads = (
            gain1_grad,
            shift1_grad,
            total(dq),
            total(dv),
            total(branch_grad),
            gain2_grad,
            shift2_grad,
            total(out_grad),
            total(upper_grad),
        )
        grad_table = jnp.concatenate([g.reshape(n, -1) for g in small_grads], axis=1)
        width = grad_table.shape[1]
        grad_table = jnp.pad(grad_table, ((0, 0), (0, rows * LANES - width)))
        d_a = [dot_tn(normed1, joined), dot_tn(attended, branch_grad), grad_table.reshape(n * rows, LANES)]
        a_grad = links.reduce(jnp.concatenate(d_a, axis=1))
        qkv_proj_grad, small_out = a_grad[:, : 4 * D], a_grad[:, 4 * D :].reshape(-1)
    block_out = living * (clips + out_home.astype(F32))
    input_grad = living_cot + in_home.astype(F32)
    pieces, at = [], 0
    for size in SMALL:
        pieces.append(small_out[at : at + size // n])
        at += size // n
    g1, s1, qb, vb, pb, g2, s2, db, ub = pieces
    return (
        block_out,
        input_grad,
        g1,
        s1,
        qkv_proj_grad[:, : 3 * D].reshape(-1),
        qb,
        vb,
        qkv_proj_grad[:, 3 * D :].reshape(-1),
        pb,
        g2,
        s2,
        up_grad.reshape(-1),
        ub,
        down_grad.reshape(-1),
        db,
    )


def solution(mesh):
    flat = P(AXES)
    tokens = P("dp", "seq", None)
    return jax.shard_map(
        functools.partial(per_device, mesh.shape["dp"], mesh.shape["seq"]),
        mesh=mesh,
        in_specs=(tokens, P("dp"), tokens) + (flat,) * 13,
        out_specs=(tokens, tokens) + (flat,) * 13,
        check_vma=False,
    )
```

```python
import functools

import jax
import jax.numpy as jnp
from jax import lax
from jax.experimental import pallas as pl
from jax.experimental.pallas import tpu as pltpu
from jax.sharding import PartitionSpec as P

D = 1024
FF = 4096
HEADS = 16
HEAD_DIM = 64
EPSILON = 1e-05
LANES = 128
BF = jnp.bfloat16
F32 = jnp.float32
AXES = ("dp", "seq")
MESH = pl.DeviceIdType.MESH


def dot(a, b):
    return jnp.dot(a, b, preferred_element_type=F32)


def dot_nt(a, b):
    return lax.dot_general(a, b, (((1,), (1,)), ((), ())), preferred_element_type=F32)


def dot_tn(a, b):
    return lax.dot_general(a, b, (((0,), (0,)), ((), ())), preferred_element_type=F32)


def soft_t(q2, k_half):
    scores = dot_nt(k_half, q2) * (HEAD_DIM**-0.5)
    top = jnp.max(scores, axis=0, keepdims=True)
    e = jnp.exp(scores - top)
    return e * (1.0 / jnp.sum(e, axis=0, keepdims=True))


def attend_pair(q2, k2, v2):
    low = lax.broadcasted_iota(jnp.int32, k2.shape, 1) < HEAD_DIM
    v_t = v2.T
    zero = jnp.zeros_like(k2)
    parts = []
    for h in range(2):
        k_half = jnp.where(low == (h == 0), k2, zero)
        p_t = soft_t(q2, k_half).astype(BF)
        parts.append(dot(v_t[h * HEAD_DIM : (h + 1) * HEAD_DIM], p_t))
    return jnp.concatenate(parts, axis=0).T.astype(BF)


def attend_kernel(q_ref, k_ref, v_ref, o_ref):
    o_ref[...] = attend_pair(q_ref[...], k_ref[...], v_ref[...])


def attend(qkv):
    t = qkv.shape[0]
    n = D // LANES
    spec = lambda off: pl.BlockSpec((t, LANES), lambda h: (0, off + h))
    return pl.pallas_call(
        attend_kernel,
        grid=(n,),
        out_shape=jax.ShapeDtypeStruct((t, D), BF),
        in_specs=[spec(0), spec(n), spec(2 * n)],
        out_specs=spec(0),
        compiler_params=pltpu.CompilerParams(vmem_limit_bytes=48 * 2**20),
        cost_estimate=pl.CostEstimate(
            flops=16 * 4 * t * t * HEAD_DIM, bytes_accessed=8 * t * D, transcendentals=16 * t * t
        ),
    )(qkv, qkv, qkv)


def attend_back_pair(q2, k2, v2, do2):
    low = lax.broadcasted_iota(jnp.int32, k2.shape, 1) < HEAD_DIM
    k_t = k2.T
    zero = jnp.zeros_like(k2)
    dq, dk, dv = [], [], []
    for h in range(2):
        mine = low == (h == 0)
        p = soft_t(q2, jnp.where(mine, k2, zero))
        dp = dot_nt(jnp.where(mine, v2, zero), do2)
        total = jnp.sum(p * dp, axis=0, keepdims=True)
        ds = (p * (dp - total)).astype(BF)
        dv.append(dot(p.astype(BF), do2))
        dk.append(dot(ds, q2))
        dq.append(dot(k_t[h * HEAD_DIM : (h + 1) * HEAD_DIM], ds))
    scale = HEAD_DIM**-0.5
    return (
        (jnp.concatenate(dq, axis=0).T * scale).astype(BF),
        (jnp.where(low, dk[0], dk[1]) * scale).astype(BF),
        jnp.where(low, dv[0], dv[1]).astype(BF),
    )


def attend_back_kernel(q_ref, k_ref, v_ref, do_ref, dq_ref, dk_ref, dv_ref):
    grads = attend_back_pair(q_ref[...], k_ref[...], v_ref[...], do_ref[...])
    dq_ref[...], dk_ref[...], dv_ref[...] = grads


def attend_back(qkv, do):
    t = qkv.shape[0]
    n = D // LANES
    spec = lambda off: pl.BlockSpec((t, LANES), lambda h: (0, off + h))
    return pl.pallas_call(
        attend_back_kernel,
        grid=(n,),
        out_shape=[jax.ShapeDtypeStruct((t, D), BF)] * 3,
        in_specs=[spec(0), spec(n), spec(2 * n), spec(0)],
        out_specs=[spec(0)] * 3,
        compiler_params=pltpu.CompilerParams(vmem_limit_bytes=48 * 2**20),
        cost_estimate=pl.CostEstimate(
            flops=16 * 10 * t * t * HEAD_DIM, bytes_accessed=14 * t * D, transcendentals=16 * t * t
        ),
    )(qkv, qkv, qkv, do)


class Links:
    def __init__(self, n_dp, n_seq):
        self.n_dp, self.n_seq = n_dp, n_seq
        self.short = n_dp == 8 and n_seq == 4
        self.dp = lax.axis_index("dp")
        self.z = lax.axis_index("seq")

    def gather(self, shard):
        return lax.all_gather(shard, AXES, axis=0, tiled=True)

    def reduce(self, grad):
        return lax.psum_scatter(grad.astype(BF), AXES, scatter_dimension=0, tiled=True).astype(F32)


    def lead(self, d, slots):
        return d % 2 if self.n_seq > slots else 0

    def shift_pairs(self, s, slots):
        n = self.n_seq
        pairs = []
        for d in range(self.n_dp):
            for z in range(n):
                to = (z + s) % n
                if 0 <= to - self.lead(d, slots) < slots:
                    pairs.append((d * n + z, d * n + to))
        return pairs

    def my_clip(self, slots):
        lead = self.dp % 2 if self.n_seq > slots else 0
        return self.z - lead

    def collect(self, x):
        slots, n = x.shape[0], self.n_seq
        clip = self.my_clip(slots)
        parts = []
        for s in range(n):
            lead = self.z - clip
            index = jnp.clip((self.z + s) % n - lead, 0, slots - 1)
            part = lax.dynamic_index_in_dim(x, index, 0, False)
            parts.append(part if s == 0 else lax.ppermute(part, AXES, self.shift_pairs(s, slots)))
        host = (clip >= 0) & (clip < slots)
        return jnp.where(host, jnp.concatenate(parts), jnp.zeros((), x.dtype))

    def hand_back(self, y, slots):
        n = self.n_seq
        rows = y.shape[0] // n
        back = []
        for s in range(n):
            part = y[s * rows : (s + 1) * rows]
            pairs = [(b, a) for a, b in self.shift_pairs(s, slots)]
            back.append(part if s == 0 else lax.ppermute(part, AXES, pairs))
        return self.by_clip(jnp.stack(back), slots)

    def by_clip(self, back, slots):
        n = self.n_seq
        lead = self.z - self.my_clip(slots)
        return jnp.stack(
            [lax.dynamic_index_in_dim(back, (c + lead - self.z) % n, 0, False) for c in range(slots)]
        )


def norm_rows(v):
    center = v - jnp.mean(v, axis=-1, keepdims=True)
    r = lax.rsqrt(jnp.mean(center * center, axis=-1, keepdims=True) + EPSILON)
    return center * r, r


def gelu_both(u):
    cdf = 0.5 * (1.0 + lax.erf(u * 0.7071067811865476))
    pdf = 0.3989422804014327 * jnp.exp(-0.5 * u * u)
    return u * cdf, cdf + u * pdf


def guarded(cond, f):
    if cond is None: f()
    else: pl.when(cond)(f)

class Copies:
    def __init__(self, send, recv, local=None):
        self.send, self.recv, self.n, self.sent = send, recv, 0, []
        self.local, self.n_local = local, 0
        self.dp, self.z = lax.axis_index("dp"), lax.axis_index("seq")
    def slots(self, k):
        self.n += k
        return list(range(self.n - k, self.n))
    def remote(self, slot, src, dst, dev):
        return pltpu.make_async_remote_copy(src_ref=src, dst_ref=dst, send_sem=self.send.at[slot], recv_sem=self.recv.at[slot], device_id=dev, device_id_type=MESH)
    def start(self, slot, src, dst, dev, cond=None):
        guarded(cond, lambda: self.remote(slot, src(), dst(), dev).start())
        self.sent.append((slot, src, dst, dev, cond))
    def arrived(self, slot, dst, cond=None):
        guarded(cond, lambda: self.remote(slot, dst(), dst(), (self.dp ^ 1, self.z)).wait_recv())
    def sent_wait(self, which=None):
        rest = []
        for slot, src, dst, dev, cond in self.sent:
            if which is None or slot == which:
                guarded(cond, lambda: self.remote(slot, src(), dst(), dev).wait_send())
            else:
                rest.append((slot, src, dst, dev, cond))
        self.sent = rest
    def finish(self):
        self.sent_wait()
    def locals(self, k):
        self.n_local += k
        return self.n_local - k
    def load(self, src, dst):
        copy = pltpu.make_async_copy(src, dst, self.local.at[self.locals(1)])
        copy.start()
        return copy


class Gather:
    def __init__(self, io, shard, out):
        self.io, self.shard, self.out = io, shard, out
        self.r = shard.shape[0]
        self.local = io.load(shard, self.at(0, 0))
        self.keys = (0, 1, 2, 3)
        self.z_slot = io.slots(4)
        self.slot = {k: {name: io.slots(2) for name in ("x", "y", "d", "own", "cx", "cy", "cd")} for k in self.keys}

    def at(self, m, k, part=None):
        io, r = self.io, self.r
        base, n = ((io.dp ^ m) * 4 + (io.z ^ k)) * r, r
        if part is not None:
            n = n // 2
            base = base + part * n
        return self.out.at[pl.ds(pl.multiple_of(base, 16), n)]

    def move(self, name, i, m, k, bit, part=None, src=None):
        io = self.io
        ref = lambda: self.at(m, k, part)
        io.start(self.slot[k][name][i], src or ref, ref, (io.dp ^ bit, io.z))

    def got(self, name, i, m, k, part=None):
        self.io.arrived(self.slot[k][name][i], lambda: self.at(m, k, part))

    def start_z(self):
        io = self.io
        for k in (1, 2):
            io.start(self.z_slot[k], lambda: self.shard, lambda: self.at(0, 0), (io.dp, io.z ^ k))

    def arrive_z(self, k):
        io = self.io
        ref = lambda: self.at(0, k)
        io.arrived(self.z_slot[k], ref)
        if k == 2:
            io.start(self.z_slot[3], ref, ref, (io.dp, io.z ^ 1))

    def spread(self, k):
        src = (lambda: self.shard) if k == 0 else None
        self.move("x", 0, 0, k, 2, src=src)
        self.move("y", 0, 0, k, 4, src=src)
        self.move("own", 0, 0, k, 1, src=src)

    def pass_on(self, k):
        self.got("x", 0, 2, k)
        self.move("d", 0, 2, k, 4, 0)
        self.got("y", 0, 4, k)
        self.move("d", 1, 4, k, 2, 1)
        self.move("cx", 0, 2, k, 1)
        self.move("cy", 0, 4, k, 1)

    def far(self, k):
        for h in range(2):
            self.got("d", h, 6, k, h)
            self.move("cd", h, 6, k, 1, h)

    def done(self):
        for k in self.keys:
            self.got("own", 0, 1, k)
            self.got("cx", 0, 3, k)
            self.got("cy", 0, 5, k)
            for h in range(2):
                self.got("cd", h, 7, k, h)


class Collect:
    def __init__(self, io, src, dst):
        self.io, self.src, self.dst = io, src, dst
        self.slots = io.slots(4)
        self.local = io.locals(1)
        self.rows = src.shape[1]
        self.host = self.valid(io.z)

    def part(self, s):
        return self.dst.at[pl.ds(s * self.rows, self.rows)]

    def valid(self, z):
        clip = z - self.io.dp % 2
        return (clip >= 0) & (clip < 3)

    def start(self):
        io = self.io
        for s in range(4):
            to = (io.z + s) % 4
            src = lambda to=to: self.src.at[jnp.clip(to - io.dp % 2, 0, 2)]
            if s == 0:
                copy = lambda: pltpu.make_async_copy(src(), self.part(0), io.local.at[self.local]).start()
                guarded(self.host, copy)
            else:
                io.start(self.slots[s], src, lambda s=s: self.part(s), (io.dp, to), self.valid(to))

    def wait(self):
        io = self.io
        copy = lambda: pltpu.make_async_copy(self.part(0), self.part(0), io.local.at[self.local]).wait()
        guarded(self.host, copy)
        for s in range(1, 4):
            io.arrived(self.slots[s], lambda s=s: self.part(s), self.host)

        def clear():
            self.dst[...] = jnp.zeros_like(self.dst)

        guarded(jnp.logical_not(self.host), clear)


N_FORE = 200
CHUNK = 128
COLS = 512


def stream(io, n, copies, body):
    base = io.locals(2 * len(copies(0, 0)))

    def make(i, slot):
        return [
            pltpu.make_async_copy(a, b, io.local.at[base + 2 * c + slot])
            for c, (a, b) in enumerate(copies(i, slot))
        ]

    for c in make(0, 0):
        c.start()

    def step(i, _):
        slot = i % 2

        @pl.when(i + 1 < n)
        def _():
            for c in make(i + 1, (i + 1) % 2):
                c.start()

        for c in make(i, slot):
            c.wait()
        body(i, slot)
        return 0

    lax.fori_loop(0, n, step, 0)


def lanes(i, width):
    return pl.ds(pl.multiple_of(i * width, LANES), width)


def meet(io):
    bar = pltpu.get_barrier_semaphore()
    partners = [(io.dp, io.z ^ k) for k in (1, 2, 3)] + [(io.dp ^ b, io.z) for b in (1, 2, 4)]
    for p in partners:
        pl.semaphore_signal(bar, inc=1, device_id=p, device_id_type=MESH)
    pl.semaphore_wait(bar, len(partners))


def spread_vectors(table, wide, vec, ub):
    wide[...] = table[...].astype(F32)
    spread_n = lax.broadcasted_iota(jnp.int32, (32, D), 0)
    spread_c = lax.broadcasted_iota(jnp.int32, (32, D), 1)
    mine = (spread_c // 32) == spread_n
    pick_l = lax.broadcasted_iota(jnp.int32, (LANES, D), 0)
    pick_c = lax.broadcasted_iota(jnp.int32, (LANES, D), 1)
    for k in range(2):
        rows = jnp.concatenate([wide[32 * n + k : 32 * n + k + 1] for n in range(32)], axis=0).astype(BF)
        for q in range(4):
            pick = jnp.where(pick_l == 32 * q + pick_c % 32, 1.0, 0.0).astype(BF)
            spread = jnp.where(mine, dot(rows, pick), 0.0)
            vec[4 * k + q : 4 * k + q + 1] = jnp.sum(spread, axis=0, keepdims=True)
    for n in range(32):
        ub[:, n * LANES : (n + 1) * LANES] = wide[32 * n + 2 : 32 * n + 3]


def forward_kernel(
    a, u, d, clips, cot,
    wa, wu, wd, og, x_out, middle_out, n1_out, n2_out, qkv_out, att_out, hidden, slope, vec,
    xv, ogv, n1, n2, qkv, att, middle, wb, hid, slo, table, wide, ub, bias,
    send, recv, local,
):
    io = Copies(send, recv, local)
    ga, gu, gd = Gather(io, a, wa), Gather(io, u, wu), Gather(io, d, wd)
    cx, cc = Collect(io, clips, xv), Collect(io, cot, ogv)
    t = xv.shape[0]
    meet(io)

    line = [(g, k) for g in (ga, gu, gd) for k in range(4)]
    place = [0]

    def advance(n=1):
        for _ in range(n):
            i = place[0]
            place[0] += 1
            if i < len(line):
                g, k = line[i]
                if k == 2 and g is not gd:
                    g.arrive_z(2)
                    (gu if g is ga else gd).start_z()
                    if g is ga:
                        cx.start()
                    else:
                        cc.start()
                elif k:
                    g.arrive_z(k)
                g.spread(k)
            if 1 <= i <= len(line):
                g, k = line[i - 1]
                g.pass_on(k)
            if 3 <= i <= len(line) + 2:
                g, k = line[i - 3]
                g.far(k)

    ga.start_z()
    advance(3)
    for g in (ga, gu, gd):
        g.local.wait()
    advance(4)
    outs = []

    ga.done()
    io.load(wa.at[:, pl.ds(4 * D, LANES)], table).wait()
    spread_vectors(table, wide, vec, ub)
    bias[:, 0:D] = vec[2:3]
    bias[:, D : 2 * D] = jnp.zeros((1, D), F32)
    bias[:, 2 * D : 3 * D] = vec[3:4]
    cx.wait()
    outs.append(io.load(xv, x_out))

    def first_norm(i, _):
        rows = pl.ds(pl.multiple_of(i * CHUNK, CHUNK), CHUNK)
        vhat, _r = norm_rows(xv[rows].astype(F32))
        n1[rows] = (vhat * vec[0:1] + vec[1:2]).astype(BF)
        return 0

    lax.fori_loop(0, t // CHUNK, first_norm, 0)
    outs.append(io.load(n1, n1_out))
    advance()

    def columns(ref, lo):
        return lambda i, slot: [(ref.at[:, pl.ds(pl.multiple_of(lo + i * COLS, LANES), COLS)], wb.at[slot])]

    def qkv_step(i, slot):
        qkv[:, lanes(i, COLS)] = (dot(n1[...], wb[slot]) + bias[:, lanes(i, COLS)]).astype(BF)

    stream(io, 3 * D // COLS, columns(wa, 0), qkv_step)
    outs.append(io.load(qkv, qkv_out))
    advance()

    def heads(i, _):
        def at(k):
            return lanes(k * (D // LANES) + i, LANES)

        att[:, at(0)] = attend_pair(qkv[:, at(0)], qkv[:, at(1)], qkv[:, at(2)])
        return 0

    n_pairs = D // LANES
    lax.fori_loop(0, n_pairs // 2, heads, 0)
    advance()
    lax.fori_loop(n_pairs // 2, n_pairs, heads, 0)
    outs.append(io.load(att, att_out))
    advance()

    def proj_step(i, slot):
        cols = lanes(i, COLS)
        middle[:, cols] = xv[:, cols].astype(F32) + (dot(att[...], wb[slot]) + vec[4:5, cols])

    stream(io, D // COLS, columns(wa, 3 * D), proj_step)
    outs.append(io.load(middle, middle_out))

    def second_norm(i, _):
        rows = pl.ds(pl.multiple_of(i * CHUNK, CHUNK), CHUNK)
        vhat, _r = norm_rows(middle[rows])
        n2[rows] = (vhat * vec[5:6] + vec[6:7]).astype(BF)
        return 0

    lax.fori_loop(0, t // CHUNK, second_norm, 0)
    outs.append(io.load(n2, n2_out))
    while place[0] < 7 + 4:
        advance()
    gu.done()

    out_base = io.locals(4)

    def hidden_out(i, slot):
        return [
            pltpu.make_async_copy(buf.at[slot], out.at[:, lanes(i, COLS)], io.local.at[out_base + 2 * c + slot])
            for c, (buf, out) in enumerate(((hid, hidden), (slo, slope)))
        ]

    def up_step(i, slot):
        @pl.when(i >= 2)
        def _():
            for c in hidden_out(i - 2, slot):
                c.wait()

        value, grad = gelu_both(dot(n2[...], wb[slot]) + ub[:, lanes(i, COLS)])
        hid[slot] = value.astype(BF)
        slo[slot] = grad.astype(BF)
        for c in hidden_out(i, slot):
            c.start()

    n_up = FF // COLS
    stream(io, n_up // 2, columns(wu, 0), up_step)
    advance()
    stream(io, n_up // 2, columns(wu, FF // 2), lambda i, slot: up_step(i + n_up // 2, slot))
    for i in (n_up - 2, n_up - 1):
        for c in hidden_out(i, i % 2):
            c.wait()
    cc.wait()
    outs.append(io.load(ogv, og))
    while place[0] < len(line) + 3:
        advance()
    gd.done()
    for c in outs:
        c.wait()
    io.finish()


def forward(a, u, d, clips, cot):
    t = clips.shape[1] * 4
    any_ = pl.BlockSpec(memory_space=pl.ANY)
    vmem = pl.BlockSpec(memory_space=pltpu.VMEM)
    sh = jax.ShapeDtypeStruct
    v = pltpu.VMEM
    return pl.pallas_call(
        forward_kernel,
        out_shape=[
            sh((D, a.shape[1]), BF),
            sh((D, FF), BF),
            sh((FF, D), BF),
            sh((t, D), BF),
            sh((t, D), BF),
            sh((t, D), F32),
            sh((t, D), BF),
            sh((t, D), BF),
            sh((t, 3 * D), BF),
            sh((t, D), BF),
            sh((t, FF), BF),
            sh((t, FF), BF),
            sh((8, D), F32),
        ],
        in_specs=[any_] * 5,
        out_specs=[any_] * 12 + [vmem],
        scratch_shapes=[
            v((t, D), BF),
            v((t, D), BF),
            v((t, D), BF),
            v((t, D), BF),
            v((t, 3 * D), BF),
            v((t, D), BF),
            v((t, D), F32),
            v((2, D, COLS), BF),
            v((2, t, COLS), BF),
            v((2, t, COLS), BF),
            v((D, LANES), BF),
            v((D, LANES), F32),
            v((1, FF), F32),
            v((1, 3 * D), F32),
            pltpu.SemaphoreType.DMA((N_FORE,)),
            pltpu.SemaphoreType.DMA((N_FORE,)),
            pltpu.SemaphoreType.DMA((48,)),
        ],
        compiler_params=pltpu.CompilerParams(
            collective_id=0, has_side_effects=True, vmem_limit_bytes=56 * 2**20
        ),
    )(a, u, d, clips, cot)


class Reduce:
    def __init__(self, io, r, s, land, pieces, stage, out):
        self.io, self.r, self.s, self.land, self.pieces = io, r, s, land, pieces
        self.stage, self.out = stage, out
        self.slot = io.slots(6)
        self.z_slot = io.slots(4)

    def half(self, j, h):
        return self.s(j).at[pl.ds(h * 2 * self.r, 2 * self.r)]

    def send(self, i, j, h, bit):
        io = self.io
        io.start(self.slot[i], lambda: self.half(j, h), lambda: self.land.at[i], (io.dp ^ bit, io.z))

    def start(self):
        self.send(0, 3, 0, 2)
        self.send(1, 3, 1, 4)
        self.send(2, 1, 0, 2)
        self.send(3, 2, 1, 4)

    def load(self, i, at):
        self.io.arrived(self.slot[i], lambda: self.land.at[i])
        return self.io.load(self.land.at[i], self.stage.at[at])

    def relay(self):
        for i, j, h, bit in ((0, 2, 0, 4), (1, 1, 1, 2)):
            self.load(i, i).wait()
            ref = self.half(j, h)
            ref[...] = (ref[...].astype(F32) + self.stage[i].astype(F32)).astype(ref.dtype)
            self.send(5 - i, j, h, bit)

    def fold(self):
        io, r = self.io, self.r
        for i in (0, 1):
            io.sent_wait(self.slot[i])
        for h, (a, b) in enumerate(((2, 5), (4, 3))):
            one, two = self.load(a, 0), self.load(b, 1)
            one.wait()
            two.wait()
            own = self.half(0, h)[...]
            total = own.astype(F32) + self.stage[0].astype(F32) + self.stage[1].astype(F32)
            self.half(3, h)[...] = total.astype(own.dtype)
        for i, k in ((0, 3), (1, 1)):
            io.start(
                self.z_slot[i],
                lambda k=k: self.piece(io.z ^ k),
                lambda i=i: self.pieces.at[i],
                (io.dp, io.z ^ 1),
            )

    def piece(self, z):
        return self.s(3).at[pl.ds(pl.multiple_of(z * self.r, self.r), self.r)]

    def take(self, i):
        spot = self.stage.at[i // 2, pl.ds(i % 2 * self.r, self.r)]
        self.io.arrived(self.z_slot[i], lambda: self.pieces.at[i])
        return self.io.load(self.pieces.at[i], spot), spot

    def cross(self):
        io = self.io
        copy, spot = self.take(0)
        copy.wait()
        ref = self.piece(io.z ^ 2)
        ref[...] = (ref[...].astype(F32) + spot[...].astype(F32)).astype(ref.dtype)
        io.start(
            self.z_slot[2], lambda: self.piece(io.z ^ 2), lambda: self.pieces.at[2], (io.dp, io.z ^ 2)
        )

    def finish(self):
        one, two = self.take(1), self.take(2)
        total = self.piece(self.io.z)[...].astype(F32)
        for copy, spot in (one, two):
            copy.wait()
            total = total + spot[...].astype(F32)
        self.out[...] = total


class HandBack:
    def __init__(self, io, src, dst):
        self.io, self.src, self.dst = io, src, dst
        self.slots = io.slots(4)
        self.rows = dst.shape[1]

    def host(self, z):
        clip = z - self.io.dp % 2
        return (clip >= 0) & (clip < 3)

    def part(self, s):
        return self.src.at[pl.ds(s * self.rows, self.rows)]

    def start(self):
        io = self.io
        for s in range(1, 4):
            to = (io.z + 4 - s) % 4
            io.start(
                self.slots[s], lambda s=s: self.part(s), lambda s=s: self.dst.at[s], (io.dp, to), self.host(io.z)
            )
        copy = io.load(self.part(0), self.dst.at[0])
        copy.wait()

    def wait(self):
        io = self.io
        for s in range(1, 4):
            io.arrived(self.slots[s], lambda s=s: self.dst.at[s], self.host((io.z + s) % 4))


N_BACK = 120
N_LOCAL = 112


def backward_kernel(
    wa, wu, wd, og, x, middle, normed1, normed2, qkv_in, attended, hidden, slope, params,
    a_out, u_out, d_out, s_out, ret_out, ret_in, a_land, u_land, d_land, s_land, a_pieces, u_pieces, d_pieces, s_pieces,
    og2, ug2, bg2, hj2, np2, n1p2, atp2, flip, qkv, ag, xv, part, wdb, wb, tiles, acc, s_d, s_u, stage_d, stage_u,
    table, table_sib, s_s, stage_s, vec, ub,
    send, recv, local, ready,
):
    io = Copies(send, recv, local)
    dp, z = io.dp, io.z
    t = og.shape[0]
    own, sib = pl.ds(0, t), pl.ds(t, t)
    core = (dp ^ 1, z)

    red_d = Reduce(io, d_out.shape[0], lambda j: s_d.at[j], d_land, d_pieces, stage_d, d_out)
    red_u = Reduce(io, u_out.shape[0], lambda j: s_u.at[j], u_land, u_pieces, stage_u, u_out)
    n_a = a_out.shape[0]
    red_a = Reduce(io, n_a, lambda j: ug2.at[pl.ds(j * 4 * n_a, 4 * n_a)], a_land, a_pieces, stage_u, a_out)
    red_s = Reduce(io, s_out.shape[0], lambda j: s_s.at[j], s_land, s_pieces, stage_s, s_out)
    back_in = HandBack(io, qkv.at[:, pl.ds(D, D)], ret_in)
    back_out = HandBack(io, qkv.at[:, pl.ds(0, D)], ret_out)

    bar = pltpu.get_barrier_semaphore()
    partners = [(dp, z ^ k) for k in (1, 2, 3)] + [(dp ^ b, z) for b in (1, 2, 4)]
    for p in partners:
        pl.semaphore_signal(bar, inc=1, device_id=p, device_id_type=MESH)

    def planes(src, dst):
        width = dst.shape[1] // 4
        return [
            io.load(
                src.at[:, pl.ds(pl.multiple_of((dp ^ (2 * j)) * width, LANES), width)],
                dst.at[own, pl.ds(j * width, width)],
            )
            for j in range(4)
        ]

    first = [io.load(og, og2.at[own])] + planes(hidden, hj2.at[:, pl.ds(0, FF // 2)])
    pl.semaphore_wait(bar, len(partners))

    def swap_planes(src, dst):
        width = dst.shape[1] // 4
        slots = io.slots(4)
        for j in range(4):
            io.start(
                slots[j],
                lambda j=j: src.at[:, pl.ds(pl.multiple_of((dp ^ (2 * j + 1)) * width, LANES), width)],
                lambda j=j: dst.at[sib, pl.ds(j * width, width)],
                core,
            )
        return [(slots[j], lambda j=j: dst.at[sib, pl.ds(j * width, width)]) for j in range(4)]

    og_slot = io.slots(1)[0]
    io.start(og_slot, lambda: og, lambda: og2.at[sib], core)
    swapped_h = swap_planes(hidden, hj2.at[:, pl.ds(0, FF // 2)])
    swapped_2 = swap_planes(normed2, np2)
    swapped_1 = swap_planes(normed1, n1p2) + swap_planes(attended, atp2)
    second = planes(normed2, np2)
    second_half = t
    d_rows = wdb.shape[1]
    w_rows = wb.shape[1]

    for c in first:
        c.wait()
    io.arrived(og_slot, lambda: og2.at[sib])
    for slot, ref in swapped_h:
        io.arrived(slot, ref)
    third = planes(normed1, n1p2) + planes(attended, atp2)
    third += [io.load(qkv_in, qkv), io.load(x, xv), io.load(middle, part)]
    width = FF // 8
    for j in (3, 1, 2, 0):
        s_d[j] = dot_tn(hj2[:, j * width : (j + 1) * width], og2[...]).astype(BF)
        if j == 3:
            red_d.send(0, 3, 0, 2)
            red_d.send(1, 3, 1, 4)
        elif j == 1:
            red_d.send(2, 1, 0, 2)
        elif j == 2:
            red_d.send(3, 2, 1, 4)
    pl.semaphore_signal(ready, inc=1, device_id=core, device_id_type=MESH)
    vec[7:8] = jnp.sum(og2[own].astype(F32), axis=0, keepdims=True)

    ug_slots = io.slots(FF // d_rows)

    def ug_copy(i):
        return io.remote(ug_slots[0] + i, ug2.at[own, lanes(i, d_rows)], ug2.at[sib, lanes(i, d_rows)], core)

    def hidden_step(i, slot):
        grad = dot_nt(og2[own], wdb[slot]) * tiles[slot].astype(F32)
        low = grad.astype(BF)
        ug2[own, lanes(i, d_rows)] = low
        ub[:, lanes(i, d_rows)] = jnp.sum(low.astype(F32), axis=0, keepdims=True)
        ug_copy(i).start()

    stream(
        io,
        FF // d_rows,
        lambda i, slot: [
            (wd.at[pl.ds(pl.multiple_of(i * d_rows, d_rows), d_rows)], wdb.at[slot]),
            (slope.at[:, lanes(i, d_rows)], tiles.at[slot]),
        ],
        hidden_step,
    )

    for c in second:
        c.wait()
    for slot, ref in swapped_2:
        io.arrived(slot, ref)
    flip[...] = np2[...].T
    for i in range(FF // d_rows):
        ug_copy(i).wait_recv()

    def up_step(i, _):
        block = dot(flip[...], ug2[:, lanes(i, 512)]).astype(BF)
        for j in range(4):
            s_u[j, :, lanes(i, 512)] = block[j * LANES : (j + 1) * LANES]
        return 0

    lax.fori_loop(0, FF // 512, up_step, 0)
    red_u.start()
    red_d.relay()

    def up_back(i, slot):
        acc[:, lanes(i, w_rows)] = dot_nt(ug2[own], wb[slot, :, 0:FF])

    w_tile = lambda ref, lo, n: lambda i, slot: [
        (ref.at[pl.ds(pl.multiple_of(i * w_rows, w_rows), w_rows), pl.ds(lo, n)], wb.at[slot, :, pl.ds(0, n)])
    ]
    stream(io, D // w_rows, w_tile(wu, 0, FF), up_back)
    for c in third:
        c.wait()
    for i in (0, 1, 4, 5, 6):
        vec[i : i + 1] = jnp.zeros((1, D), F32)
    chunk = 128

    def second_norm(i, _):
        rows = pl.ds(pl.multiple_of(i * chunk, chunk), chunk)
        e = acc[rows]
        vhat, r = norm_rows(part[rows])
        g = e * params[5:6]
        grad = r * (
            g - jnp.mean(g, axis=-1, keepdims=True) - vhat * jnp.mean(g * vhat, axis=-1, keepdims=True)
        )
        vec[5:6] += jnp.sum(e * vhat, axis=0, keepdims=True)
        vec[6:7] += jnp.sum(e, axis=0, keepdims=True)
        part[rows] = grad
        low = (og2[rows].astype(F32) + grad).astype(BF)
        bg2[rows] = low
        vec[4:5] += jnp.sum(low.astype(F32), axis=0, keepdims=True)
        return 0

    lax.fori_loop(0, t // chunk, second_norm, 0)
    bg_slot = io.slots(1)[0]
    io.start(bg_slot, lambda: bg2.at[own], lambda: bg2.at[sib], core)

    def proj_back(i, slot):
        ag[:, lanes(i, w_rows)] = dot_nt(bg2[own], wb[slot, :, 0:D]).astype(BF)

    stream(io, D // w_rows, w_tile(wa, 3 * D, D), proj_back)

    def heads(i, _):
        def at(k):
            return lanes(k * (D // LANES) + i, LANES)

        dq, dk, dv = attend_back_pair(qkv[:, at(0)], qkv[:, at(1)], qkv[:, at(2)], ag[:, at(0)])
        for k, grad in enumerate((dq, dk, dv)):
            hj2[own, at(k)] = grad
        vec[2:3, at(0)] = jnp.sum(dq.astype(F32), axis=0, keepdims=True)
        vec[3:4, at(0)] = jnp.sum(dv.astype(F32), axis=0, keepdims=True)
        return 0

    n_pairs = D // LANES
    lax.fori_loop(0, n_pairs // 2, heads, 0)
    red_d.fold()
    lax.fori_loop(n_pairs // 2, n_pairs, heads, 0)
    jn_slot = io.slots(1)[0]
    pl.semaphore_wait(ready, 1)
    io.start(jn_slot, lambda: hj2.at[own], lambda: hj2.at[sib], core)
    red_u.relay()
    red_d.cross()

    def qkv_back(i, slot):
        acc[:, lanes(i, w_rows)] = dot_nt(hj2[own], wb[slot, :, 0 : 3 * D])

    stream(io, D // w_rows, w_tile(wa, 0, 3 * D), qkv_back)

    def first_norm(i, _):
        rows = pl.ds(pl.multiple_of(i * chunk, chunk), chunk)
        e = acc[rows]
        vhat, r = norm_rows(xv[rows].astype(F32))
        g = e * params[0:1]
        grad = r * (
            g - jnp.mean(g, axis=-1, keepdims=True) - vhat * jnp.mean(g * vhat, axis=-1, keepdims=True)
        )
        vec[0:1] += jnp.sum(e * vhat, axis=0, keepdims=True)
        vec[1:2] += jnp.sum(e, axis=0, keepdims=True)
        qkv[rows, D : 2 * D] = (part[rows] + grad).astype(BF)
        return 0

    lax.fori_loop(0, t // chunk, first_norm, 0)
    back_in.start()

    spread_n = lax.broadcasted_iota(jnp.int32, (32, D), 0)
    spread_c = lax.broadcasted_iota(jnp.int32, (32, D), 1)
    mine = (spread_c // 32) == spread_n
    pick_c = lax.broadcasted_iota(jnp.int32, (D, LANES), 0)
    pick_l = lax.broadcasted_iota(jnp.int32, (D, LANES), 1)
    table[...] = jnp.zeros_like(table)
    for k in range(2):
        rows = jnp.zeros((32, LANES), F32)
        for q in range(4):
            spread = jnp.where(mine, vec[4 * k + q : 4 * k + q + 1], 0.0)
            pick = jnp.where(pick_l == 32 * q + pick_c % 32, 1.0, 0.0)
            rows = rows + jnp.dot(spread, pick, preferred_element_type=F32, precision=lax.Precision.HIGHEST)
        for n in range(32):
            table[8 * n + k : 8 * n + k + 1] = rows[n : n + 1]
    for n in range(32):
        table[8 * n + 2 : 8 * n + 3] = ub[:, n * LANES : (n + 1) * LANES]
    table_slot = io.slots(1)[0]
    io.start(table_slot, lambda: table, lambda: table_sib, core)

    for slot in range(FF // d_rows):
        ug_copy(slot).wait_send()
    for slot, ref in swapped_1:
        io.arrived(slot, ref)
    flip[...] = atp2[...].T
    io.arrived(bg_slot, lambda: bg2.at[sib])

    def proj_step(i, _):
        block = dot(flip[...], bg2[:, lanes(i, 512)]).astype(BF)
        ug2[own, lanes(6 + i, 512)] = block
        return 0

    lax.fori_loop(0, D // 512, proj_step, 0)
    flip[...] = n1p2[...].T
    io.arrived(jn_slot, lambda: hj2.at[sib])

    def qkv_step(i, _):
        block = dot(flip[...], hj2[:, lanes(i, 512)]).astype(BF)
        ug2[own, lanes(i, 512)] = block
        return 0

    lax.fori_loop(0, 3 * D // 512, qkv_step, 0)
    red_a.start()
    io.arrived(table_slot, lambda: table_sib)
    for j in range(4):
        rows = pl.ds(pl.multiple_of((dp ^ (2 * j)) * 32, 32), 32)
        s_s[j] = table[rows] + table_sib[rows]
    red_s.start()
    red_d.finish()

    load_middle = io.load(middle, part)
    acc[...] = jnp.zeros_like(acc)

    def down_step(i, slot):
        acc[...] += dot(tiles[slot], wdb[slot])

    stream(
        io,
        FF // d_rows,
        lambda i, slot: [
            (wd.at[pl.ds(pl.multiple_of(i * d_rows, d_rows), d_rows)], wdb.at[slot]),
            (hidden.at[:, lanes(i, d_rows)], tiles.at[slot]),
        ],
        down_step,
    )
    load_middle.wait()
    qkv[:, 0:D] = (acc[...] + (part[...] - xv[...].astype(F32)) + params[7:8]).astype(BF)
    back_out.start()

    red_u.fold()
    red_u.cross()
    red_s.relay()
    red_a.relay()
    red_u.finish()
    red_s.fold()
    red_a.fold()
    red_s.cross()
    red_a.cross()
    red_s.finish()
    back_in.wait()
    back_out.wait()
    red_a.finish()
    io.finish()


def backward(wa, wu, wd, og, x, middle, normed1, normed2, qkv, attended, hidden, slope, params):
    t = og.shape[0]
    any_ = pl.BlockSpec(memory_space=pl.ANY)
    vmem = pl.BlockSpec(memory_space=pltpu.VMEM)
    sh = jax.ShapeDtypeStruct
    ra, rd, rs = D // 32, FF // 32, 8
    outs = [
        (sh((ra, FF), F32), vmem),
        (sh((ra, FF), F32), vmem),
        (sh((rd, D), F32), vmem),
        (sh((rs, LANES), F32), vmem),
        (sh((4, t // 4, D), BF), any_),
        (sh((4, t // 4, D), BF), any_),
    ]
    for count, k in ((6, 2), (3, 1)):
        outs += [
            (sh((count, k * ra, FF), BF), any_),
            (sh((count, k * ra, FF), BF), any_),
            (sh((count, k * rd, D), BF), any_),
            (sh((count, k * rs, LANES), F32), any_),
        ]
    v = pltpu.VMEM
    results = pl.pallas_call(
        backward_kernel,
        out_shape=[o for o, _ in outs],
        in_specs=[any_] * 12 + [vmem],
        out_specs=[o for _, o in outs],
        scratch_shapes=[
            v((2 * t, D), BF),
            v((2 * t, FF), BF),
            v((2 * t, D), BF),
            v((2 * t, 3 * D), BF),
            v((2 * t, D // 2), BF),
            v((2 * t, D // 2), BF),
            v((2 * t, D // 2), BF),
            v((D // 2, 2 * t), BF),
            v((t, 3 * D), BF),
            v((t, D), BF),
            v((t, D), BF),
            v((t, D), F32),
            v((2, 512, D), BF),
            v((2, 256, FF), BF),
            v((2, t, 512), BF),
            v((t, D), F32),
            v((4, 4 * rd, D), BF),
            v((4, 4 * ra, FF), BF),
            v((2, 2 * rd, D), BF),
            v((2, 2 * ra, FF), BF),
            v((32 * rs, LANES), F32),
            v((32 * rs, LANES), F32),
            v((4, 4 * rs, LANES), F32),
            v((2, 2 * rs, LANES), F32),
            v((8, D), F32),
            v((1, FF), F32),
            pltpu.SemaphoreType.DMA((N_BACK,)),
            pltpu.SemaphoreType.DMA((N_BACK,)),
            pltpu.SemaphoreType.DMA((N_LOCAL,)),
            pltpu.SemaphoreType.REGULAR,
        ],
        compiler_params=pltpu.CompilerParams(
            collective_id=1, has_side_effects=True, vmem_limit_bytes=60 * 2**20
        ),
    )(wa, wu, wd, og, x, middle, normed1, normed2, qkv, attended, hidden, slope, params)
    return results[:6]


def norm_parts(v):
    center = v - jnp.mean(v, axis=-1, keepdims=True)
    r = lax.rsqrt(jnp.mean(center * center, axis=-1, keepdims=True) + EPSILON)
    return center * r, r


def norm_back(vhat, r, gain, e):
    t = e * gain
    grad = r * (
        t - jnp.mean(t, axis=-1, keepdims=True) - vhat * jnp.mean(t * vhat, axis=-1, keepdims=True)
    )
    return grad, jnp.sum(e * vhat, axis=0), jnp.sum(e, axis=0)


SMALL = (D, D, D, D, D, D, D, D, FF)


def per_device(
    n_dp,
    n_seq,
    clips,
    counts,
    out_cotangent,
    norm1_gain,
    norm1_shift,
    qkv_weight,
    query_bias,
    value_bias,
    proj_weight,
    proj_bias,
    norm2_gain,
    norm2_shift,
    up_weight,
    up_bias,
    down_weight,
    down_bias,
):
    links = Links(n_dp, n_seq)
    n = n_dp * n_seq
    slots = clips.shape[0]
    rows = D // n
    small = (
        norm1_gain,
        norm1_shift,
        query_bias,
        value_bias,
        proj_bias,
        norm2_gain,
        norm2_shift,
        down_bias,
        up_bias,
    )
    packed = jnp.concatenate(small)
    packed = jnp.pad(packed, (0, rows * LANES - packed.shape[0])).reshape(rows, LANES)
    shard_a = jnp.concatenate(
        [qkv_weight.reshape(rows, 3 * D), proj_weight.reshape(rows, D), packed], axis=1
    ).astype(BF)
    shard_u = up_weight.reshape(rows, FF).astype(BF)
    shard_d = down_weight.reshape(FF // n, D).astype(BF)

    living = (jnp.arange(slots) < counts[0]).astype(F32)[:, None, None]
    living_cot = living * out_cotangent
    tokens = (clips.astype(BF), living_cot.astype(BF))
    if links.short:
        saved = forward(shard_a, shard_u, shard_d, *tokens)
        qkv_proj_grad, up_grad, down_grad, small_grad, out_back, in_back = backward(*saved)
        out_home, in_home = links.by_clip(out_back, slots), links.by_clip(in_back, slots)
        small_out = small_grad[:3].reshape(-1)
    else:
        a_mat, u_mat, d_mat = (links.gather(shard) for shard in (shard_a, shard_u, shard_d))
        x, out_grad = (links.collect(t) for t in tokens)
        x = x.astype(F32)

        table = a_mat[:, 4 * D :].reshape(n_dp, n_seq, rows * LANES)
        table = table.reshape(n, rows * LANES).astype(F32)
        vectors, at = [], 0
        for size in SMALL:
            vectors.append(table[:, at : at + size // n].reshape(size))
            at += size // n
        gain1, shift1, q_bias, v_bias, p_bias, gain2, shift2, d_bias, u_bias = vectors

        vhat1, r1 = norm_parts(x)
        normed1 = (vhat1 * gain1 + shift1).astype(BF)
        qkv_bias = jnp.concatenate([q_bias, jnp.zeros_like(q_bias), v_bias])
        qkv_mat, proj_mat = a_mat[:, : 3 * D], a_mat[:, 3 * D : 4 * D]
        qkv = (dot(normed1, qkv_mat) + qkv_bias).astype(BF)
        attended = attend(qkv)
        branch = dot(attended, proj_mat) + p_bias
        middle = x + branch
        vhat2, r2 = norm_parts(middle)
        normed2 = (vhat2 * gain2 + shift2).astype(BF)
        hidden, slope = gelu_both(dot(normed2, u_mat) + u_bias)
        hidden = hidden.astype(BF)
        slope = slope.astype(BF)
        out_part = branch + dot(hidden, d_mat) + d_bias
        out_home = links.hand_back(out_part.astype(BF), slots)
        down_grad = links.reduce(dot_tn(hidden, out_grad))
        upper_grad = (dot_nt(out_grad, d_mat) * slope).astype(BF)
        up_grad = links.reduce(dot_tn(normed2, upper_grad))
        part, gain2_grad, shift2_grad = norm_back(vhat2, r2, gain2, dot_nt(upper_grad, u_mat))
        branch_grad = (out_grad.astype(F32) + part).astype(BF)
        dq, dk, dv = attend_back(qkv, dot_nt(branch_grad, proj_mat).astype(BF))
        joined = jnp.concatenate([dq, dk, dv], axis=1)
        first_part, gain1_grad, shift1_grad = norm_back(vhat1, r1, gain1, dot_nt(joined, qkv_mat))
        in_home = links.hand_back((part + first_part).astype(BF), slots)
        total = lambda g: jnp.sum(g.astype(F32), axis=0)
        small_grads = (
            gain1_grad,
            shift1_grad,
            total(dq),
            total(dv),
            total(branch_grad),
            gain2_grad,
            shift2_grad,
            total(out_grad),
            total(upper_grad),
        )
        grad_table = jnp.concatenate([g.reshape(n, -1) for g in small_grads], axis=1)
        width = grad_table.shape[1]
        grad_table = jnp.pad(grad_table, ((0, 0), (0, rows * LANES - width)))
        d_a = [dot_tn(normed1, joined), dot_tn(attended, branch_grad), grad_table.reshape(n * rows, LANES)]
        a_grad = links.reduce(jnp.concatenate(d_a, axis=1))
        qkv_proj_grad, small_out = a_grad[:, : 4 * D], a_grad[:, 4 * D :].reshape(-1)
    block_out = living * (clips + out_home.astype(F32))
    input_grad = living_cot + in_home.astype(F32)
    pieces, at = [], 0
    for size in SMALL:
        pieces.append(small_out[at : at + size // n])
        at += size // n
    g1, s1, qb, vb, pb, g2, s2, db, ub = pieces
    return (
        block_out,
        input_grad,
        g1,
        s1,
        qkv_proj_grad[:, : 3 * D].reshape(-1),
        qb,
        vb,
        qkv_proj_grad[:, 3 * D :].reshape(-1),
        pb,
        g2,
        s2,
        up_grad.reshape(-1),
        ub,
        down_grad.reshape(-1),
        db,
    )


def solution(mesh):
    flat = P(AXES)
    tokens = P("dp", "seq", None)
    return jax.shard_map(
        functools.partial(per_device, mesh.shape["dp"], mesh.shape["seq"]),
        mesh=mesh,
        in_specs=(tokens, P("dp"), tokens) + (flat,) * 13,
        out_specs=(tokens, tokens) + (flat,) * 13,
        check_vma=False,
    )
```

```python
import functools

import jax
import jax.numpy as jnp
from jax import lax
from jax.experimental import pallas as pl
from jax.experimental.pallas import tpu as pltpu
from jax.sharding import PartitionSpec as P

D = 1024
FF = 4096
HEADS = 16
HEAD_DIM = 64
EPSILON = 1e-05
LANES = 128
BF = jnp.bfloat16
F32 = jnp.float32
AXES = ("dp", "seq")
MESH = pl.DeviceIdType.MESH


def dot(a, b):
    return jnp.dot(a, b, preferred_element_type=F32)


def dot_nt(a, b):
    return lax.dot_general(a, b, (((1,), (1,)), ((), ())), preferred_element_type=F32)


def dot_tn(a, b):
    return lax.dot_general(a, b, (((0,), (0,)), ((), ())), preferred_element_type=F32)


def soft_t(q2, k_half):
    scores = dot_nt(k_half, q2) * (HEAD_DIM**-0.5)
    top = jnp.max(scores, axis=0, keepdims=True)
    e = jnp.exp(scores - top)
    return e * (1.0 / jnp.sum(e, axis=0, keepdims=True))


def attend_pair(q2, k2, v2):
    low = lax.broadcasted_iota(jnp.int32, k2.shape, 1) < HEAD_DIM
    v_t = v2.T
    zero = jnp.zeros_like(k2)
    parts = []
    for h in range(2):
        k_half = jnp.where(low == (h == 0), k2, zero)
        p_t = soft_t(q2, k_half).astype(BF)
        parts.append(dot(v_t[h * HEAD_DIM : (h + 1) * HEAD_DIM], p_t))
    return jnp.concatenate(parts, axis=0).T.astype(BF)


def attend_kernel(q_ref, k_ref, v_ref, o_ref):
    o_ref[...] = attend_pair(q_ref[...], k_ref[...], v_ref[...])


def attend(qkv):
    t = qkv.shape[0]
    n = D // LANES
    spec = lambda off: pl.BlockSpec((t, LANES), lambda h: (0, off + h))
    return pl.pallas_call(
        attend_kernel,
        grid=(n,),
        out_shape=jax.ShapeDtypeStruct((t, D), BF),
        in_specs=[spec(0), spec(n), spec(2 * n)],
        out_specs=spec(0),
        compiler_params=pltpu.CompilerParams(vmem_limit_bytes=48 * 2**20),
        cost_estimate=pl.CostEstimate(
            flops=16 * 4 * t * t * HEAD_DIM, bytes_accessed=8 * t * D, transcendentals=16 * t * t
        ),
    )(qkv, qkv, qkv)


def attend_back_pair(q2, k2, v2, do2):
    low = lax.broadcasted_iota(jnp.int32, k2.shape, 1) < HEAD_DIM
    k_t = k2.T
    zero = jnp.zeros_like(k2)
    dq, dk, dv = [], [], []
    for h in range(2):
        mine = low == (h == 0)
        p = soft_t(q2, jnp.where(mine, k2, zero))
        dp = dot_nt(jnp.where(mine, v2, zero), do2)
        total = jnp.sum(p * dp, axis=0, keepdims=True)
        ds = (p * (dp - total)).astype(BF)
        dv.append(dot(p.astype(BF), do2))
        dk.append(dot(ds, q2))
        dq.append(dot(k_t[h * HEAD_DIM : (h + 1) * HEAD_DIM], ds))
    scale = HEAD_DIM**-0.5
    return (
        (jnp.concatenate(dq, axis=0).T * scale).astype(BF),
        (jnp.where(low, dk[0], dk[1]) * scale).astype(BF),
        jnp.where(low, dv[0], dv[1]).astype(BF),
    )


def attend_back_kernel(q_ref, k_ref, v_ref, do_ref, dq_ref, dk_ref, dv_ref):
    grads = attend_back_pair(q_ref[...], k_ref[...], v_ref[...], do_ref[...])
    dq_ref[...], dk_ref[...], dv_ref[...] = grads


def attend_back(qkv, do):
    t = qkv.shape[0]
    n = D // LANES
    spec = lambda off: pl.BlockSpec((t, LANES), lambda h: (0, off + h))
    return pl.pallas_call(
        attend_back_kernel,
        grid=(n,),
        out_shape=[jax.ShapeDtypeStruct((t, D), BF)] * 3,
        in_specs=[spec(0), spec(n), spec(2 * n), spec(0)],
        out_specs=[spec(0)] * 3,
        compiler_params=pltpu.CompilerParams(vmem_limit_bytes=48 * 2**20),
        cost_estimate=pl.CostEstimate(
            flops=16 * 10 * t * t * HEAD_DIM, bytes_accessed=14 * t * D, transcendentals=16 * t * t
        ),
    )(qkv, qkv, qkv, do)


class Links:
    def __init__(self, n_dp, n_seq):
        self.n_dp, self.n_seq = n_dp, n_seq
        self.short = n_dp == 8 and n_seq == 4
        self.dp = lax.axis_index("dp")
        self.z = lax.axis_index("seq")

    def gather(self, shard):
        return lax.all_gather(shard, AXES, axis=0, tiled=True)

    def reduce(self, grad):
        return lax.psum_scatter(grad.astype(BF), AXES, scatter_dimension=0, tiled=True).astype(F32)


    def lead(self, d, slots):
        return d % 2 if self.n_seq > slots else 0

    def shift_pairs(self, s, slots):
        n = self.n_seq
        pairs = []
        for d in range(self.n_dp):
            for z in range(n):
                to = (z + s) % n
                if 0 <= to - self.lead(d, slots) < slots:
                    pairs.append((d * n + z, d * n + to))
        return pairs

    def my_clip(self, slots):
        lead = self.dp % 2 if self.n_seq > slots else 0
        return self.z - lead

    def collect(self, x):
        slots, n = x.shape[0], self.n_seq
        clip = self.my_clip(slots)
        parts = []
        for s in range(n):
            lead = self.z - clip
            index = jnp.clip((self.z + s) % n - lead, 0, slots - 1)
            part = lax.dynamic_index_in_dim(x, index, 0, False)
            parts.append(part if s == 0 else lax.ppermute(part, AXES, self.shift_pairs(s, slots)))
        host = (clip >= 0) & (clip < slots)
        return jnp.where(host, jnp.concatenate(parts), jnp.zeros((), x.dtype))

    def hand_back(self, y, slots):
        n = self.n_seq
        rows = y.shape[0] // n
        back = []
        for s in range(n):
            part = y[s * rows : (s + 1) * rows]
            pairs = [(b, a) for a, b in self.shift_pairs(s, slots)]
            back.append(part if s == 0 else lax.ppermute(part, AXES, pairs))
        return self.by_clip(jnp.stack(back), slots)

    def by_clip(self, back, slots):
        n = self.n_seq
        lead = self.z - self.my_clip(slots)
        return jnp.stack(
            [lax.dynamic_index_in_dim(back, (c + lead - self.z) % n, 0, False) for c in range(slots)]
        )


def norm_rows(v):
    center = v - jnp.mean(v, axis=-1, keepdims=True)
    r = lax.rsqrt(jnp.mean(center * center, axis=-1, keepdims=True) + EPSILON)
    return center * r, r


def gelu_both(u):
    cdf = 0.5 * (1.0 + lax.erf(u * 0.7071067811865476))
    pdf = 0.3989422804014327 * jnp.exp(-0.5 * u * u)
    return u * cdf, cdf + u * pdf


def guarded(cond, f):
    if cond is None: f()
    else: pl.when(cond)(f)

class Copies:
    def __init__(self, send, recv, local=None):
        self.send, self.recv, self.n, self.sent = send, recv, 0, []
        self.local, self.n_local = local, 0
        self.dp, self.z = lax.axis_index("dp"), lax.axis_index("seq")
    def slots(self, k):
        self.n += k
        return list(range(self.n - k, self.n))
    def remote(self, slot, src, dst, dev):
        return pltpu.make_async_remote_copy(src_ref=src, dst_ref=dst, send_sem=self.send.at[slot], recv_sem=self.recv.at[slot], device_id=dev, device_id_type=MESH)
    def start(self, slot, src, dst, dev, cond=None):
        guarded(cond, lambda: self.remote(slot, src(), dst(), dev).start())
        self.sent.append((slot, src, dst, dev, cond))
    def arrived(self, slot, dst, cond=None):
        guarded(cond, lambda: self.remote(slot, dst(), dst(), (self.dp ^ 1, self.z)).wait_recv())
    def sent_wait(self, which=None):
        rest = []
        for slot, src, dst, dev, cond in self.sent:
            if which is None or slot == which:
                guarded(cond, lambda: self.remote(slot, src(), dst(), dev).wait_send())
            else:
                rest.append((slot, src, dst, dev, cond))
        self.sent = rest
    def finish(self):
        self.sent_wait()
    def locals(self, k):
        self.n_local += k
        return self.n_local - k
    def load(self, src, dst):
        copy = pltpu.make_async_copy(src, dst, self.local.at[self.locals(1)])
        copy.start()
        return copy


class Gather:
    def __init__(self, io, shard, out):
        self.io, self.shard, self.out = io, shard, out
        self.r = shard.shape[0]
        self.local = io.load(shard, self.at(0, 0))
        self.keys = (0, 1, 2, 3)
        self.z_slot = io.slots(4)
        self.slot = {k: {name: io.slots(2) for name in ("x", "y", "d", "own", "cx", "cy", "cd")} for k in self.keys}

    def at(self, m, k, part=None):
        io, r = self.io, self.r
        base, n = ((io.dp ^ m) * 4 + (io.z ^ k)) * r, r
        if part is not None:
            n = n // 2
            base = base + part * n
        return self.out.at[pl.ds(pl.multiple_of(base, 16), n)]

    def move(self, name, i, m, k, bit, part=None, src=None):
        io = self.io
        ref = lambda: self.at(m, k, part)
        io.start(self.slot[k][name][i], src or ref, ref, (io.dp ^ bit, io.z))

    def got(self, name, i, m, k, part=None):
        self.io.arrived(self.slot[k][name][i], lambda: self.at(m, k, part))

    def start_z(self):
        io = self.io
        for k in (1, 2):
            io.start(self.z_slot[k], lambda: self.shard, lambda: self.at(0, 0), (io.dp, io.z ^ k))

    def arrive_z(self, k):
        io = self.io
        ref = lambda: self.at(0, k)
        io.arrived(self.z_slot[k], ref)
        if k == 2:
            io.start(self.z_slot[3], ref, ref, (io.dp, io.z ^ 1))

    def spread(self, k):
        src = (lambda: self.shard) if k == 0 else None
        self.move("x", 0, 0, k, 2, src=src)
        self.move("y", 0, 0, k, 4, src=src)
        self.move("own", 0, 0, k, 1, src=src)

    def pass_on(self, k):
        self.got("x", 0, 2, k)
        self.move("d", 0, 2, k, 4, 0)
        self.got("y", 0, 4, k)
        self.move("d", 1, 4, k, 2, 1)
        self.move("cx", 0, 2, k, 1)
        self.move("cy", 0, 4, k, 1)

    def far(self, k):
        for h in range(2):
            self.got("d", h, 6, k, h)
            self.move("cd", h, 6, k, 1, h)

    def done(self):
        for k in self.keys:
            self.got("own", 0, 1, k)
            self.got("cx", 0, 3, k)
            self.got("cy", 0, 5, k)
            for h in range(2):
                self.got("cd", h, 7, k, h)


class Collect:
    def __init__(self, io, src, dst):
        self.io, self.src, self.dst = io, src, dst
        self.slots = io.slots(4)
        self.local = io.locals(1)
        self.rows = src.shape[1]
        self.host = self.valid(io.z)

    def part(self, s):
        return self.dst.at[pl.ds(s * self.rows, self.rows)]

    def valid(self, z):
        clip = z - self.io.dp % 2
        return (clip >= 0) & (clip < 3)

    def start(self):
        io = self.io
        for s in range(4):
            to = (io.z + s) % 4
            src = lambda to=to: self.src.at[jnp.clip(to - io.dp % 2, 0, 2)]
            if s == 0:
                copy = lambda: pltpu.make_async_copy(src(), self.part(0), io.local.at[self.local]).start()
                guarded(self.host, copy)
            else:
                io.start(self.slots[s], src, lambda s=s: self.part(s), (io.dp, to), self.valid(to))

    def wait(self):
        io = self.io
        copy = lambda: pltpu.make_async_copy(self.part(0), self.part(0), io.local.at[self.local]).wait()
        guarded(self.host, copy)
        for s in range(1, 4):
            io.arrived(self.slots[s], lambda s=s: self.part(s), self.host)

        def clear():
            self.dst[...] = jnp.zeros_like(self.dst)

        guarded(jnp.logical_not(self.host), clear)


N_FORE = 200
CHUNK = 128
COLS = 512


def stream(io, n, copies, body):
    base = io.locals(2 * len(copies(0, 0)))

    def make(i, slot):
        return [
            pltpu.make_async_copy(a, b, io.local.at[base + 2 * c + slot])
            for c, (a, b) in enumerate(copies(i, slot))
        ]

    for c in make(0, 0):
        c.start()

    def step(i, _):
        slot = i % 2

        @pl.when(i + 1 < n)
        def _():
            for c in make(i + 1, (i + 1) % 2):
                c.start()

        for c in make(i, slot):
            c.wait()
        body(i, slot)
        return 0

    lax.fori_loop(0, n, step, 0)


def lanes(i, width):
    return pl.ds(pl.multiple_of(i * width, LANES), width)


def meet(io):
    bar = pltpu.get_barrier_semaphore()
    partners = [(io.dp, io.z ^ k) for k in (1, 2, 3)] + [(io.dp ^ b, io.z) for b in (1, 2, 4)]
    for p in partners:
        pl.semaphore_signal(bar, inc=1, device_id=p, device_id_type=MESH)
    pl.semaphore_wait(bar, len(partners))


def spread_vectors(table, wide, vec, ub):
    wide[...] = table[...].astype(F32)
    spread_n = lax.broadcasted_iota(jnp.int32, (32, D), 0)
    spread_c = lax.broadcasted_iota(jnp.int32, (32, D), 1)
    mine = (spread_c // 32) == spread_n
    pick_l = lax.broadcasted_iota(jnp.int32, (LANES, D), 0)
    pick_c = lax.broadcasted_iota(jnp.int32, (LANES, D), 1)
    for k in range(2):
        rows = jnp.concatenate([wide[32 * n + k : 32 * n + k + 1] for n in range(32)], axis=0).astype(BF)
        for q in range(4):
            pick = jnp.where(pick_l == 32 * q + pick_c % 32, 1.0, 0.0).astype(BF)
            spread = jnp.where(mine, dot(rows, pick), 0.0)
            vec[4 * k + q : 4 * k + q + 1] = jnp.sum(spread, axis=0, keepdims=True)
    for n in range(32):
        ub[:, n * LANES : (n + 1) * LANES] = wide[32 * n + 2 : 32 * n + 3]


def forward_kernel(
    a, u, d, clips, cot,
    wa, wu, wd, og, x_out, middle_out, n1_out, n2_out, qkv_out, att_out, hidden, slope, vec, d_terms,
    xv, og2, n1, n2, qkv, att, middle, wb, hid, hid2, terms, slo, table, wide, ub, bias,
    send, recv, local,
):
    io = Copies(send, recv, local)
    ga, gu, gd = Gather(io, a, wa), Gather(io, u, wu), Gather(io, d, wd)
    t = xv.shape[0]
    own, sib = pl.ds(0, t), pl.ds(t, t)
    core = (io.dp ^ 1, io.z)
    cx, cc = Collect(io, clips, xv), Collect(io, cot, og2.at[own])
    meet(io)

    line = [(g, k) for g in (ga, gu, gd) for k in range(4)]
    place = [0]

    def advance(n=1):
        for _ in range(n):
            i = place[0]
            place[0] += 1
            if i < len(line):
                g, k = line[i]
                if k == 2 and g is not gd:
                    g.arrive_z(2)
                    (gu if g is ga else gd).start_z()
                    if g is ga:
                        cx.start()
                    else:
                        cc.start()
                elif k:
                    g.arrive_z(k)
                g.spread(k)
            if 1 <= i <= len(line):
                g, k = line[i - 1]
                g.pass_on(k)
            if 3 <= i <= len(line) + 2:
                g, k = line[i - 3]
                g.far(k)

    ga.start_z()
    advance(3)
    for g in (ga, gu, gd):
        g.local.wait()
    advance(4)
    outs = []

    ga.done()
    io.load(wa.at[:, pl.ds(4 * D, LANES)], table).wait()
    spread_vectors(table, wide, vec, ub)
    bias[:, 0:D] = vec[2:3]
    bias[:, D : 2 * D] = jnp.zeros((1, D), F32)
    bias[:, 2 * D : 3 * D] = vec[3:4]
    cx.wait()
    outs.append(io.load(xv, x_out))

    def first_norm(i, _):
        rows = pl.ds(pl.multiple_of(i * CHUNK, CHUNK), CHUNK)
        vhat, _r = norm_rows(xv[rows].astype(F32))
        n1[rows] = (vhat * vec[0:1] + vec[1:2]).astype(BF)
        return 0

    lax.fori_loop(0, t // CHUNK, first_norm, 0)
    outs.append(io.load(n1, n1_out))
    advance()

    def columns(ref, lo):
        return lambda i, slot: [(ref.at[:, pl.ds(pl.multiple_of(lo + i * COLS, LANES), COLS)], wb.at[slot])]

    def qkv_step(i, slot):
        qkv[:, lanes(i, COLS)] = (dot(n1[...], wb[slot]) + bias[:, lanes(i, COLS)]).astype(BF)

    stream(io, 3 * D // COLS, columns(wa, 0), qkv_step)
    outs.append(io.load(qkv, qkv_out))
    advance()

    def heads(i, _):
        def at(k):
            return lanes(k * (D // LANES) + i, LANES)

        att[:, at(0)] = attend_pair(qkv[:, at(0)], qkv[:, at(1)], qkv[:, at(2)])
        return 0

    n_pairs = D // LANES
    lax.fori_loop(0, n_pairs // 2, heads, 0)
    advance()
    lax.fori_loop(n_pairs // 2, n_pairs, heads, 0)
    outs.append(io.load(att, att_out))
    advance()

    def proj_step(i, slot):
        cols = lanes(i, COLS)
        middle[:, cols] = xv[:, cols].astype(F32) + (dot(att[...], wb[slot]) + vec[4:5, cols])

    stream(io, D // COLS, columns(wa, 3 * D), proj_step)
    outs.append(io.load(middle, middle_out))

    def second_norm(i, _):
        rows = pl.ds(pl.multiple_of(i * CHUNK, CHUNK), CHUNK)
        vhat, _r = norm_rows(middle[rows])
        n2[rows] = (vhat * vec[5:6] + vec[6:7]).astype(BF)
        return 0

    lax.fori_loop(0, t // CHUNK, second_norm, 0)
    outs.append(io.load(n2, n2_out))
    while place[0] < 7 + 4:
        advance()
    gu.done()

    out_base = io.locals(2)
    hid_slots = io.slots(4)

    def slope_out(i, slot):
        return pltpu.make_async_copy(slo.at[slot], slope.at[:, lanes(i, COLS)], io.local.at[out_base + slot])

    def hid_copy(i):
        j = (io.dp ^ i) // 2
        return io.remote(hid_slots[0] + j, hid.at[:, lanes(i, COLS)], hid2.at[sib, lanes(j, COLS)], core)

    def up_step(i, slot):
        @pl.when(i >= 2)
        def _():
            slope_out(i - 2, slot).wait()

        value, grad = gelu_both(dot(n2[...], wb[slot]) + ub[:, lanes(i, COLS)])
        hid[:, lanes(i, COLS)] = value.astype(BF)
        slo[slot] = grad.astype(BF)
        slope_out(i, slot).start()

        @pl.when((io.dp ^ i) % 2 == 1)
        def _():
            hid_copy(i).start()

        @pl.when((io.dp ^ i) % 2 == 0)
        def _():
            hid2[own, lanes((io.dp ^ i) // 2, COLS)] = value.astype(BF)

    n_up = FF // COLS
    stream(io, n_up // 2, columns(wu, 0), up_step)
    advance()
    stream(io, n_up // 2, columns(wu, FF // 2), lambda i, slot: up_step(i + n_up // 2, slot))
    outs.append(io.load(hid, hidden))
    advance()
    cc.wait()
    outs.append(io.load(og2.at[own], og))
    og_slot = io.slots(1)[0]
    io.start(og_slot, lambda: og2.at[own], lambda: og2.at[sib], core)
    for i in (n_up - 2, n_up - 1):
        slope_out(i, i % 2).wait()
    advance()
    io.arrived(og_slot, lambda: og2.at[sib])
    for j in range(4):
        hid_copy(io.dp ^ (2 * j + 1)).wait()

    def down_terms(j, _):
        terms[j] = dot_tn(hid2[:, lanes(j, COLS)], og2[...]).astype(BF)
        return 0

    lax.fori_loop(0, 2, down_terms, 0)
    advance()
    lax.fori_loop(2, 4, down_terms, 0)
    outs.append(io.load(terms, d_terms))
    while place[0] < len(line) + 3:
        advance()
    gd.done()
    for c in outs:
        c.wait()
    io.finish()


def forward(a, u, d, clips, cot):
    t = clips.shape[1] * 4
    any_ = pl.BlockSpec(memory_space=pl.ANY)
    vmem = pl.BlockSpec(memory_space=pltpu.VMEM)
    sh = jax.ShapeDtypeStruct
    v = pltpu.VMEM
    return pl.pallas_call(
        forward_kernel,
        out_shape=[
            sh((D, a.shape[1]), BF),
            sh((D, FF), BF),
            sh((FF, D), BF),
            sh((t, D), BF),
            sh((t, D), BF),
            sh((t, D), F32),
            sh((t, D), BF),
            sh((t, D), BF),
            sh((t, 3 * D), BF),
            sh((t, D), BF),
            sh((t, FF), BF),
            sh((t, FF), BF),
            sh((8, D), F32),
            sh((4, FF // 8, D), BF),
        ],
        in_specs=[any_] * 5,
        out_specs=[any_] * 12 + [vmem, any_],
        scratch_shapes=[
            v((t, D), BF),
            v((2 * t, D), BF),
            v((t, D), BF),
            v((t, D), BF),
            v((t, 3 * D), BF),
            v((t, D), BF),
            v((t, D), F32),
            v((2, D, COLS), BF),
            v((t, FF), BF),
            v((2 * t, FF // 2), BF),
            v((4, FF // 8, D), BF),
            v((2, t, COLS), BF),
            v((D, LANES), BF),
            v((D, LANES), F32),
            v((1, FF), F32),
            v((1, 3 * D), F32),
            pltpu.SemaphoreType.DMA((N_FORE,)),
            pltpu.SemaphoreType.DMA((N_FORE,)),
            pltpu.SemaphoreType.DMA((48,)),
        ],
        compiler_params=pltpu.CompilerParams(
            collective_id=0, has_side_effects=True, vmem_limit_bytes=56 * 2**20
        ),
    )(a, u, d, clips, cot)


class Reduce:
    def __init__(self, io, r, s, land, pieces, stage, out):
        self.io, self.r, self.s, self.land, self.pieces = io, r, s, land, pieces
        self.stage, self.out = stage, out
        self.slot = io.slots(6)
        self.z_slot = io.slots(4)

    def half(self, j, h):
        return self.s(j).at[pl.ds(h * 2 * self.r, 2 * self.r)]

    def send(self, i, j, h, bit):
        io = self.io
        io.start(self.slot[i], lambda: self.half(j, h), lambda: self.land.at[i], (io.dp ^ bit, io.z))

    def start(self):
        self.send(0, 3, 0, 2)
        self.send(1, 3, 1, 4)
        self.send(2, 1, 0, 2)
        self.send(3, 2, 1, 4)

    def load(self, i, at):
        self.io.arrived(self.slot[i], lambda: self.land.at[i])
        return self.io.load(self.land.at[i], self.stage.at[at])

    def relay(self):
        for i, j, h, bit in ((0, 2, 0, 4), (1, 1, 1, 2)):
            self.load(i, i).wait()
            ref = self.half(j, h)
            ref[...] = (ref[...].astype(F32) + self.stage[i].astype(F32)).astype(ref.dtype)
            self.send(5 - i, j, h, bit)

    def fold(self):
        io, r = self.io, self.r
        for i in (0, 1):
            io.sent_wait(self.slot[i])
        for h, (a, b) in enumerate(((2, 5), (4, 3))):
            one, two = self.load(a, 0), self.load(b, 1)
            one.wait()
            two.wait()
            own = self.half(0, h)[...]
            total = own.astype(F32) + self.stage[0].astype(F32) + self.stage[1].astype(F32)
            self.half(3, h)[...] = total.astype(own.dtype)
        for i, k in ((0, 3), (1, 1)):
            io.start(
                self.z_slot[i],
                lambda k=k: self.piece(io.z ^ k),
                lambda i=i: self.pieces.at[i],
                (io.dp, io.z ^ 1),
            )

    def piece(self, z):
        return self.s(3).at[pl.ds(pl.multiple_of(z * self.r, self.r), self.r)]

    def take(self, i):
        spot = self.stage.at[i // 2, pl.ds(i % 2 * self.r, self.r)]
        self.io.arrived(self.z_slot[i], lambda: self.pieces.at[i])
        return self.io.load(self.pieces.at[i], spot), spot

    def cross(self):
        io = self.io
        copy, spot = self.take(0)
        copy.wait()
        ref = self.piece(io.z ^ 2)
        ref[...] = (ref[...].astype(F32) + spot[...].astype(F32)).astype(ref.dtype)
        io.start(
            self.z_slot[2], lambda: self.piece(io.z ^ 2), lambda: self.pieces.at[2], (io.dp, io.z ^ 2)
        )

    def finish(self):
        one, two = self.take(1), self.take(2)
        total = self.piece(self.io.z)[...].astype(F32)
        for copy, spot in (one, two):
            copy.wait()
            total = total + spot[...].astype(F32)
        self.out[...] = total


class HandBack:
    def __init__(self, io, src, dst):
        self.io, self.src, self.dst = io, src, dst
        self.slots = io.slots(4)
        self.rows = dst.shape[1]

    def host(self, z):
        clip = z - self.io.dp % 2
        return (clip >= 0) & (clip < 3)

    def part(self, s):
        return self.src.at[pl.ds(s * self.rows, self.rows)]

    def start(self):
        io = self.io
        for s in range(1, 4):
            to = (io.z + 4 - s) % 4
            io.start(
                self.slots[s], lambda s=s: self.part(s), lambda s=s: self.dst.at[s], (io.dp, to), self.host(io.z)
            )
        copy = io.load(self.part(0), self.dst.at[0])
        copy.wait()

    def wait(self):
        io = self.io
        for s in range(1, 4):
            io.arrived(self.slots[s], lambda s=s: self.dst.at[s], self.host((io.z + s) % 4))


N_BACK = 140
N_LOCAL = 150


def backward_kernel(
    wa, wu, wd, og_in, x, middle, normed1, normed2, qkv_in, attended, hidden, slope, params, d_terms,
    qkv_out, p_out, u_out, d_out, s_out, ret_out, ret_in,
    a_land, u_land, d_land, s_land, a_pieces, u_pieces, d_pieces, s_pieces,
    og, ug2, bg2, jn2, np2, n1p2, atp2, flip, qkv, ag, ob, xv, part, wdb, wb, tiles, hid, acc, s_d, s_u,
    stage_d, stage_u, stage_a, table, table_sib, s_s, stage_s, vec, ub,
    send, recv, local,
):
    io = Copies(send, recv, local)
    dp, z = io.dp, io.z
    t = og.shape[0]
    own, sib = pl.ds(0, t), pl.ds(t, t)
    core = (dp ^ 1, z)

    red_d = Reduce(io, d_out.shape[0], lambda j: s_d.at[j], d_land, d_pieces, stage_d, d_out)
    red_u = Reduce(io, u_out.shape[0], lambda j: s_u.at[j], u_land, u_pieces, stage_u, u_out)
    n_a = p_out.shape[0]

    def part_of_a(c):
        blocks = lambda j: ug2.at[pl.ds(j * 4 * n_a, 4 * n_a), pl.ds(c * D, D)]
        out = p_out if c == 3 else qkv_out.at[:, pl.ds(c * D, D)]
        return Reduce(io, n_a, blocks, a_land.at[c], a_pieces.at[c], stage_a, out)

    red_q, red_k, red_v, red_p = (part_of_a(c) for c in range(4))
    red_s = Reduce(io, s_out.shape[0], lambda j: s_s.at[j], s_land, s_pieces, stage_s, s_out)
    back_in = HandBack(io, qkv.at[:, pl.ds(D, D)], ret_in)
    back_out = HandBack(io, ob, ret_out)

    def planes(src, dst):
        width = dst.shape[1] // 4
        return [
            io.load(
                src.at[:, pl.ds(pl.multiple_of((dp ^ (2 * j)) * width, LANES), width)],
                dst.at[own, pl.ds(j * width, width)],
            )
            for j in range(4)
        ]

    load_d = io.load(d_terms, s_d)
    load_og = io.load(og_in, og)
    load_x = [io.load(x, xv), io.load(middle, part)]
    meet(io)
    load_d.wait()
    red_d.start()

    def swap_planes(src, dst):
        width = dst.shape[1] // 4
        slots = io.slots(4)
        for j in range(4):
            io.start(
                slots[j],
                lambda j=j: src.at[:, pl.ds(pl.multiple_of((dp ^ (2 * j + 1)) * width, LANES), width)],
                lambda j=j: dst.at[sib, pl.ds(j * width, width)],
                core,
            )
        return [(slots[j], lambda j=j: dst.at[sib, pl.ds(j * width, width)]) for j in range(4)]

    swapped_2 = swap_planes(normed2, np2)
    d_rows = wdb.shape[1]
    w_rows = wb.shape[1]
    load_og.wait()

    acc[...] = jnp.zeros_like(acc)
    ug_slots = io.slots(FF // d_rows)

    def ug_copy(i):
        return io.remote(ug_slots[0] + i, ug2.at[own, lanes(i, d_rows)], ug2.at[sib, lanes(i, d_rows)], core)

    def hidden_step(i, slot):
        grad = dot_nt(og[...], wdb[slot]) * tiles[slot].astype(F32)
        low = grad.astype(BF)
        ug2[own, lanes(i, d_rows)] = low
        ub[:, lanes(i, d_rows)] = jnp.sum(low.astype(F32), axis=0, keepdims=True)
        ug_copy(i).start()
        acc[...] += dot(hid[slot], wdb[slot])

    stream(
        io,
        FF // d_rows,
        lambda i, slot: [
            (wd.at[pl.ds(pl.multiple_of(i * d_rows, d_rows), d_rows)], wdb.at[slot]),
            (slope.at[:, lanes(i, d_rows)], tiles.at[slot]),
            (hidden.at[:, lanes(i, d_rows)], hid.at[slot]),
        ],
        hidden_step,
    )
    for c in load_x:
        c.wait()
    ob[...] = (acc[...] + (part[...] - xv[...].astype(F32)) + params[7:8]).astype(BF)
    back_out.start()
    second = planes(normed2, np2)
    third = planes(normed1, n1p2) + planes(attended, atp2)
    third += [io.load(qkv_in, qkv)]
    swapped_1 = swap_planes(normed1, n1p2)
    swapped_3 = swap_planes(attended, atp2)

    for c in second:
        c.wait()
    for slot, ref in swapped_2:
        io.arrived(slot, ref)
    flip[...] = np2[...].T
    for i in range(FF // d_rows):
        ug_copy(i).wait_recv()

    def up_step(i, _):
        block = dot(flip[...], ug2[:, lanes(i, COLS)]).astype(BF)
        for j in range(4):
            s_u[j, :, lanes(i, COLS)] = block[j * LANES : (j + 1) * LANES]
        return 0

    lax.fori_loop(0, FF // COLS, up_step, 0)
    red_d.relay()
    red_u.start()

    def up_back(i, slot):
        acc[:, lanes(i, w_rows)] = dot_nt(ug2[own], wb[slot, :, 0:FF])

    w_tile = lambda ref, lo, n: lambda i, slot: [
        (ref.at[pl.ds(pl.multiple_of(i * w_rows, w_rows), w_rows), pl.ds(lo, n)], wb.at[slot, :, pl.ds(0, n)])
    ]
    stream(io, D // w_rows, w_tile(wu, 0, FF), up_back)
    for c in third:
        c.wait()
    vec[...] = jnp.zeros_like(vec)

    def second_norm(i, _):
        rows = pl.ds(pl.multiple_of(i * CHUNK, CHUNK), CHUNK)
        e = acc[rows]
        vhat, r = norm_rows(part[rows])
        g = e * params[5:6]
        grad = r * (
            g - jnp.mean(g, axis=-1, keepdims=True) - vhat * jnp.mean(g * vhat, axis=-1, keepdims=True)
        )
        vec[5:6] += jnp.sum(e * vhat, axis=0, keepdims=True)
        vec[6:7] += jnp.sum(e, axis=0, keepdims=True)
        part[rows] = grad
        out_grad = og[rows].astype(F32)
        low = (out_grad + grad).astype(BF)
        bg2[rows] = low
        vec[4:5] += jnp.sum(low.astype(F32), axis=0, keepdims=True)
        vec[7:8] += jnp.sum(out_grad, axis=0, keepdims=True)
        return 0

    lax.fori_loop(0, t // CHUNK, second_norm, 0)
    bg_slot = io.slots(1)[0]
    io.start(bg_slot, lambda: bg2.at[own], lambda: bg2.at[sib], core)

    def proj_back(i, slot):
        ag[:, lanes(i, w_rows)] = dot_nt(bg2[own], wb[slot, :, 0:D]).astype(BF)

    stream(io, D // w_rows, w_tile(wa, 3 * D, D), proj_back)
    for slot in range(FF // d_rows):
        ug_copy(slot).wait_send()
    for slot, ref in swapped_3:
        io.arrived(slot, ref)
    flip[...] = atp2[...].T
    io.arrived(bg_slot, lambda: bg2.at[sib])

    def proj_step(i, _):
        ug2[own, lanes(6 + i, COLS)] = dot(flip[...], bg2[:, lanes(i, COLS)]).astype(BF)
        return 0

    lax.fori_loop(0, D // COLS, proj_step, 0)
    red_p.start()

    def heads(i, _):
        def at(k):
            return lanes(k * (D // LANES) + i, LANES)

        dq, dk, dv = attend_back_pair(qkv[:, at(0)], qkv[:, at(1)], qkv[:, at(2)], ag[:, at(0)])
        for k, grad in enumerate((dq, dk, dv)):
            jn2[own, at(k)] = grad
        vec[2:3, at(0)] = jnp.sum(dq.astype(F32), axis=0, keepdims=True)
        vec[3:4, at(0)] = jnp.sum(dv.astype(F32), axis=0, keepdims=True)
        return 0

    n_pairs = D // LANES
    lax.fori_loop(0, n_pairs // 2, heads, 0)
    red_d.fold()
    lax.fori_loop(n_pairs // 2, n_pairs, heads, 0)
    jn_slot = io.slots(1)[0]
    io.start(jn_slot, lambda: jn2.at[own], lambda: jn2.at[sib], core)
    red_u.relay()
    red_d.cross()

    for slot, ref in swapped_1:
        io.arrived(slot, ref)
    flip[...] = n1p2[...].T

    def first_back(i, slot):
        acc[:, lanes(i, w_rows)] = dot_nt(jn2[own], wb[slot, :, 0 : 3 * D])

    stream(io, D // w_rows, w_tile(wa, 0, 3 * D), first_back)
    io.arrived(jn_slot, lambda: jn2.at[sib])

    def qkv_step(i, _):
        ug2[own, lanes(i, COLS)] = dot(flip[...], jn2[:, lanes(i, COLS)]).astype(BF)
        return 0

    for c, red in enumerate((red_q, red_k, red_v)):
        lax.fori_loop(c * D // COLS, (c + 1) * D // COLS, qkv_step, 0)
        red.start()
    red_p.relay()
    red_d.finish()

    def first_norm(i, _):
        rows = pl.ds(pl.multiple_of(i * CHUNK, CHUNK), CHUNK)
        e = acc[rows]
        vhat, r = norm_rows(xv[rows].astype(F32))
        g = e * params[0:1]
        grad = r * (
            g - jnp.mean(g, axis=-1, keepdims=True) - vhat * jnp.mean(g * vhat, axis=-1, keepdims=True)
        )
        vec[0:1] += jnp.sum(e * vhat, axis=0, keepdims=True)
        vec[1:2] += jnp.sum(e, axis=0, keepdims=True)
        qkv[rows, D : 2 * D] = (part[rows] + grad).astype(BF)
        return 0

    lax.fori_loop(0, t // CHUNK, first_norm, 0)
    back_in.start()

    spread_n = lax.broadcasted_iota(jnp.int32, (32, D), 0)
    spread_c = lax.broadcasted_iota(jnp.int32, (32, D), 1)
    mine = (spread_c // 32) == spread_n
    pick_c = lax.broadcasted_iota(jnp.int32, (D, LANES), 0)
    pick_l = lax.broadcasted_iota(jnp.int32, (D, LANES), 1)
    table[...] = jnp.zeros_like(table)
    for k in range(2):
        rows = jnp.zeros((32, LANES), F32)
        for q in range(4):
            spread = jnp.where(mine, vec[4 * k + q : 4 * k + q + 1], 0.0)
            pick = jnp.where(pick_l == 32 * q + pick_c % 32, 1.0, 0.0)
            rows = rows + jnp.dot(spread, pick, preferred_element_type=F32, precision=lax.Precision.HIGHEST)
        for n in range(32):
            table[8 * n + k : 8 * n + k + 1] = rows[n : n + 1]
    for n in range(32):
        table[8 * n + 2 : 8 * n + 3] = ub[:, n * LANES : (n + 1) * LANES]
    table_slot = io.slots(1)[0]
    io.start(table_slot, lambda: table, lambda: table_sib, core)

    io.arrived(table_slot, lambda: table_sib)
    for j in range(4):
        rows = pl.ds(pl.multiple_of((dp ^ (2 * j)) * 32, 32), 32)
        s_s[j] = table[rows] + table_sib[rows]
    red_s.start()

    red_u.fold()
    red_q.relay()
    red_k.relay()
    red_v.relay()
    red_s.relay()
    red_u.cross()
    red_p.fold()
    red_q.fold()
    red_k.fold()
    red_p.cross()
    red_v.fold()
    red_q.cross()
    red_k.cross()
    red_s.fold()
    red_v.cross()
    red_s.cross()
    for red in (red_u, red_p, red_q, red_k):
        red.finish()
    back_in.wait()
    back_out.wait()
    red_v.finish()
    red_s.finish()
    io.finish()


def backward(*saved):
    t = saved[3].shape[0]
    any_ = pl.BlockSpec(memory_space=pl.ANY)
    vmem = pl.BlockSpec(memory_space=pltpu.VMEM)
    sh = jax.ShapeDtypeStruct
    ra, rd, rs = D // 32, FF // 32, 8
    outs = [
        (sh((ra, 3 * D), F32), vmem),
        (sh((ra, D), F32), vmem),
        (sh((ra, FF), F32), vmem),
        (sh((rd, D), F32), vmem),
        (sh((rs, LANES), F32), vmem),
        (sh((4, t // 4, D), BF), any_),
        (sh((4, t // 4, D), BF), any_),
    ]
    for count, k in ((6, 2), (3, 1)):
        outs += [
            (sh((4, count, k * ra, D), BF), any_),
            (sh((count, k * ra, FF), BF), any_),
            (sh((count, k * rd, D), BF), any_),
            (sh((count, k * rs, LANES), F32), any_),
        ]
    v = pltpu.VMEM
    results = pl.pallas_call(
        backward_kernel,
        out_shape=[o for o, _ in outs],
        in_specs=[any_] * 12 + [vmem, any_],
        out_specs=[o for _, o in outs],
        scratch_shapes=[
            v((t, D), BF),
            v((2 * t, FF), BF),
            v((2 * t, D), BF),
            v((2 * t, 3 * D), BF),
            v((2 * t, D // 2), BF),
            v((2 * t, D // 2), BF),
            v((2 * t, D // 2), BF),
            v((D // 2, 2 * t), BF),
            v((t, 3 * D), BF),
            v((t, D), BF),
            v((t, D), BF),
            v((t, D), BF),
            v((t, D), F32),
            v((2, 512, D), BF),
            v((2, 256, FF), BF),
            v((2, t, 512), BF),
            v((2, t, 512), BF),
            v((t, D), F32),
            v((4, 4 * rd, D), BF),
            v((4, 4 * ra, FF), BF),
            v((2, 2 * rd, D), BF),
            v((2, 2 * ra, FF), BF),
            v((2, 2 * ra, D), BF),
            v((32 * rs, LANES), F32),
            v((32 * rs, LANES), F32),
            v((4, 4 * rs, LANES), F32),
            v((2, 2 * rs, LANES), F32),
            v((8, D), F32),
            v((1, FF), F32),
            pltpu.SemaphoreType.DMA((N_BACK,)),
            pltpu.SemaphoreType.DMA((N_BACK,)),
            pltpu.SemaphoreType.DMA((N_LOCAL,)),
        ],
        compiler_params=pltpu.CompilerParams(
            collective_id=1, has_side_effects=True, vmem_limit_bytes=60 * 2**20
        ),
    )(*saved)
    return results[:7]


def norm_parts(v):
    center = v - jnp.mean(v, axis=-1, keepdims=True)
    r = lax.rsqrt(jnp.mean(center * center, axis=-1, keepdims=True) + EPSILON)
    return center * r, r


def norm_back(vhat, r, gain, e):
    t = e * gain
    grad = r * (
        t - jnp.mean(t, axis=-1, keepdims=True) - vhat * jnp.mean(t * vhat, axis=-1, keepdims=True)
    )
    return grad, jnp.sum(e * vhat, axis=0), jnp.sum(e, axis=0)


SMALL = (D, D, D, D, D, D, D, D, FF)


def per_device(
    n_dp,
    n_seq,
    clips,
    counts,
    out_cotangent,
    norm1_gain,
    norm1_shift,
    qkv_weight,
    query_bias,
    value_bias,
    proj_weight,
    proj_bias,
    norm2_gain,
    norm2_shift,
    up_weight,
    up_bias,
    down_weight,
    down_bias,
):
    links = Links(n_dp, n_seq)
    n = n_dp * n_seq
    slots = clips.shape[0]
    rows = D // n
    small = (
        norm1_gain,
        norm1_shift,
        query_bias,
        value_bias,
        proj_bias,
        norm2_gain,
        norm2_shift,
        down_bias,
        up_bias,
    )
    packed = jnp.concatenate(small)
    packed = jnp.pad(packed, (0, rows * LANES - packed.shape[0])).reshape(rows, LANES)
    shard_a = jnp.concatenate(
        [qkv_weight.reshape(rows, 3 * D), proj_weight.reshape(rows, D), packed], axis=1
    ).astype(BF)
    shard_u = up_weight.reshape(rows, FF).astype(BF)
    shard_d = down_weight.reshape(FF // n, D).astype(BF)

    living = (jnp.arange(slots) < counts[0]).astype(F32)[:, None, None]
    living_cot = living * out_cotangent
    tokens = (clips.astype(BF), living_cot.astype(BF))
    if links.short:
        saved = forward(shard_a, shard_u, shard_d, *tokens)
        qkv_grad, proj_grad, up_grad, down_grad, small_grad, out_back, in_back = backward(*saved)
        out_home, in_home = links.by_clip(out_back, slots), links.by_clip(in_back, slots)
        small_out = small_grad[:3].reshape(-1)
    else:
        a_mat, u_mat, d_mat = (links.gather(shard) for shard in (shard_a, shard_u, shard_d))
        x, out_grad = (links.collect(t) for t in tokens)
        x = x.astype(F32)

        table = a_mat[:, 4 * D :].reshape(n_dp, n_seq, rows * LANES)
        table = table.reshape(n, rows * LANES).astype(F32)
        vectors, at = [], 0
        for size in SMALL:
            vectors.append(table[:, at : at + size // n].reshape(size))
            at += size // n
        gain1, shift1, q_bias, v_bias, p_bias, gain2, shift2, d_bias, u_bias = vectors

        vhat1, r1 = norm_parts(x)
        normed1 = (vhat1 * gain1 + shift1).astype(BF)
        qkv_bias = jnp.concatenate([q_bias, jnp.zeros_like(q_bias), v_bias])
        qkv_mat, proj_mat = a_mat[:, : 3 * D], a_mat[:, 3 * D : 4 * D]
        qkv = (dot(normed1, qkv_mat) + qkv_bias).astype(BF)
        attended = attend(qkv)
        branch = dot(attended, proj_mat) + p_bias
        middle = x + branch
        vhat2, r2 = norm_parts(middle)
        normed2 = (vhat2 * gain2 + shift2).astype(BF)
        hidden, slope = gelu_both(dot(normed2, u_mat) + u_bias)
        hidden = hidden.astype(BF)
        slope = slope.astype(BF)
        out_part = branch + dot(hidden, d_mat) + d_bias
        out_home = links.hand_back(out_part.astype(BF), slots)
        down_grad = links.reduce(dot_tn(hidden, out_grad))
        upper_grad = (dot_nt(out_grad, d_mat) * slope).astype(BF)
        up_grad = links.reduce(dot_tn(normed2, upper_grad))
        part, gain2_grad, shift2_grad = norm_back(vhat2, r2, gain2, dot_nt(upper_grad, u_mat))
        branch_grad = (out_grad.astype(F32) + part).astype(BF)
        dq, dk, dv = attend_back(qkv, dot_nt(branch_grad, proj_mat).astype(BF))
        joined = jnp.concatenate([dq, dk, dv], axis=1)
        first_part, gain1_grad, shift1_grad = norm_back(vhat1, r1, gain1, dot_nt(joined, qkv_mat))
        in_home = links.hand_back((part + first_part).astype(BF), slots)
        total = lambda g: jnp.sum(g.astype(F32), axis=0)
        small_grads = (
            gain1_grad,
            shift1_grad,
            total(dq),
            total(dv),
            total(branch_grad),
            gain2_grad,
            shift2_grad,
            total(out_grad),
            total(upper_grad),
        )
        grad_table = jnp.concatenate([g.reshape(n, -1) for g in small_grads], axis=1)
        width = grad_table.shape[1]
        grad_table = jnp.pad(grad_table, ((0, 0), (0, rows * LANES - width)))
        d_a = [dot_tn(normed1, joined), dot_tn(attended, branch_grad), grad_table.reshape(n * rows, LANES)]
        a_grad = links.reduce(jnp.concatenate(d_a, axis=1))
        qkv_grad, proj_grad = a_grad[:, : 3 * D], a_grad[:, 3 * D : 4 * D]
        small_out = a_grad[:, 4 * D :].reshape(-1)
    block_out = living * (clips + out_home.astype(F32))
    input_grad = living_cot + in_home.astype(F32)
    pieces, at = [], 0
    for size in SMALL:
        pieces.append(small_out[at : at + size // n])
        at += size // n
    g1, s1, qb, vb, pb, g2, s2, db, ub = pieces
    return (
        block_out,
        input_grad,
        g1,
        s1,
        qkv_grad.reshape(-1),
        qb,
        vb,
        proj_grad.reshape(-1),
        pb,
        g2,
        s2,
        up_grad.reshape(-1),
        ub,
        down_grad.reshape(-1),
        db,
    )


def solution(mesh):
    flat = P(AXES)
    tokens = P("dp", "seq", None)
    return jax.shard_map(
        functools.partial(per_device, mesh.shape["dp"], mesh.shape["seq"]),
        mesh=mesh,
        in_specs=(tokens, P("dp"), tokens) + (flat,) * 13,
        out_specs=(tokens, tokens) + (flat,) * 13,
        check_vma=False,
    )
```

```python
import functools

import jax
import jax.numpy as jnp
from jax import lax
from jax.experimental import pallas as pl
from jax.experimental.pallas import tpu as pltpu
from jax.sharding import PartitionSpec as P

D = 1024
FF = 4096
HEADS = 16
HEAD_DIM = 64
EPSILON = 1e-05
LANES = 128
BF = jnp.bfloat16
F32 = jnp.float32
AXES = ("dp", "seq")
MESH = pl.DeviceIdType.MESH


def dot(a, b):
    return jnp.dot(a, b, preferred_element_type=F32)


def dot_nt(a, b):
    return lax.dot_general(a, b, (((1,), (1,)), ((), ())), preferred_element_type=F32)


def dot_tn(a, b):
    return lax.dot_general(a, b, (((0,), (0,)), ((), ())), preferred_element_type=F32)


def soft_t(q2, k_half):
    scores = dot_nt(k_half, q2) * (HEAD_DIM**-0.5)
    top = jnp.max(scores, axis=0, keepdims=True)
    e = jnp.exp(scores - top)
    return e * (1.0 / jnp.sum(e, axis=0, keepdims=True))


def attend_pair(q2, k2, v2):
    low = lax.broadcasted_iota(jnp.int32, k2.shape, 1) < HEAD_DIM
    v_t = v2.T
    zero = jnp.zeros_like(k2)
    parts = []
    for h in range(2):
        k_half = jnp.where(low == (h == 0), k2, zero)
        p_t = soft_t(q2, k_half).astype(BF)
        parts.append(dot(v_t[h * HEAD_DIM : (h + 1) * HEAD_DIM], p_t))
    return jnp.concatenate(parts, axis=0).T.astype(BF)


def attend_kernel(q_ref, k_ref, v_ref, o_ref):
    o_ref[...] = attend_pair(q_ref[...], k_ref[...], v_ref[...])


def attend(qkv):
    t = qkv.shape[0]
    n = D // LANES
    spec = lambda off: pl.BlockSpec((t, LANES), lambda h: (0, off + h))
    return pl.pallas_call(
        attend_kernel,
        grid=(n,),
        out_shape=jax.ShapeDtypeStruct((t, D), BF),
        in_specs=[spec(0), spec(n), spec(2 * n)],
        out_specs=spec(0),
        compiler_params=pltpu.CompilerParams(vmem_limit_bytes=48 * 2**20),
        cost_estimate=pl.CostEstimate(
            flops=16 * 4 * t * t * HEAD_DIM, bytes_accessed=8 * t * D, transcendentals=16 * t * t
        ),
    )(qkv, qkv, qkv)


def attend_back_pair(q2, k2, v2, do2):
    low = lax.broadcasted_iota(jnp.int32, k2.shape, 1) < HEAD_DIM
    k_t = k2.T
    zero = jnp.zeros_like(k2)
    dq, dk, dv = [], [], []
    for h in range(2):
        mine = low == (h == 0)
        p = soft_t(q2, jnp.where(mine, k2, zero))
        dp = dot_nt(jnp.where(mine, v2, zero), do2)
        total = jnp.sum(p * dp, axis=0, keepdims=True)
        ds = (p * (dp - total)).astype(BF)
        dv.append(dot(p.astype(BF), do2))
        dk.append(dot(ds, q2))
        dq.append(dot(k_t[h * HEAD_DIM : (h + 1) * HEAD_DIM], ds))
    scale = HEAD_DIM**-0.5
    return (
        (jnp.concatenate(dq, axis=0).T * scale).astype(BF),
        (jnp.where(low, dk[0], dk[1]) * scale).astype(BF),
        jnp.where(low, dv[0], dv[1]).astype(BF),
    )


def attend_back_kernel(q_ref, k_ref, v_ref, do_ref, dq_ref, dk_ref, dv_ref):
    grads = attend_back_pair(q_ref[...], k_ref[...], v_ref[...], do_ref[...])
    dq_ref[...], dk_ref[...], dv_ref[...] = grads


def attend_back(qkv, do):
    t = qkv.shape[0]
    n = D // LANES
    spec = lambda off: pl.BlockSpec((t, LANES), lambda h: (0, off + h))
    return pl.pallas_call(
        attend_back_kernel,
        grid=(n,),
        out_shape=[jax.ShapeDtypeStruct((t, D), BF)] * 3,
        in_specs=[spec(0), spec(n), spec(2 * n), spec(0)],
        out_specs=[spec(0)] * 3,
        compiler_params=pltpu.CompilerParams(vmem_limit_bytes=48 * 2**20),
        cost_estimate=pl.CostEstimate(
            flops=16 * 10 * t * t * HEAD_DIM, bytes_accessed=14 * t * D, transcendentals=16 * t * t
        ),
    )(qkv, qkv, qkv, do)


class Links:
    def __init__(self, n_dp, n_seq):
        self.n_dp, self.n_seq = n_dp, n_seq
        self.short = n_dp == 8 and n_seq == 4
        self.dp = lax.axis_index("dp")
        self.z = lax.axis_index("seq")

    def gather(self, shard):
        return lax.all_gather(shard, AXES, axis=0, tiled=True)

    def reduce(self, grad):
        return lax.psum_scatter(grad.astype(BF), AXES, scatter_dimension=0, tiled=True).astype(F32)


    def lead(self, d, slots):
        return d % 2 if self.n_seq > slots else 0

    def shift_pairs(self, s, slots):
        n = self.n_seq
        pairs = []
        for d in range(self.n_dp):
            for z in range(n):
                to = (z + s) % n
                if 0 <= to - self.lead(d, slots) < slots:
                    pairs.append((d * n + z, d * n + to))
        return pairs

    def my_clip(self, slots):
        lead = self.dp % 2 if self.n_seq > slots else 0
        return self.z - lead

    def collect(self, x):
        slots, n = x.shape[0], self.n_seq
        clip = self.my_clip(slots)
        parts = []
        for s in range(n):
            lead = self.z - clip
            index = jnp.clip((self.z + s) % n - lead, 0, slots - 1)
            part = lax.dynamic_index_in_dim(x, index, 0, False)
            parts.append(part if s == 0 else lax.ppermute(part, AXES, self.shift_pairs(s, slots)))
        host = (clip >= 0) & (clip < slots)
        return jnp.where(host, jnp.concatenate(parts), jnp.zeros((), x.dtype))

    def hand_back(self, y, slots):
        n = self.n_seq
        rows = y.shape[0] // n
        back = []
        for s in range(n):
            part = y[s * rows : (s + 1) * rows]
            pairs = [(b, a) for a, b in self.shift_pairs(s, slots)]
            back.append(part if s == 0 else lax.ppermute(part, AXES, pairs))
        return self.by_clip(jnp.stack(back), slots)

    def by_clip(self, back, slots):
        n = self.n_seq
        lead = self.z - self.my_clip(slots)
        return jnp.stack(
            [lax.dynamic_index_in_dim(back, (c + lead - self.z) % n, 0, False) for c in range(slots)]
        )


def norm_rows(v):
    center = v - jnp.mean(v, axis=-1, keepdims=True)
    r = lax.rsqrt(jnp.mean(center * center, axis=-1, keepdims=True) + EPSILON)
    return center * r, r


def gelu_both(u):
    cdf = 0.5 * (1.0 + lax.erf(u * 0.7071067811865476))
    pdf = 0.3989422804014327 * jnp.exp(-0.5 * u * u)
    return u * cdf, cdf + u * pdf


def guarded(cond, f):
    if cond is None: f()
    else: pl.when(cond)(f)

class Copies:
    def __init__(self, send, recv, local=None):
        self.send, self.recv, self.n, self.sent = send, recv, 0, []
        self.local, self.n_local = local, 0
        self.dp, self.z = lax.axis_index("dp"), lax.axis_index("seq")
    def slots(self, k):
        self.n += k
        return list(range(self.n - k, self.n))
    def remote(self, slot, src, dst, dev):
        return pltpu.make_async_remote_copy(src_ref=src, dst_ref=dst, send_sem=self.send.at[slot], recv_sem=self.recv.at[slot], device_id=dev, device_id_type=MESH)
    def start(self, slot, src, dst, dev, cond=None):
        guarded(cond, lambda: self.remote(slot, src(), dst(), dev).start())
        self.sent.append((slot, src, dst, dev, cond))
    def arrived(self, slot, dst, cond=None):
        guarded(cond, lambda: self.remote(slot, dst(), dst(), (self.dp ^ 1, self.z)).wait_recv())
    def sent_wait(self, which=None):
        rest = []
        for slot, src, dst, dev, cond in self.sent:
            if which is None or slot == which:
                guarded(cond, lambda: self.remote(slot, src(), dst(), dev).wait_send())
            else:
                rest.append((slot, src, dst, dev, cond))
        self.sent = rest
    def finish(self):
        self.sent_wait()
    def locals(self, k):
        self.n_local += k
        return self.n_local - k
    def load(self, src, dst):
        copy = pltpu.make_async_copy(src, dst, self.local.at[self.locals(1)])
        copy.start()
        return copy


class Gather:
    def __init__(self, io, shard, out):
        self.io, self.shard, self.out = io, shard, out
        self.r = shard.shape[0]
        self.local = io.load(shard, self.at(0, 0))
        self.keys = (0, 1, 2, 3)
        self.z_slot = io.slots(4)
        self.slot = {k: {name: io.slots(2) for name in ("x", "y", "d", "own", "cx", "cy", "cd")} for k in self.keys}

    def at(self, m, k, part=None):
        io, r = self.io, self.r
        base, n = ((io.dp ^ m) * 4 + (io.z ^ k)) * r, r
        if part is not None:
            n = n // 2
            base = base + part * n
        return self.out.at[pl.ds(pl.multiple_of(base, 16), n)]

    def move(self, name, i, m, k, bit, part=None, src=None):
        io = self.io
        ref = lambda: self.at(m, k, part)
        io.start(self.slot[k][name][i], src or ref, ref, (io.dp ^ bit, io.z))

    def got(self, name, i, m, k, part=None):
        self.io.arrived(self.slot[k][name][i], lambda: self.at(m, k, part))

    def start_z(self):
        io = self.io
        for k in (1, 2):
            io.start(self.z_slot[k], lambda: self.shard, lambda: self.at(0, 0), (io.dp, io.z ^ k))

    def arrive_z(self, k):
        io = self.io
        ref = lambda: self.at(0, k)
        io.arrived(self.z_slot[k], ref)
        if k == 2:
            io.start(self.z_slot[3], ref, ref, (io.dp, io.z ^ 1))

    def spread(self, k):
        src = (lambda: self.shard) if k == 0 else None
        self.move("x", 0, 0, k, 2, src=src)
        self.move("y", 0, 0, k, 4, src=src)
        self.move("own", 0, 0, k, 1, src=src)

    def pass_on(self, k):
        self.got("x", 0, 2, k)
        self.move("d", 0, 2, k, 4, 0)
        self.got("y", 0, 4, k)
        self.move("d", 1, 4, k, 2, 1)
        self.move("cx", 0, 2, k, 1)
        self.move("cy", 0, 4, k, 1)

    def far(self, k):
        for h in range(2):
            self.got("d", h, 6, k, h)
            self.move("cd", h, 6, k, 1, h)

    def done(self):
        for k in self.keys:
            self.got("own", 0, 1, k)
            self.got("cx", 0, 3, k)
            self.got("cy", 0, 5, k)
            for h in range(2):
                self.got("cd", h, 7, k, h)


class Collect:
    def __init__(self, io, src, dst):
        self.io, self.src, self.dst = io, src, dst
        self.slots = io.slots(4)
        self.local = io.locals(1)
        self.rows = src.shape[1]
        self.host = self.valid(io.z)

    def part(self, s):
        return self.dst.at[pl.ds(s * self.rows, self.rows)]

    def valid(self, z):
        clip = z - self.io.dp % 2
        return (clip >= 0) & (clip < 3)

    def start(self):
        io = self.io
        for s in range(4):
            to = (io.z + s) % 4
            src = lambda to=to: self.src.at[jnp.clip(to - io.dp % 2, 0, 2)]
            if s == 0:
                copy = lambda: pltpu.make_async_copy(src(), self.part(0), io.local.at[self.local]).start()
                guarded(self.host, copy)
            else:
                io.start(self.slots[s], src, lambda s=s: self.part(s), (io.dp, to), self.valid(to))

    def wait(self):
        io = self.io
        copy = lambda: pltpu.make_async_copy(self.part(0), self.part(0), io.local.at[self.local]).wait()
        guarded(self.host, copy)
        for s in range(1, 4):
            io.arrived(self.slots[s], lambda s=s: self.part(s), self.host)

        def clear():
            self.dst[...] = jnp.zeros_like(self.dst)

        guarded(jnp.logical_not(self.host), clear)


N_FORE = 200
CHUNK = 128
COLS = 512


def stream(io, n, copies, body):
    base = io.locals(2 * len(copies(0, 0)))

    def make(i, slot):
        return [
            pltpu.make_async_copy(a, b, io.local.at[base + 2 * c + slot])
            for c, (a, b) in enumerate(copies(i, slot))
        ]

    for c in make(0, 0):
        c.start()

    def step(i, _):
        slot = i % 2

        @pl.when(i + 1 < n)
        def _():
            for c in make(i + 1, (i + 1) % 2):
                c.start()

        for c in make(i, slot):
            c.wait()
        body(i, slot)
        return 0

    lax.fori_loop(0, n, step, 0)


def lanes(i, width):
    return pl.ds(pl.multiple_of(i * width, LANES), width)


def meet(io):
    bar = pltpu.get_barrier_semaphore()
    partners = [(io.dp, io.z ^ k) for k in (1, 2, 3)] + [(io.dp ^ b, io.z) for b in (1, 2, 4)]
    for p in partners:
        pl.semaphore_signal(bar, inc=1, device_id=p, device_id_type=MESH)
    pl.semaphore_wait(bar, len(partners))


def spread_vectors(table, wide, vec, ub):
    wide[...] = table[...].astype(F32)
    spread_n = lax.broadcasted_iota(jnp.int32, (32, D), 0)
    spread_c = lax.broadcasted_iota(jnp.int32, (32, D), 1)
    mine = (spread_c // 32) == spread_n
    pick_l = lax.broadcasted_iota(jnp.int32, (LANES, D), 0)
    pick_c = lax.broadcasted_iota(jnp.int32, (LANES, D), 1)
    for k in range(2):
        rows = jnp.concatenate([wide[32 * n + k : 32 * n + k + 1] for n in range(32)], axis=0).astype(BF)
        for q in range(4):
            pick = jnp.where(pick_l == 32 * q + pick_c % 32, 1.0, 0.0).astype(BF)
            spread = jnp.where(mine, dot(rows, pick), 0.0)
            vec[4 * k + q : 4 * k + q + 1] = jnp.sum(spread, axis=0, keepdims=True)
    for n in range(32):
        ub[:, n * LANES : (n + 1) * LANES] = wide[32 * n + 2 : 32 * n + 3]


def forward_kernel(
    a, u, d, clips, cot,
    wa, wu, wd, og, x_out, middle_out, n1_out, n2_out, qkv_out, att_out, hidden, slope, vec, d_terms,
    xv, og2, n1, n2, qkv, att, middle, wb, hid, hid2, terms, slo, table, wide, ub, bias,
    send, recv, local,
):
    io = Copies(send, recv, local)
    ga, gu, gd = Gather(io, a, wa), Gather(io, u, wu), Gather(io, d, wd)
    t = xv.shape[0]
    own, sib = pl.ds(0, t), pl.ds(t, t)
    core = (io.dp ^ 1, io.z)
    cx, cc = Collect(io, clips, xv), Collect(io, cot, og2.at[own])
    meet(io)

    line = [(g, k) for g in (ga, gu, gd) for k in range(4)]
    place = [0]

    def advance(n=1):
        for _ in range(n):
            i = place[0]
            place[0] += 1
            if i < len(line):
                g, k = line[i]
                if k == 2 and g is not gd:
                    g.arrive_z(2)
                    (gu if g is ga else gd).start_z()
                    if g is ga:
                        cx.start()
                    else:
                        cc.start()
                elif k:
                    g.arrive_z(k)
                g.spread(k)
            if 1 <= i <= len(line):
                g, k = line[i - 1]
                g.pass_on(k)
            if 3 <= i <= len(line) + 2:
                g, k = line[i - 3]
                g.far(k)

    ga.start_z()
    advance(3)
    for g in (ga, gu, gd):
        g.local.wait()
    advance(4)
    outs = []

    ga.done()
    io.load(wa.at[:, pl.ds(4 * D, LANES)], table).wait()
    spread_vectors(table, wide, vec, ub)
    bias[:, 0:D] = vec[2:3]
    bias[:, D : 2 * D] = jnp.zeros((1, D), F32)
    bias[:, 2 * D : 3 * D] = vec[3:4]
    cx.wait()
    outs.append(io.load(xv, x_out))

    def first_norm(i, _):
        rows = pl.ds(pl.multiple_of(i * CHUNK, CHUNK), CHUNK)
        vhat, _r = norm_rows(xv[rows].astype(F32))
        n1[rows] = (vhat * vec[0:1] + vec[1:2]).astype(BF)
        return 0

    lax.fori_loop(0, t // CHUNK, first_norm, 0)
    outs.append(io.load(n1, n1_out))
    advance()

    def columns(ref, lo):
        return lambda i, slot: [(ref.at[:, pl.ds(pl.multiple_of(lo + i * COLS, LANES), COLS)], wb.at[slot])]

    def qkv_step(i, slot):
        qkv[:, lanes(i, COLS)] = (dot(n1[...], wb[slot]) + bias[:, lanes(i, COLS)]).astype(BF)

    stream(io, 3 * D // COLS, columns(wa, 0), qkv_step)
    outs.append(io.load(qkv, qkv_out))
    advance()

    def heads(i, _):
        def at(k):
            return lanes(k * (D // LANES) + i, LANES)

        att[:, at(0)] = attend_pair(qkv[:, at(0)], qkv[:, at(1)], qkv[:, at(2)])
        return 0

    n_pairs = D // LANES
    lax.fori_loop(0, n_pairs // 2, heads, 0)
    advance()
    lax.fori_loop(n_pairs // 2, n_pairs, heads, 0)
    outs.append(io.load(att, att_out))
    advance()

    def proj_step(i, slot):
        cols = lanes(i, COLS)
        middle[:, cols] = xv[:, cols].astype(F32) + (dot(att[...], wb[slot]) + vec[4:5, cols])

    stream(io, D // COLS, columns(wa, 3 * D), proj_step)
    outs.append(io.load(middle, middle_out))

    def second_norm(i, _):
        rows = pl.ds(pl.multiple_of(i * CHUNK, CHUNK), CHUNK)
        vhat, _r = norm_rows(middle[rows])
        n2[rows] = (vhat * vec[5:6] + vec[6:7]).astype(BF)
        return 0

    lax.fori_loop(0, t // CHUNK, second_norm, 0)
    outs.append(io.load(n2, n2_out))
    while place[0] < 7 + 4:
        advance()
    gu.done()

    out_base = io.locals(2)
    hid_slots = io.slots(4)

    def slope_out(i, slot):
        return pltpu.make_async_copy(slo.at[slot], slope.at[:, lanes(i, COLS)], io.local.at[out_base + slot])

    def hid_copy(i):
        j = (io.dp ^ i) // 2
        return io.remote(hid_slots[0] + j, hid.at[:, lanes(i, COLS)], hid2.at[sib, lanes(j, COLS)], core)

    def up_step(i, slot):
        @pl.when(i >= 2)
        def _():
            slope_out(i - 2, slot).wait()

        value, grad = gelu_both(dot(n2[...], wb[slot]) + ub[:, lanes(i, COLS)])
        hid[:, lanes(i, COLS)] = value.astype(BF)
        slo[slot] = grad.astype(BF)
        slope_out(i, slot).start()

        @pl.when((io.dp ^ i) % 2 == 1)
        def _():
            hid_copy(i).start()

        @pl.when((io.dp ^ i) % 2 == 0)
        def _():
            hid2[own, lanes((io.dp ^ i) // 2, COLS)] = value.astype(BF)

    n_up = FF // COLS
    stream(io, n_up // 2, columns(wu, 0), up_step)
    advance()
    stream(io, n_up // 2, columns(wu, FF // 2), lambda i, slot: up_step(i + n_up // 2, slot))
    outs.append(io.load(hid, hidden))
    advance()
    cc.wait()
    outs.append(io.load(og2.at[own], og))
    og_slot = io.slots(1)[0]
    io.start(og_slot, lambda: og2.at[own], lambda: og2.at[sib], core)
    for i in (n_up - 2, n_up - 1):
        slope_out(i, i % 2).wait()
    advance()
    io.arrived(og_slot, lambda: og2.at[sib])
    for j in range(4):
        hid_copy(io.dp ^ (2 * j + 1)).wait()

    def down_terms(j, _):
        terms[j] = dot_tn(hid2[:, lanes(j, COLS)], og2[...]).astype(BF)
        return 0

    lax.fori_loop(0, 2, down_terms, 0)
    advance()
    lax.fori_loop(2, 4, down_terms, 0)
    outs.append(io.load(terms, d_terms))
    while place[0] < len(line) + 3:
        advance()
    gd.done()
    for c in outs:
        c.wait()
    io.finish()


def forward(a, u, d, clips, cot):
    t = clips.shape[1] * 4
    any_ = pl.BlockSpec(memory_space=pl.ANY)
    vmem = pl.BlockSpec(memory_space=pltpu.VMEM)
    sh = jax.ShapeDtypeStruct
    v = pltpu.VMEM
    return pl.pallas_call(
        forward_kernel,
        out_shape=[
            sh((D, a.shape[1]), BF),
            sh((D, FF), BF),
            sh((FF, D), BF),
            sh((t, D), BF),
            sh((t, D), BF),
            sh((t, D), F32),
            sh((t, D), BF),
            sh((t, D), BF),
            sh((t, 3 * D), BF),
            sh((t, D), BF),
            sh((t, FF), BF),
            sh((t, FF), BF),
            sh((8, D), F32),
            sh((4, FF // 8, D), BF),
        ],
        in_specs=[any_] * 5,
        out_specs=[any_] * 12 + [vmem, any_],
        scratch_shapes=[
            v((t, D), BF),
            v((2 * t, D), BF),
            v((t, D), BF),
            v((t, D), BF),
            v((t, 3 * D), BF),
            v((t, D), BF),
            v((t, D), F32),
            v((2, D, COLS), BF),
            v((t, FF), BF),
            v((2 * t, FF // 2), BF),
            v((4, FF // 8, D), BF),
            v((2, t, COLS), BF),
            v((D, LANES), BF),
            v((D, LANES), F32),
            v((1, FF), F32),
            v((1, 3 * D), F32),
            pltpu.SemaphoreType.DMA((N_FORE,)),
            pltpu.SemaphoreType.DMA((N_FORE,)),
            pltpu.SemaphoreType.DMA((48,)),
        ],
        compiler_params=pltpu.CompilerParams(
            collective_id=0, has_side_effects=True, vmem_limit_bytes=56 * 2**20
        ),
    )(a, u, d, clips, cot)


class Reduce:
    def __init__(self, io, r, s, land, pieces, stage, out, direct=False):
        self.io, self.r, self.s, self.land, self.pieces = io, r, s, land, pieces
        self.direct = direct
        self.stage, self.out = stage, out
        self.slot = io.slots(6)
        self.z_slot = io.slots(4)

    def half(self, j, h):
        return self.s(j).at[pl.ds(h * 2 * self.r, 2 * self.r)]

    def send(self, i, j, h, bit):
        io = self.io
        io.start(self.slot[i], lambda: self.half(j, h), lambda: self.land.at[i], (io.dp ^ bit, io.z))

    def start(self):
        self.send(0, 3, 0, 2)
        self.send(1, 3, 1, 4)
        self.send(2, 1, 0, 2)
        self.send(3, 2, 1, 4)

    def load(self, i, at):
        self.io.arrived(self.slot[i], lambda: self.land.at[i])
        return self.io.load(self.land.at[i], self.stage.at[at])

    def relay(self):
        for i, j, h, bit in ((0, 2, 0, 4), (1, 1, 1, 2)):
            self.load(i, i).wait()
            ref = self.half(j, h)
            ref[...] = (ref[...].astype(F32) + self.stage[i].astype(F32)).astype(ref.dtype)
            self.send(5 - i, j, h, bit)

    def fold(self):
        io, r = self.io, self.r
        for i in (0, 1):
            io.sent_wait(self.slot[i])
        for h, (a, b) in enumerate(((2, 5), (4, 3))):
            one, two = self.load(a, 0), self.load(b, 1)
            one.wait()
            two.wait()
            own = self.half(0, h)[...]
            total = own.astype(F32) + self.stage[0].astype(F32) + self.stage[1].astype(F32)
            self.half(3, h)[...] = total.astype(own.dtype)
        for i, k, by in ((0, 3, 3 if self.direct else 1), (1, 1, 1), (2, 2, 2))[: 3 if self.direct else 2]:
            io.start(
                self.z_slot[i],
                lambda k=k: self.piece(io.z ^ k),
                lambda i=i: self.pieces.at[i],
                (io.dp, io.z ^ by),
            )

    def piece(self, z):
        return self.s(3).at[pl.ds(pl.multiple_of(z * self.r, self.r), self.r)]

    def take(self, i):
        spot = self.stage.at[i // 2, pl.ds(i % 2 * self.r, self.r)]
        self.io.arrived(self.z_slot[i], lambda: self.pieces.at[i])
        return self.io.load(self.pieces.at[i], spot), spot

    def cross(self):
        io = self.io
        copy, spot = self.take(0)
        copy.wait()
        ref = self.piece(io.z ^ 2)
        ref[...] = (ref[...].astype(F32) + spot[...].astype(F32)).astype(ref.dtype)
        io.start(
            self.z_slot[2], lambda: self.piece(io.z ^ 2), lambda: self.pieces.at[2], (io.dp, io.z ^ 2)
        )

    def finish(self):
        taken = [self.take(i) for i in ((1, 2, 0) if self.direct else (1, 2))]
        total = self.piece(self.io.z)[...].astype(F32)
        for copy, spot in taken:
            copy.wait()
            total = total + spot[...].astype(F32)
        self.out[...] = total


class HandBack:
    def __init__(self, io, src, dst):
        self.io, self.src, self.dst = io, src, dst
        self.slots = io.slots(4)
        self.rows = dst.shape[1]

    def host(self, z):
        clip = z - self.io.dp % 2
        return (clip >= 0) & (clip < 3)

    def part(self, s):
        return self.src.at[pl.ds(s * self.rows, self.rows)]

    def start(self):
        io = self.io
        for s in range(1, 4):
            to = (io.z + 4 - s) % 4
            io.start(
                self.slots[s], lambda s=s: self.part(s), lambda s=s: self.dst.at[s], (io.dp, to), self.host(io.z)
            )
        copy = io.load(self.part(0), self.dst.at[0])
        copy.wait()

    def wait(self):
        io = self.io
        for s in range(1, 4):
            io.arrived(self.slots[s], lambda s=s: self.dst.at[s], self.host((io.z + s) % 4))


N_BACK = 140
N_LOCAL = 150


def backward_kernel(
    wa, wu, wd, og_in, x, middle, normed1, normed2, qkv_in, attended, hidden, slope, params, d_terms,
    qkv_out, p_out, u_out, d_out, s_out, ret_out, ret_in,
    a_land, u_land, d_land, s_land, a_pieces, u_pieces, d_pieces, s_pieces,
    og, ug2, bg2, jn2, np2, n1p2, atp2, flip, qkv, ag, ob, xv, part, wdb, wb, tiles, hid, acc, s_d, s_u,
    stage_d, stage_u, stage_a, table, table_sib, s_s, stage_s, vec, ub,
    send, recv, local,
):
    io = Copies(send, recv, local)
    dp, z = io.dp, io.z
    t = og.shape[0]
    own, sib = pl.ds(0, t), pl.ds(t, t)
    core = (dp ^ 1, z)

    red_d = Reduce(io, d_out.shape[0], lambda j: s_d.at[j], d_land, d_pieces, stage_d, d_out)
    red_u = Reduce(io, u_out.shape[0], lambda j: s_u.at[j], u_land, u_pieces, stage_u, u_out)
    n_a = p_out.shape[0]

    def part_of_a(c):
        blocks = lambda j: ug2.at[pl.ds(j * 4 * n_a, 4 * n_a), pl.ds(c * D, D)]
        out = p_out if c == 3 else qkv_out.at[:, pl.ds(c * D, D)]
        return Reduce(io, n_a, blocks, a_land.at[c], a_pieces.at[c], stage_a, out, direct=c == 2)

    red_q, red_k, red_v, red_p = (part_of_a(c) for c in range(4))
    red_s = Reduce(io, s_out.shape[0], lambda j: s_s.at[j], s_land, s_pieces, stage_s, s_out, direct=True)
    back_in = HandBack(io, qkv.at[:, pl.ds(D, D)], ret_in)
    back_out = HandBack(io, ob, ret_out)

    def planes(src, dst):
        width = dst.shape[1] // 4
        return [
            io.load(
                src.at[:, pl.ds(pl.multiple_of((dp ^ (2 * j)) * width, LANES), width)],
                dst.at[own, pl.ds(j * width, width)],
            )
            for j in range(4)
        ]

    load_d = io.load(d_terms, s_d)
    load_og = io.load(og_in, og)
    load_x = [io.load(x, xv), io.load(middle, part)]
    meet(io)
    load_d.wait()
    red_d.start()

    def swap_planes(src, dst):
        width = dst.shape[1] // 4
        slots = io.slots(4)
        for j in range(4):
            io.start(
                slots[j],
                lambda j=j: src.at[:, pl.ds(pl.multiple_of((dp ^ (2 * j + 1)) * width, LANES), width)],
                lambda j=j: dst.at[sib, pl.ds(j * width, width)],
                core,
            )
        return [(slots[j], lambda j=j: dst.at[sib, pl.ds(j * width, width)]) for j in range(4)]

    swapped_2 = swap_planes(normed2, np2)
    d_rows = wdb.shape[1]
    w_rows = wb.shape[1]
    load_og.wait()

    acc[...] = jnp.zeros_like(acc)
    ug_slots = io.slots(FF // d_rows)

    def ug_copy(i):
        return io.remote(ug_slots[0] + i, ug2.at[own, lanes(i, d_rows)], ug2.at[sib, lanes(i, d_rows)], core)

    def hidden_step(i, slot):
        grad = dot_nt(og[...], wdb[slot]) * tiles[slot].astype(F32)
        low = grad.astype(BF)
        ug2[own, lanes(i, d_rows)] = low
        ub[:, lanes(i, d_rows)] = jnp.sum(low.astype(F32), axis=0, keepdims=True)
        ug_copy(i).start()
        acc[...] += dot(hid[slot], wdb[slot])

    stream(
        io,
        FF // d_rows,
        lambda i, slot: [
            (wd.at[pl.ds(pl.multiple_of(i * d_rows, d_rows), d_rows)], wdb.at[slot]),
            (slope.at[:, lanes(i, d_rows)], tiles.at[slot]),
            (hidden.at[:, lanes(i, d_rows)], hid.at[slot]),
        ],
        hidden_step,
    )
    for c in load_x:
        c.wait()
    ob[...] = (acc[...] + (part[...] - xv[...].astype(F32)) + params[7:8]).astype(BF)
    back_out.start()
    second = planes(normed2, np2)
    third = planes(normed1, n1p2) + planes(attended, atp2)
    third += [io.load(qkv_in, qkv)]
    swapped_1 = swap_planes(normed1, n1p2)
    swapped_3 = swap_planes(attended, atp2)

    for c in second:
        c.wait()
    for slot, ref in swapped_2:
        io.arrived(slot, ref)
    flip[...] = np2[...].T
    for i in range(FF // d_rows):
        ug_copy(i).wait_recv()

    def up_step(i, _):
        block = dot(flip[...], ug2[:, lanes(i, COLS)]).astype(BF)
        for j in range(4):
            s_u[j, :, lanes(i, COLS)] = block[j * LANES : (j + 1) * LANES]
        return 0

    lax.fori_loop(0, FF // COLS, up_step, 0)
    red_d.relay()
    red_u.start()

    def up_back(i, slot):
        acc[:, lanes(i, w_rows)] = dot_nt(ug2[own], wb[slot, :, 0:FF])

    w_tile = lambda ref, lo, n: lambda i, slot: [
        (ref.at[pl.ds(pl.multiple_of(i * w_rows, w_rows), w_rows), pl.ds(lo, n)], wb.at[slot, :, pl.ds(0, n)])
    ]
    stream(io, D // w_rows, w_tile(wu, 0, FF), up_back)
    for c in third:
        c.wait()
    vec[...] = jnp.zeros_like(vec)

    def second_norm(i, _):
        rows = pl.ds(pl.multiple_of(i * CHUNK, CHUNK), CHUNK)
        e = acc[rows]
        vhat, r = norm_rows(part[rows])
        g = e * params[5:6]
        grad = r * (
            g - jnp.mean(g, axis=-1, keepdims=True) - vhat * jnp.mean(g * vhat, axis=-1, keepdims=True)
        )
        vec[5:6] += jnp.sum(e * vhat, axis=0, keepdims=True)
        vec[6:7] += jnp.sum(e, axis=0, keepdims=True)
        part[rows] = grad
        out_grad = og[rows].astype(F32)
        low = (out_grad + grad).astype(BF)
        bg2[rows] = low
        vec[4:5] += jnp.sum(low.astype(F32), axis=0, keepdims=True)
        vec[7:8] += jnp.sum(out_grad, axis=0, keepdims=True)
        return 0

    lax.fori_loop(0, t // CHUNK, second_norm, 0)
    bg_slot = io.slots(1)[0]
    io.start(bg_slot, lambda: bg2.at[own], lambda: bg2.at[sib], core)

    def proj_back(i, slot):
        ag[:, lanes(i, w_rows)] = dot_nt(bg2[own], wb[slot, :, 0:D]).astype(BF)

    stream(io, D // w_rows, w_tile(wa, 3 * D, D), proj_back)
    for slot in range(FF // d_rows):
        ug_copy(slot).wait_send()
    for slot, ref in swapped_3:
        io.arrived(slot, ref)
    flip[...] = atp2[...].T
    io.arrived(bg_slot, lambda: bg2.at[sib])

    def proj_step(i, _):
        ug2[own, lanes(6 + i, COLS)] = dot(flip[...], bg2[:, lanes(i, COLS)]).astype(BF)
        return 0

    lax.fori_loop(0, D // COLS, proj_step, 0)
    red_p.start()

    def heads(i, _):
        def at(k):
            return lanes(k * (D // LANES) + i, LANES)

        dq, dk, dv = attend_back_pair(qkv[:, at(0)], qkv[:, at(1)], qkv[:, at(2)], ag[:, at(0)])
        for k, grad in enumerate((dq, dk, dv)):
            jn2[own, at(k)] = grad
        vec[2:3, at(0)] = jnp.sum(dq.astype(F32), axis=0, keepdims=True)
        vec[3:4, at(0)] = jnp.sum(dv.astype(F32), axis=0, keepdims=True)
        return 0

    n_pairs = D // LANES
    lax.fori_loop(0, n_pairs // 2, heads, 0)
    red_d.fold()
    lax.fori_loop(n_pairs // 2, n_pairs, heads, 0)
    jn_slot = io.slots(1)[0]
    io.start(jn_slot, lambda: jn2.at[own], lambda: jn2.at[sib], core)
    red_u.relay()
    red_d.cross()

    for slot, ref in swapped_1:
        io.arrived(slot, ref)
    flip[...] = n1p2[...].T

    def first_back(i, slot):
        acc[:, lanes(i, w_rows)] = dot_nt(jn2[own], wb[slot, :, 0 : 3 * D])

    stream(io, D // w_rows, w_tile(wa, 0, 3 * D), first_back)
    def first_norm(i, _):
        rows = pl.ds(pl.multiple_of(i * CHUNK, CHUNK), CHUNK)
        e = acc[rows]
        vhat, r = norm_rows(xv[rows].astype(F32))
        g = e * params[0:1]
        grad = r * (
            g - jnp.mean(g, axis=-1, keepdims=True) - vhat * jnp.mean(g * vhat, axis=-1, keepdims=True)
        )
        vec[0:1] += jnp.sum(e * vhat, axis=0, keepdims=True)
        vec[1:2] += jnp.sum(e, axis=0, keepdims=True)
        qkv[rows, D : 2 * D] = (part[rows] + grad).astype(BF)
        return 0

    lax.fori_loop(0, t // CHUNK, first_norm, 0)
    back_in.start()

    io.arrived(jn_slot, lambda: jn2.at[sib])

    def qkv_step(i, _):
        ug2[own, lanes(i, COLS)] = dot(flip[...], jn2[:, lanes(i, COLS)]).astype(BF)
        return 0

    for c, red in enumerate((red_q, red_k, red_v)):
        lax.fori_loop(c * D // COLS, (c + 1) * D // COLS, qkv_step, 0)
        red.start()
    red_p.relay()
    red_d.finish()

    spread_n = lax.broadcasted_iota(jnp.int32, (32, D), 0)
    spread_c = lax.broadcasted_iota(jnp.int32, (32, D), 1)
    mine = (spread_c // 32) == spread_n
    pick_c = lax.broadcasted_iota(jnp.int32, (D, LANES), 0)
    pick_l = lax.broadcasted_iota(jnp.int32, (D, LANES), 1)
    table[...] = jnp.zeros_like(table)
    for k in range(2):
        rows = jnp.zeros((32, LANES), F32)
        for q in range(4):
            spread = jnp.where(mine, vec[4 * k + q : 4 * k + q + 1], 0.0)
            pick = jnp.where(pick_l == 32 * q + pick_c % 32, 1.0, 0.0)
            rows = rows + jnp.dot(spread, pick, preferred_element_type=F32, precision=lax.Precision.HIGHEST)
        for n in range(32):
            table[8 * n + k : 8 * n + k + 1] = rows[n : n + 1]
    for n in range(32):
        table[8 * n + 2 : 8 * n + 3] = ub[:, n * LANES : (n + 1) * LANES]
    table_slot = io.slots(1)[0]
    io.start(table_slot, lambda: table, lambda: table_sib, core)

    io.arrived(table_slot, lambda: table_sib)
    for j in range(4):
        rows = pl.ds(pl.multiple_of((dp ^ (2 * j)) * 32, 32), 32)
        s_s[j] = table[rows] + table_sib[rows]
    red_s.start()

    red_u.fold()
    red_q.relay()
    red_k.relay()
    red_v.relay()
    red_s.relay()
    red_u.cross()
    red_p.fold()
    red_q.fold()
    red_k.fold()
    red_p.cross()
    red_v.fold()
    red_s.fold()
    red_q.cross()
    red_k.cross()
    for red in (red_u, red_p, red_q, red_k):
        red.finish()
    back_in.wait()
    back_out.wait()
    red_v.finish()
    red_s.finish()
    io.finish()


def backward(*saved):
    t = saved[3].shape[0]
    any_ = pl.BlockSpec(memory_space=pl.ANY)
    vmem = pl.BlockSpec(memory_space=pltpu.VMEM)
    sh = jax.ShapeDtypeStruct
    ra, rd, rs = D // 32, FF // 32, 8
    outs = [
        (sh((ra, 3 * D), F32), vmem),
        (sh((ra, D), F32), vmem),
        (sh((ra, FF), F32), vmem),
        (sh((rd, D), F32), vmem),
        (sh((rs, LANES), F32), vmem),
        (sh((4, t // 4, D), BF), any_),
        (sh((4, t // 4, D), BF), any_),
    ]
    for count, k in ((6, 2), (3, 1)):
        outs += [
            (sh((4, count, k * ra, D), BF), any_),
            (sh((count, k * ra, FF), BF), any_),
            (sh((count, k * rd, D), BF), any_),
            (sh((count, k * rs, LANES), F32), any_),
        ]
    v = pltpu.VMEM
    results = pl.pallas_call(
        backward_kernel,
        out_shape=[o for o, _ in outs],
        in_specs=[any_] * 12 + [vmem, any_],
        out_specs=[o for _, o in outs],
        scratch_shapes=[
            v((t, D), BF),
            v((2 * t, FF), BF),
            v((2 * t, D), BF),
            v((2 * t, 3 * D), BF),
            v((2 * t, D // 2), BF),
            v((2 * t, D // 2), BF),
            v((2 * t, D // 2), BF),
            v((D // 2, 2 * t), BF),
            v((t, 3 * D), BF),
            v((t, D), BF),
            v((t, D), BF),
            v((t, D), BF),
            v((t, D), F32),
            v((2, 512, D), BF),
            v((2, 256, FF), BF),
            v((2, t, 512), BF),
            v((2, t, 512), BF),
            v((t, D), F32),
            v((4, 4 * rd, D), BF),
            v((4, 4 * ra, FF), BF),
            v((2, 2 * rd, D), BF),
            v((2, 2 * ra, FF), BF),
            v((2, 2 * ra, D), BF),
            v((32 * rs, LANES), F32),
            v((32 * rs, LANES), F32),
            v((4, 4 * rs, LANES), F32),
            v((2, 2 * rs, LANES), F32),
            v((8, D), F32),
            v((1, FF), F32),
            pltpu.SemaphoreType.DMA((N_BACK,)),
            pltpu.SemaphoreType.DMA((N_BACK,)),
            pltpu.SemaphoreType.DMA((N_LOCAL,)),
        ],
        compiler_params=pltpu.CompilerParams(
            collective_id=1, has_side_effects=True, vmem_limit_bytes=60 * 2**20
        ),
    )(*saved)
    return results[:7]


def norm_parts(v):
    center = v - jnp.mean(v, axis=-1, keepdims=True)
    r = lax.rsqrt(jnp.mean(center * center, axis=-1, keepdims=True) + EPSILON)
    return center * r, r


def norm_back(vhat, r, gain, e):
    t = e * gain
    grad = r * (
        t - jnp.mean(t, axis=-1, keepdims=True) - vhat * jnp.mean(t * vhat, axis=-1, keepdims=True)
    )
    return grad, jnp.sum(e * vhat, axis=0), jnp.sum(e, axis=0)


SMALL = (D, D, D, D, D, D, D, D, FF)


def per_device(
    n_dp,
    n_seq,
    clips,
    counts,
    out_cotangent,
    norm1_gain,
    norm1_shift,
    qkv_weight,
    query_bias,
    value_bias,
    proj_weight,
    proj_bias,
    norm2_gain,
    norm2_shift,
    up_weight,
    up_bias,
    down_weight,
    down_bias,
):
    links = Links(n_dp, n_seq)
    n = n_dp * n_seq
    slots = clips.shape[0]
    rows = D // n
    small = (
        norm1_gain,
        norm1_shift,
        query_bias,
        value_bias,
        proj_bias,
        norm2_gain,
        norm2_shift,
        down_bias,
        up_bias,
    )
    packed = jnp.concatenate(small)
    packed = jnp.pad(packed, (0, rows * LANES - packed.shape[0])).reshape(rows, LANES)
    shard_a = jnp.concatenate(
        [qkv_weight.reshape(rows, 3 * D), proj_weight.reshape(rows, D), packed], axis=1
    ).astype(BF)
    shard_u = up_weight.reshape(rows, FF).astype(BF)
    shard_d = down_weight.reshape(FF // n, D).astype(BF)

    living = (jnp.arange(slots) < counts[0]).astype(F32)[:, None, None]
    living_cot = living * out_cotangent
    tokens = (clips.astype(BF), living_cot.astype(BF))
    if links.short:
        saved = forward(shard_a, shard_u, shard_d, *tokens)
        qkv_grad, proj_grad, up_grad, down_grad, small_grad, out_back, in_back = backward(*saved)
        out_home, in_home = links.by_clip(out_back, slots), links.by_clip(in_back, slots)
        small_out = small_grad[:3].reshape(-1)
    else:
        a_mat, u_mat, d_mat = (links.gather(shard) for shard in (shard_a, shard_u, shard_d))
        x, out_grad = (links.collect(t) for t in tokens)
        x = x.astype(F32)

        table = a_mat[:, 4 * D :].reshape(n_dp, n_seq, rows * LANES)
        table = table.reshape(n, rows * LANES).astype(F32)
        vectors, at = [], 0
        for size in SMALL:
            vectors.append(table[:, at : at + size // n].reshape(size))
            at += size // n
        gain1, shift1, q_bias, v_bias, p_bias, gain2, shift2, d_bias, u_bias = vectors

        vhat1, r1 = norm_parts(x)
        normed1 = (vhat1 * gain1 + shift1).astype(BF)
        qkv_bias = jnp.concatenate([q_bias, jnp.zeros_like(q_bias), v_bias])
        qkv_mat, proj_mat = a_mat[:, : 3 * D], a_mat[:, 3 * D : 4 * D]
        qkv = (dot(normed1, qkv_mat) + qkv_bias).astype(BF)
        attended = attend(qkv)
        branch = dot(attended, proj_mat) + p_bias
        middle = x + branch
        vhat2, r2 = norm_parts(middle)
        normed2 = (vhat2 * gain2 + shift2).astype(BF)
        hidden, slope = gelu_both(dot(normed2, u_mat) + u_bias)
        hidden = hidden.astype(BF)
        slope = slope.astype(BF)
        out_part = branch + dot(hidden, d_mat) + d_bias
        out_home = links.hand_back(out_part.astype(BF), slots)
        down_grad = links.reduce(dot_tn(hidden, out_grad))
        upper_grad = (dot_nt(out_grad, d_mat) * slope).astype(BF)
        up_grad = links.reduce(dot_tn(normed2, upper_grad))
        part, gain2_grad, shift2_grad = norm_back(vhat2, r2, gain2, dot_nt(upper_grad, u_mat))
        branch_grad = (out_grad.astype(F32) + part).astype(BF)
        dq, dk, dv = attend_back(qkv, dot_nt(branch_grad, proj_mat).astype(BF))
        joined = jnp.concatenate([dq, dk, dv], axis=1)
        first_part, gain1_grad, shift1_grad = norm_back(vhat1, r1, gain1, dot_nt(joined, qkv_mat))
        in_home = links.hand_back((part + first_part).astype(BF), slots)
        total = lambda g: jnp.sum(g.astype(F32), axis=0)
        small_grads = (
            gain1_grad,
            shift1_grad,
            total(dq),
            total(dv),
            total(branch_grad),
            gain2_grad,
            shift2_grad,
            total(out_grad),
            total(upper_grad),
        )
        grad_table = jnp.concatenate([g.reshape(n, -1) for g in small_grads], axis=1)
        width = grad_table.shape[1]
        grad_table = jnp.pad(grad_table, ((0, 0), (0, rows * LANES - width)))
        d_a = [dot_tn(normed1, joined), dot_tn(attended, branch_grad), grad_table.reshape(n * rows, LANES)]
        a_grad = links.reduce(jnp.concatenate(d_a, axis=1))
        qkv_grad, proj_grad = a_grad[:, : 3 * D], a_grad[:, 3 * D : 4 * D]
        small_out = a_grad[:, 4 * D :].reshape(-1)
    block_out = living * (clips + out_home.astype(F32))
    input_grad = living_cot + in_home.astype(F32)
    pieces, at = [], 0
    for size in SMALL:
        pieces.append(small_out[at : at + size // n])
        at += size // n
    g1, s1, qb, vb, pb, g2, s2, db, ub = pieces
    return (
        block_out,
        input_grad,
        g1,
        s1,
        qkv_grad.reshape(-1),
        qb,
        vb,
        proj_grad.reshape(-1),
        pb,
        g2,
        s2,
        up_grad.reshape(-1),
        ub,
        down_grad.reshape(-1),
        db,
    )


def solution(mesh):
    flat = P(AXES)
    tokens = P("dp", "seq", None)
    return jax.shard_map(
        functools.partial(per_device, mesh.shape["dp"], mesh.shape["seq"]),
        mesh=mesh,
        in_specs=(tokens, P("dp"), tokens) + (flat,) * 13,
        out_specs=(tokens, tokens) + (flat,) * 13,
        check_vma=False,
    )
```

```python
import functools

import jax
import jax.numpy as jnp
from jax import lax
from jax.experimental import pallas as pl
from jax.experimental.pallas import tpu as pltpu
from jax.sharding import PartitionSpec as P

D = 1024
FF = 4096
HEADS = 16
HEAD_DIM = 64
EPSILON = 1e-05
LANES = 128
BF = jnp.bfloat16
F32 = jnp.float32
AXES = ("dp", "seq")
MESH = pl.DeviceIdType.MESH


def dot(a, b):
    return jnp.dot(a, b, preferred_element_type=F32)


def dot_nt(a, b):
    return lax.dot_general(a, b, (((1,), (1,)), ((), ())), preferred_element_type=F32)


def dot_tn(a, b):
    return lax.dot_general(a, b, (((0,), (0,)), ((), ())), preferred_element_type=F32)


def soft_t(q2, k_half):
    scores = dot_nt(k_half, q2) * (HEAD_DIM**-0.5)
    top = jnp.max(scores, axis=0, keepdims=True)
    e = jnp.exp(scores - top)
    return e * (1.0 / jnp.sum(e, axis=0, keepdims=True))


def attend_pair(q2, k2, v2):
    low = lax.broadcasted_iota(jnp.int32, k2.shape, 1) < HEAD_DIM
    v_t = v2.T
    zero = jnp.zeros_like(k2)
    parts = []
    for h in range(2):
        k_half = jnp.where(low == (h == 0), k2, zero)
        p_t = soft_t(q2, k_half).astype(BF)
        parts.append(dot(v_t[h * HEAD_DIM : (h + 1) * HEAD_DIM], p_t))
    return jnp.concatenate(parts, axis=0).T.astype(BF)


def attend_kernel(q_ref, k_ref, v_ref, o_ref):
    o_ref[...] = attend_pair(q_ref[...], k_ref[...], v_ref[...])


def attend(qkv):
    t = qkv.shape[0]
    n = D // LANES
    spec = lambda off: pl.BlockSpec((t, LANES), lambda h: (0, off + h))
    return pl.pallas_call(
        attend_kernel,
        grid=(n,),
        out_shape=jax.ShapeDtypeStruct((t, D), BF),
        in_specs=[spec(0), spec(n), spec(2 * n)],
        out_specs=spec(0),
        compiler_params=pltpu.CompilerParams(vmem_limit_bytes=48 * 2**20),
        cost_estimate=pl.CostEstimate(
            flops=16 * 4 * t * t * HEAD_DIM, bytes_accessed=8 * t * D, transcendentals=16 * t * t
        ),
    )(qkv, qkv, qkv)


def attend_back_pair(q2, k2, v2, do2):
    low = lax.broadcasted_iota(jnp.int32, k2.shape, 1) < HEAD_DIM
    k_t = k2.T
    zero = jnp.zeros_like(k2)
    dq, dk, dv = [], [], []
    for h in range(2):
        mine = low == (h == 0)
        p = soft_t(q2, jnp.where(mine, k2, zero))
        dp = dot_nt(jnp.where(mine, v2, zero), do2)
        total = jnp.sum(p * dp, axis=0, keepdims=True)
        ds = (p * (dp - total)).astype(BF)
        dv.append(dot(p.astype(BF), do2))
        dk.append(dot(ds, q2))
        dq.append(dot(k_t[h * HEAD_DIM : (h + 1) * HEAD_DIM], ds))
    scale = HEAD_DIM**-0.5
    return (
        (jnp.concatenate(dq, axis=0).T * scale).astype(BF),
        (jnp.where(low, dk[0], dk[1]) * scale).astype(BF),
        jnp.where(low, dv[0], dv[1]).astype(BF),
    )


def attend_back_kernel(q_ref, k_ref, v_ref, do_ref, dq_ref, dk_ref, dv_ref):
    grads = attend_back_pair(q_ref[...], k_ref[...], v_ref[...], do_ref[...])
    dq_ref[...], dk_ref[...], dv_ref[...] = grads


def attend_back(qkv, do):
    t = qkv.shape[0]
    n = D // LANES
    spec = lambda off: pl.BlockSpec((t, LANES), lambda h: (0, off + h))
    return pl.pallas_call(
        attend_back_kernel,
        grid=(n,),
        out_shape=[jax.ShapeDtypeStruct((t, D), BF)] * 3,
        in_specs=[spec(0), spec(n), spec(2 * n), spec(0)],
        out_specs=[spec(0)] * 3,
        compiler_params=pltpu.CompilerParams(vmem_limit_bytes=48 * 2**20),
        cost_estimate=pl.CostEstimate(
            flops=16 * 10 * t * t * HEAD_DIM, bytes_accessed=14 * t * D, transcendentals=16 * t * t
        ),
    )(qkv, qkv, qkv, do)


class Links:
    def __init__(self, n_dp, n_seq):
        self.n_dp, self.n_seq = n_dp, n_seq
        self.short = n_dp == 8 and n_seq == 4
        self.dp = lax.axis_index("dp")
        self.z = lax.axis_index("seq")

    def gather(self, shard):
        return lax.all_gather(shard, AXES, axis=0, tiled=True)

    def reduce(self, grad):
        return lax.psum_scatter(grad.astype(BF), AXES, scatter_dimension=0, tiled=True).astype(F32)


    def lead(self, d, slots):
        return d % 2 if self.n_seq > slots else 0

    def shift_pairs(self, s, slots):
        n = self.n_seq
        pairs = []
        for d in range(self.n_dp):
            for z in range(n):
                to = (z + s) % n
                if 0 <= to - self.lead(d, slots) < slots:
                    pairs.append((d * n + z, d * n + to))
        return pairs

    def my_clip(self, slots):
        lead = self.dp % 2 if self.n_seq > slots else 0
        return self.z - lead

    def collect(self, x):
        slots, n = x.shape[0], self.n_seq
        clip = self.my_clip(slots)
        parts = []
        for s in range(n):
            lead = self.z - clip
            index = jnp.clip((self.z + s) % n - lead, 0, slots - 1)
            part = lax.dynamic_index_in_dim(x, index, 0, False)
            parts.append(part if s == 0 else lax.ppermute(part, AXES, self.shift_pairs(s, slots)))
        host = (clip >= 0) & (clip < slots)
        return jnp.where(host, jnp.concatenate(parts), jnp.zeros((), x.dtype))

    def hand_back(self, y, slots):
        n = self.n_seq
        rows = y.shape[0] // n
        back = []
        for s in range(n):
            part = y[s * rows : (s + 1) * rows]
            pairs = [(b, a) for a, b in self.shift_pairs(s, slots)]
            back.append(part if s == 0 else lax.ppermute(part, AXES, pairs))
        return self.by_clip(jnp.stack(back), slots)

    def by_clip(self, back, slots):
        n = self.n_seq
        lead = self.z - self.my_clip(slots)
        return jnp.stack(
            [lax.dynamic_index_in_dim(back, (c + lead - self.z) % n, 0, False) for c in range(slots)]
        )


def norm_rows(v):
    center = v - jnp.mean(v, axis=-1, keepdims=True)
    r = lax.rsqrt(jnp.mean(center * center, axis=-1, keepdims=True) + EPSILON)
    return center * r, r


def gelu_both(u):
    cdf = 0.5 * (1.0 + lax.erf(u * 0.7071067811865476))
    pdf = 0.3989422804014327 * jnp.exp(-0.5 * u * u)
    return u * cdf, cdf + u * pdf


def guarded(cond, f):
    if cond is None: f()
    else: pl.when(cond)(f)

class Copies:
    def __init__(self, send, recv, local=None):
        self.send, self.recv, self.n, self.sent = send, recv, 0, []
        self.local, self.n_local = local, 0
        self.dp, self.z = lax.axis_index("dp"), lax.axis_index("seq")
    def slots(self, k):
        self.n += k
        return list(range(self.n - k, self.n))
    def remote(self, slot, src, dst, dev):
        return pltpu.make_async_remote_copy(src_ref=src, dst_ref=dst, send_sem=self.send.at[slot], recv_sem=self.recv.at[slot], device_id=dev, device_id_type=MESH)
    def start(self, slot, src, dst, dev, cond=None):
        guarded(cond, lambda: self.remote(slot, src(), dst(), dev).start())
        self.sent.append((slot, src, dst, dev, cond))
    def arrived(self, slot, dst, cond=None):
        guarded(cond, lambda: self.remote(slot, dst(), dst(), (self.dp ^ 1, self.z)).wait_recv())
    def sent_wait(self, which=None):
        rest = []
        for slot, src, dst, dev, cond in self.sent:
            if which is None or slot == which:
                guarded(cond, lambda: self.remote(slot, src(), dst(), dev).wait_send())
            else:
                rest.append((slot, src, dst, dev, cond))
        self.sent = rest
    def finish(self):
        self.sent_wait()
    def locals(self, k):
        self.n_local += k
        return self.n_local - k
    def load(self, src, dst):
        copy = pltpu.make_async_copy(src, dst, self.local.at[self.locals(1)])
        copy.start()
        return copy


class Gather:
    def __init__(self, io, shard, out):
        self.io, self.shard, self.out = io, shard, out
        self.r = shard.shape[0]
        self.keys = (0, 1, 2, 3)
        self.z_slot = io.slots(4)
        self.slot = {k: {name: io.slots(2) for name in ("x", "y", "d", "own", "cx", "cy", "cd")} for k in self.keys}

    def at(self, m, k, part=None):
        io, r = self.io, self.r
        base, n = ((io.dp ^ m) * 4 + (io.z ^ k)) * r, r
        if part is not None:
            n = n // 2
            base = base + part * n
        return self.out.at[pl.ds(pl.multiple_of(base, 16), n)]

    def move(self, name, i, m, k, bit, part=None, src=None):
        io = self.io
        ref = lambda: self.at(m, k, part)
        io.start(self.slot[k][name][i], src or ref, ref, (io.dp ^ bit, io.z))

    def got(self, name, i, m, k, part=None):
        self.io.arrived(self.slot[k][name][i], lambda: self.at(m, k, part))

    def begin(self):
        self.local = self.io.load(self.shard, self.at(0, 0))

    def start_z(self):
        io = self.io
        for k in (1, 2):
            io.start(self.z_slot[k], lambda: self.shard, lambda: self.at(0, 0), (io.dp, io.z ^ k))

    def arrive_z(self, k):
        io = self.io
        ref = lambda: self.at(0, k)
        io.arrived(self.z_slot[k], ref)
        if k == 2:
            io.start(self.z_slot[3], ref, ref, (io.dp, io.z ^ 1))

    def spread(self, k):
        src = (lambda: self.shard) if k == 0 else None
        self.move("x", 0, 0, k, 2, src=src)
        self.move("y", 0, 0, k, 4, src=src)
        self.move("own", 0, 0, k, 1, src=src)

    def pass_on(self, k):
        self.got("x", 0, 2, k)
        self.move("d", 0, 2, k, 4, 0)
        self.got("y", 0, 4, k)
        self.move("d", 1, 4, k, 2, 1)
        self.move("cx", 0, 2, k, 1)
        self.move("cy", 0, 4, k, 1)

    def far(self, k):
        for h in range(2):
            self.got("d", h, 6, k, h)
            self.move("cd", h, 6, k, 1, h)

    def done(self):
        for k in self.keys:
            self.got("own", 0, 1, k)
            self.got("cx", 0, 3, k)
            self.got("cy", 0, 5, k)
            for h in range(2):
                self.got("cd", h, 7, k, h)


class Collect:
    def __init__(self, io, src, dst):
        self.io, self.src, self.dst = io, src, dst
        self.slots = io.slots(4)
        self.local = io.locals(1)
        self.rows = src.shape[1]
        self.host = self.valid(io.z)

    def part(self, s):
        return self.dst.at[pl.ds(s * self.rows, self.rows)]

    def valid(self, z):
        clip = z - self.io.dp % 2
        return (clip >= 0) & (clip < 3)

    def start(self):
        io = self.io
        for s in range(4):
            to = (io.z + s) % 4
            src = lambda to=to: self.src.at[jnp.clip(to - io.dp % 2, 0, 2)]
            if s == 0:
                copy = lambda: pltpu.make_async_copy(src(), self.part(0), io.local.at[self.local]).start()
                guarded(self.host, copy)
            else:
                io.start(self.slots[s], src, lambda s=s: self.part(s), (io.dp, to), self.valid(to))

    def wait(self):
        io = self.io
        copy = lambda: pltpu.make_async_copy(self.part(0), self.part(0), io.local.at[self.local]).wait()
        guarded(self.host, copy)
        for s in range(1, 4):
            io.arrived(self.slots[s], lambda s=s: self.part(s), self.host)

        def clear():
            self.dst[...] = jnp.zeros_like(self.dst)

        guarded(jnp.logical_not(self.host), clear)


N_FORE = 200
CHUNK = 128
COLS = 512


def stream(io, n, copies, body):
    base = io.locals(2 * len(copies(0, 0)))

    def make(i, slot):
        return [
            pltpu.make_async_copy(a, b, io.local.at[base + 2 * c + slot])
            for c, (a, b) in enumerate(copies(i, slot))
        ]

    for c in make(0, 0):
        c.start()

    def step(i, _):
        slot = i % 2

        @pl.when(i + 1 < n)
        def _():
            for c in make(i + 1, (i + 1) % 2):
                c.start()

        for c in make(i, slot):
            c.wait()
        body(i, slot)
        return 0

    lax.fori_loop(0, n, step, 0)


def lanes(i, width):
    return pl.ds(pl.multiple_of(i * width, LANES), width)


def meet(io):
    bar = pltpu.get_barrier_semaphore()
    partners = [(io.dp, io.z ^ k) for k in (1, 2, 3)] + [(io.dp ^ b, io.z) for b in (1, 2, 4)]
    for p in partners:
        pl.semaphore_signal(bar, inc=1, device_id=p, device_id_type=MESH)
    pl.semaphore_wait(bar, len(partners))


def spread_vectors(table, wide, vec, ub):
    wide[...] = table[...].astype(F32)
    spread_n = lax.broadcasted_iota(jnp.int32, (32, D), 0)
    spread_c = lax.broadcasted_iota(jnp.int32, (32, D), 1)
    mine = (spread_c // 32) == spread_n
    pick_l = lax.broadcasted_iota(jnp.int32, (LANES, D), 0)
    pick_c = lax.broadcasted_iota(jnp.int32, (LANES, D), 1)
    for k in range(2):
        rows = jnp.concatenate([wide[32 * n + k : 32 * n + k + 1] for n in range(32)], axis=0).astype(BF)
        for q in range(4):
            pick = jnp.where(pick_l == 32 * q + pick_c % 32, 1.0, 0.0).astype(BF)
            spread = jnp.where(mine, dot(rows, pick), 0.0)
            vec[4 * k + q : 4 * k + q + 1] = jnp.sum(spread, axis=0, keepdims=True)
    for n in range(32):
        ub[:, n * LANES : (n + 1) * LANES] = wide[32 * n + 2 : 32 * n + 3]


def forward_kernel(
    qkv_flat, proj_flat, small, up_flat, down_flat, clips, cot, living,
    wa, wu, wd, og, x_out, middle_out, n1_out, n2_out, qkv_out, att_out, hidden, slope, vec, d_terms,
    wide_q, wide_p, wide_s, wide_u, wide_d, a, u, d, wide_x, wide_c, low_x, low_c, xv, og2, n1, n2, qkv, att, middle, wb, hid, hid2, terms, slo, table, wide, ub, bias,
    send, recv, local,
):
    io = Copies(send, recv, local)
    ga, gu, gd = Gather(io, a, wa), Gather(io, u, wu), Gather(io, d, wd)
    t = xv.shape[0]
    own, sib = pl.ds(0, t), pl.ds(t, t)
    core = (io.dp ^ 1, io.z)
    cx, cc = Collect(io, low_x, xv), Collect(io, low_c, og2.at[own])
    load_a = [io.load(qkv_flat, wide_q), io.load(proj_flat, wide_p), io.load(small, wide_s)]
    load_u, load_d = io.load(up_flat, wide_u), io.load(down_flat, wide_d)
    load_x, load_c = io.load(clips, wide_x), io.load(cot, wide_c)

    def fill(dst, at, flat):
        n = dst.shape[0]
        tiles = flat.shape[0] // n
        for c in range(tiles):
            dst[:, at + c * LANES : at + (c + 1) * LANES] = flat[pl.ds(c, n, stride=tiles), :].astype(BF)

    for c in load_a:
        c.wait()
    fill(a, 0, wide_q)
    fill(a, 3 * D, wide_p)
    a[:, 4 * D : 4 * D + LANES] = wide_s[...].astype(BF)
    ga.begin()
    meet(io)

    line = [(g, k) for g in (ga, gu, gd) for k in range(4)]
    place = [0]

    def advance(n=1):
        for _ in range(n):
            i = place[0]
            place[0] += 1
            if i < len(line):
                g, k = line[i]
                if k == 2 and g is not gd:
                    g.arrive_z(2)
                    (gu if g is ga else gd).start_z()
                    if g is ga:
                        cx.start()
                    else:
                        cc.start()
                elif k:
                    g.arrive_z(k)
                g.spread(k)
            if 1 <= i <= len(line):
                g, k = line[i - 1]
                g.pass_on(k)
            if 3 <= i <= len(line) + 2:
                g, k = line[i - 3]
                g.far(k)

    ga.start_z()
    advance()
    load_x.wait()
    low_x[...] = wide_x[...].astype(BF)
    load_u.wait()
    fill(u, 0, wide_u)
    gu.begin()
    advance(2)
    load_d.wait()
    fill(d, 0, wide_d)
    gd.begin()
    for g in (ga, gu, gd):
        g.local.wait()
    load_c.wait()
    for c in range(3):
        low_c[c] = (wide_c[c] * living[c : c + 1, 0:1]).astype(BF)
    advance(4)
    outs = []

    ga.done()
    io.load(wa.at[:, pl.ds(4 * D, LANES)], table).wait()
    spread_vectors(table, wide, vec, ub)
    bias[:, 0:D] = vec[2:3]
    bias[:, D : 2 * D] = jnp.zeros((1, D), F32)
    bias[:, 2 * D : 3 * D] = vec[3:4]
    cx.wait()
    outs.append(io.load(xv, x_out))

    def first_norm(i, _):
        rows = pl.ds(pl.multiple_of(i * CHUNK, CHUNK), CHUNK)
        vhat, _r = norm_rows(xv[rows].astype(F32))
        n1[rows] = (vhat * vec[0:1] + vec[1:2]).astype(BF)
        return 0

    lax.fori_loop(0, t // CHUNK, first_norm, 0)
    outs.append(io.load(n1, n1_out))
    advance()

    def columns(ref, lo):
        return lambda i, slot: [(ref.at[:, pl.ds(pl.multiple_of(lo + i * COLS, LANES), COLS)], wb.at[slot])]

    def qkv_step(i, slot):
        qkv[:, lanes(i, COLS)] = (dot(n1[...], wb[slot]) + bias[:, lanes(i, COLS)]).astype(BF)

    stream(io, 3 * D // COLS, columns(wa, 0), qkv_step)
    outs.append(io.load(qkv, qkv_out))
    advance()

    def heads(i, _):
        def at(k):
            return lanes(k * (D // LANES) + i, LANES)

        att[:, at(0)] = attend_pair(qkv[:, at(0)], qkv[:, at(1)], qkv[:, at(2)])
        return 0

    n_pairs = D // LANES
    lax.fori_loop(0, n_pairs // 2, heads, 0)
    advance()
    lax.fori_loop(n_pairs // 2, n_pairs, heads, 0)
    outs.append(io.load(att, att_out))
    advance()

    def proj_step(i, slot):
        cols = lanes(i, COLS)
        middle[:, cols] = xv[:, cols].astype(F32) + (dot(att[...], wb[slot]) + vec[4:5, cols])

    stream(io, D // COLS, columns(wa, 3 * D), proj_step)
    outs.append(io.load(middle, middle_out))

    def second_norm(i, _):
        rows = pl.ds(pl.multiple_of(i * CHUNK, CHUNK), CHUNK)
        vhat, _r = norm_rows(middle[rows])
        n2[rows] = (vhat * vec[5:6] + vec[6:7]).astype(BF)
        return 0

    lax.fori_loop(0, t // CHUNK, second_norm, 0)
    outs.append(io.load(n2, n2_out))
    while place[0] < 7 + 4:
        advance()
    gu.done()

    out_base = io.locals(2)
    hid_slots = io.slots(4)

    def slope_out(i, slot):
        return pltpu.make_async_copy(slo.at[slot], slope.at[:, lanes(i, COLS)], io.local.at[out_base + slot])

    def hid_copy(i):
        j = (io.dp ^ i) // 2
        return io.remote(hid_slots[0] + j, hid.at[:, lanes(i, COLS)], hid2.at[sib, lanes(j, COLS)], core)

    def up_step(i, slot):
        @pl.when(i >= 2)
        def _():
            slope_out(i - 2, slot).wait()

        value, grad = gelu_both(dot(n2[...], wb[slot]) + ub[:, lanes(i, COLS)])
        hid[:, lanes(i, COLS)] = value.astype(BF)
        slo[slot] = grad.astype(BF)
        slope_out(i, slot).start()

        @pl.when((io.dp ^ i) % 2 == 1)
        def _():
            hid_copy(i).start()

        @pl.when((io.dp ^ i) % 2 == 0)
        def _():
            hid2[own, lanes((io.dp ^ i) // 2, COLS)] = value.astype(BF)

    n_up = FF // COLS
    stream(io, n_up // 2, columns(wu, 0), up_step)
    advance()
    stream(io, n_up // 2, columns(wu, FF // 2), lambda i, slot: up_step(i + n_up // 2, slot))
    outs.append(io.load(hid, hidden))
    advance()
    cc.wait()
    outs.append(io.load(og2.at[own], og))
    og_slot = io.slots(1)[0]
    io.start(og_slot, lambda: og2.at[own], lambda: og2.at[sib], core)
    for i in (n_up - 2, n_up - 1):
        slope_out(i, i % 2).wait()
    advance()
    io.arrived(og_slot, lambda: og2.at[sib])
    for j in range(4):
        hid_copy(io.dp ^ (2 * j + 1)).wait()

    def down_terms(j, _):
        terms[j] = dot_tn(hid2[:, lanes(j, COLS)], og2[...]).astype(BF)
        return 0

    lax.fori_loop(0, 2, down_terms, 0)
    advance()
    lax.fori_loop(2, 4, down_terms, 0)
    outs.append(io.load(terms, d_terms))
    while place[0] < len(line) + 3:
        advance()
    gd.done()
    for c in outs:
        c.wait()
    io.finish()


def forward(*args):
    clips = args[5]
    n = 32
    t = clips.shape[1] * 4
    any_ = pl.BlockSpec(memory_space=pl.ANY)
    vmem = pl.BlockSpec(memory_space=pltpu.VMEM)
    sh = jax.ShapeDtypeStruct
    v = pltpu.VMEM
    return pl.pallas_call(
        forward_kernel,
        out_shape=[
            sh((D, 4 * D + LANES), BF),
            sh((D, FF), BF),
            sh((FF, D), BF),
            sh((t, D), BF),
            sh((t, D), BF),
            sh((t, D), F32),
            sh((t, D), BF),
            sh((t, D), BF),
            sh((t, 3 * D), BF),
            sh((t, D), BF),
            sh((t, FF), BF),
            sh((t, FF), BF),
            sh((8, D), F32),
            sh((4, FF // 8, D), BF),
        ],
        in_specs=[any_] * 7 + [vmem],
        out_specs=[any_] * 12 + [vmem, any_],
        scratch_shapes=[v(w.shape, F32) for w in args[:5]]
        + [
            v((D // n, 4 * D + LANES), BF),
            v((D // n, FF), BF),
            v((FF // n, D), BF),
            v(clips.shape, F32),
            v(clips.shape, F32),
            v(clips.shape, BF),
            v(clips.shape, BF),
            v((t, D), BF),
            v((2 * t, D), BF),
            v((t, D), BF),
            v((t, D), BF),
            v((t, 3 * D), BF),
            v((t, D), BF),
            v((t, D), F32),
            v((2, D, COLS), BF),
            v((t, FF), BF),
            v((2 * t, FF // 2), BF),
            v((4, FF // 8, D), BF),
            v((2, t, COLS), BF),
            v((D, LANES), BF),
            v((D, LANES), F32),
            v((1, FF), F32),
            v((1, 3 * D), F32),
            pltpu.SemaphoreType.DMA((N_FORE,)),
            pltpu.SemaphoreType.DMA((N_FORE,)),
            pltpu.SemaphoreType.DMA((48,)),
        ],
        compiler_params=pltpu.CompilerParams(
            collective_id=0, has_side_effects=True, vmem_limit_bytes=56 * 2**20
        ),
    )(*args)


class Reduce:
    def __init__(self, io, r, s, land, pieces, stage, out, direct=False):
        self.io, self.r, self.s, self.land, self.pieces = io, r, s, land, pieces
        self.direct = direct
        self.stage, self.out = stage, out
        self.slot = io.slots(6)
        self.z_slot = io.slots(4)

    def half(self, j, h):
        return self.s(j).at[pl.ds(h * 2 * self.r, 2 * self.r)]

    def send(self, i, j, h, bit):
        io = self.io
        io.start(self.slot[i], lambda: self.half(j, h), lambda: self.land.at[i], (io.dp ^ bit, io.z))

    def start(self):
        self.send(0, 3, 0, 2)
        self.send(1, 3, 1, 4)
        self.send(2, 1, 0, 2)
        self.send(3, 2, 1, 4)

    def load(self, i, at):
        self.io.arrived(self.slot[i], lambda: self.land.at[i])
        return self.io.load(self.land.at[i], self.stage.at[at])

    def relay(self):
        for i, j, h, bit in ((0, 2, 0, 4), (1, 1, 1, 2)):
            self.load(i, i).wait()
            ref = self.half(j, h)
            ref[...] = (ref[...].astype(F32) + self.stage[i].astype(F32)).astype(ref.dtype)
            self.send(5 - i, j, h, bit)

    def fold(self):
        io, r = self.io, self.r
        for i in (0, 1):
            io.sent_wait(self.slot[i])
        for h, (a, b) in enumerate(((2, 5), (4, 3))):
            one, two = self.load(a, 0), self.load(b, 1)
            one.wait()
            two.wait()
            own = self.half(0, h)[...]
            total = own.astype(F32) + self.stage[0].astype(F32) + self.stage[1].astype(F32)
            self.half(3, h)[...] = total.astype(own.dtype)
        for i, k, by in ((0, 3, 3 if self.direct else 1), (1, 1, 1), (2, 2, 2))[: 3 if self.direct else 2]:
            io.start(
                self.z_slot[i],
                lambda k=k: self.piece(io.z ^ k),
                lambda i=i: self.pieces.at[i],
                (io.dp, io.z ^ by),
            )

    def piece(self, z):
        return self.s(3).at[pl.ds(pl.multiple_of(z * self.r, self.r), self.r)]

    def take(self, i):
        spot = self.stage.at[i // 2, pl.ds(i % 2 * self.r, self.r)]
        self.io.arrived(self.z_slot[i], lambda: self.pieces.at[i])
        return self.io.load(self.pieces.at[i], spot), spot

    def cross(self):
        io = self.io
        copy, spot = self.take(0)
        copy.wait()
        ref = self.piece(io.z ^ 2)
        ref[...] = (ref[...].astype(F32) + spot[...].astype(F32)).astype(ref.dtype)
        io.start(
            self.z_slot[2], lambda: self.piece(io.z ^ 2), lambda: self.pieces.at[2], (io.dp, io.z ^ 2)
        )

    def finish(self):
        taken = [self.take(i) for i in ((1, 2, 0) if self.direct else (1, 2))]
        total = self.piece(self.io.z)[...].astype(F32)
        for copy, spot in taken:
            copy.wait()
            total = total + spot[...].astype(F32)
        self.out[...] = total


class HandBack:
    def __init__(self, io, src, dst):
        self.io, self.src, self.dst = io, src, dst
        self.slots = io.slots(4)
        self.local = io.locals(1)
        self.rows = dst.shape[1]

    def host(self, z):
        clip = z - self.io.dp % 2
        return (clip >= 0) & (clip < 3)

    def part(self, s):
        return self.src.at[pl.ds(s * self.rows, self.rows)]

    def start(self):
        io = self.io
        for s in range(1, 4):
            to = (io.z + 4 - s) % 4
            io.start(
                self.slots[s], lambda s=s: self.part(s), lambda s=s: self.dst.at[s], (io.dp, to), self.host(io.z)
            )
        copy = io.load(self.part(0), self.dst.at[0])
        copy.wait()

    def wait(self):
        io = self.io
        for s in range(1, 4):
            io.arrived(self.slots[s], lambda s=s: self.dst.at[s], self.host((io.z + s) % 4))


N_BACK = 140
N_LOCAL = 150


def backward_kernel(
    wa, wu, wd, og_in, x, middle, normed1, normed2, qkv_in, attended, hidden, slope, params, d_terms,
    qkv_out, p_out, u_out, d_out, s_out, ret_out, ret_in,
    a_land, u_land, d_land, s_land, a_pieces, u_pieces, d_pieces, s_pieces,
    og, ug2, bg2, jn2, np2, n1p2, atp2, flip, qkv, ag, ob, xv, part, wdb, wb, tiles, hid, acc, s_d, s_u,
    stage_d, stage_u, stage_a, table, table_sib, s_s, stage_s, vec, ub,
    send, recv, local,
):
    io = Copies(send, recv, local)
    dp, z = io.dp, io.z
    t = og.shape[0]
    own, sib = pl.ds(0, t), pl.ds(t, t)
    core = (dp ^ 1, z)

    red_d = Reduce(io, d_out.shape[0], lambda j: s_d.at[j], d_land, d_pieces, stage_d, d_out)
    red_u = Reduce(io, u_out.shape[0], lambda j: s_u.at[j], u_land, u_pieces, stage_u, u_out)
    n_a = p_out.shape[0]

    def part_of_a(c):
        blocks = lambda j: ug2.at[pl.ds(j * 4 * n_a, 4 * n_a), pl.ds(c * D, D)]
        out = p_out if c == 3 else qkv_out.at[:, pl.ds(c * D, D)]
        return Reduce(io, n_a, blocks, a_land.at[c], a_pieces.at[c], stage_a, out, direct=c == 2)

    red_q, red_k, red_v, red_p = (part_of_a(c) for c in range(4))
    red_s = Reduce(io, s_out.shape[0], lambda j: s_s.at[j], s_land, s_pieces, stage_s, s_out, direct=True)
    back_in = HandBack(io, qkv.at[:, pl.ds(D, D)], ret_in)
    back_out = HandBack(io, ob, ret_out)

    def planes(src, dst):
        width = dst.shape[1] // 4
        return [
            io.load(
                src.at[:, pl.ds(pl.multiple_of((dp ^ (2 * j)) * width, LANES), width)],
                dst.at[own, pl.ds(j * width, width)],
            )
            for j in range(4)
        ]

    load_d = io.load(d_terms, s_d)
    load_og = io.load(og_in, og)
    load_x = [io.load(x, xv), io.load(middle, part)]
    meet(io)
    load_d.wait()
    red_d.start()

    def swap_planes(src, dst):
        width = dst.shape[1] // 4
        slots = io.slots(4)
        for j in range(4):
            io.start(
                slots[j],
                lambda j=j: src.at[:, pl.ds(pl.multiple_of((dp ^ (2 * j + 1)) * width, LANES), width)],
                lambda j=j: dst.at[sib, pl.ds(j * width, width)],
                core,
            )
        return [(slots[j], lambda j=j: dst.at[sib, pl.ds(j * width, width)]) for j in range(4)]

    swapped_2 = swap_planes(normed2, np2)
    d_rows = wdb.shape[1]
    w_rows = wb.shape[1]
    load_og.wait()

    acc[...] = jnp.zeros_like(acc)
    ug_slots = io.slots(FF // d_rows)

    def ug_copy(i):
        return io.remote(ug_slots[0] + i, ug2.at[own, lanes(i, d_rows)], ug2.at[sib, lanes(i, d_rows)], core)

    def hidden_step(i, slot):
        grad = dot_nt(og[...], wdb[slot]) * tiles[slot].astype(F32)
        low = grad.astype(BF)
        ug2[own, lanes(i, d_rows)] = low
        ub[:, lanes(i, d_rows)] = jnp.sum(low.astype(F32), axis=0, keepdims=True)
        ug_copy(i).start()
        acc[...] += dot(hid[slot], wdb[slot])

    stream(
        io,
        FF // d_rows,
        lambda i, slot: [
            (wd.at[pl.ds(pl.multiple_of(i * d_rows, d_rows), d_rows)], wdb.at[slot]),
            (slope.at[:, lanes(i, d_rows)], tiles.at[slot]),
            (hidden.at[:, lanes(i, d_rows)], hid.at[slot]),
        ],
        hidden_step,
    )
    for c in load_x:
        c.wait()
    ob[...] = (acc[...] + (part[...] - xv[...].astype(F32)) + params[7:8]).astype(BF)
    back_out.start()
    second = planes(normed2, np2)
    third = planes(normed1, n1p2) + planes(attended, atp2)
    third += [io.load(qkv_in, qkv)]
    swapped_1 = swap_planes(normed1, n1p2)
    swapped_3 = swap_planes(attended, atp2)

    for c in second:
        c.wait()
    for slot, ref in swapped_2:
        io.arrived(slot, ref)
    flip[...] = np2[...].T
    for i in range(FF // d_rows):
        ug_copy(i).wait_recv()

    def up_step(i, _):
        block = dot(flip[...], ug2[:, lanes(i, COLS)]).astype(BF)
        for j in range(4):
            s_u[j, :, lanes(i, COLS)] = block[j * LANES : (j + 1) * LANES]
        return 0

    lax.fori_loop(0, FF // COLS, up_step, 0)
    red_d.relay()
    red_u.start()

    def up_back(i, slot):
        acc[:, lanes(i, w_rows)] = dot_nt(ug2[own], wb[slot, :, 0:FF])

    w_tile = lambda ref, lo, n: lambda i, slot: [
        (ref.at[pl.ds(pl.multiple_of(i * w_rows, w_rows), w_rows), pl.ds(lo, n)], wb.at[slot, :, pl.ds(0, n)])
    ]
    stream(io, D // w_rows, w_tile(wu, 0, FF), up_back)
    for c in third:
        c.wait()
    vec[...] = jnp.zeros_like(vec)

    def second_norm(i, _):
        rows = pl.ds(pl.multiple_of(i * CHUNK, CHUNK), CHUNK)
        e = acc[rows]
        vhat, r = norm_rows(part[rows])
        g = e * params[5:6]
        grad = r * (
            g - jnp.mean(g, axis=-1, keepdims=True) - vhat * jnp.mean(g * vhat, axis=-1, keepdims=True)
        )
        vec[5:6] += jnp.sum(e * vhat, axis=0, keepdims=True)
        vec[6:7] += jnp.sum(e, axis=0, keepdims=True)
        part[rows] = grad
        out_grad = og[rows].astype(F32)
        low = (out_grad + grad).astype(BF)
        bg2[rows] = low
        vec[4:5] += jnp.sum(low.astype(F32), axis=0, keepdims=True)
        vec[7:8] += jnp.sum(out_grad, axis=0, keepdims=True)
        return 0

    lax.fori_loop(0, t // CHUNK, second_norm, 0)
    bg_slot = io.slots(1)[0]
    io.start(bg_slot, lambda: bg2.at[own], lambda: bg2.at[sib], core)

    def proj_back(i, slot):
        ag[:, lanes(i, w_rows)] = dot_nt(bg2[own], wb[slot, :, 0:D]).astype(BF)

    stream(io, D // w_rows, w_tile(wa, 3 * D, D), proj_back)
    for slot in range(FF // d_rows):
        ug_copy(slot).wait_send()
    for slot, ref in swapped_3:
        io.arrived(slot, ref)
    flip[...] = atp2[...].T
    io.arrived(bg_slot, lambda: bg2.at[sib])

    def proj_step(i, _):
        ug2[own, lanes(6 + i, COLS)] = dot(flip[...], bg2[:, lanes(i, COLS)]).astype(BF)
        return 0

    lax.fori_loop(0, D // COLS, proj_step, 0)
    red_p.start()

    def heads(i, _):
        def at(k):
            return lanes(k * (D // LANES) + i, LANES)

        dq, dk, dv = attend_back_pair(qkv[:, at(0)], qkv[:, at(1)], qkv[:, at(2)], ag[:, at(0)])
        for k, grad in enumerate((dq, dk, dv)):
            jn2[own, at(k)] = grad
        vec[2:3, at(0)] = jnp.sum(dq.astype(F32), axis=0, keepdims=True)
        vec[3:4, at(0)] = jnp.sum(dv.astype(F32), axis=0, keepdims=True)
        return 0

    n_pairs = D // LANES
    lax.fori_loop(0, n_pairs // 2, heads, 0)
    red_d.fold()
    lax.fori_loop(n_pairs // 2, n_pairs, heads, 0)
    jn_slot = io.slots(1)[0]
    io.start(jn_slot, lambda: jn2.at[own], lambda: jn2.at[sib], core)
    red_u.relay()
    red_d.cross()

    for slot, ref in swapped_1:
        io.arrived(slot, ref)
    flip[...] = n1p2[...].T

    def first_back(i, slot):
        acc[:, lanes(i, w_rows)] = dot_nt(jn2[own], wb[slot, :, 0 : 3 * D])

    stream(io, D // w_rows, w_tile(wa, 0, 3 * D), first_back)
    def first_norm(i, _):
        rows = pl.ds(pl.multiple_of(i * CHUNK, CHUNK), CHUNK)
        e = acc[rows]
        vhat, r = norm_rows(xv[rows].astype(F32))
        g = e * params[0:1]
        grad = r * (
            g - jnp.mean(g, axis=-1, keepdims=True) - vhat * jnp.mean(g * vhat, axis=-1, keepdims=True)
        )
        vec[0:1] += jnp.sum(e * vhat, axis=0, keepdims=True)
        vec[1:2] += jnp.sum(e, axis=0, keepdims=True)
        qkv[rows, D : 2 * D] = (part[rows] + grad).astype(BF)
        return 0

    lax.fori_loop(0, t // CHUNK, first_norm, 0)
    back_in.start()

    io.arrived(jn_slot, lambda: jn2.at[sib])

    def qkv_step(i, _):
        ug2[own, lanes(i, COLS)] = dot(flip[...], jn2[:, lanes(i, COLS)]).astype(BF)
        return 0

    for c, red in enumerate((red_q, red_k, red_v)):
        lax.fori_loop(c * D // COLS, (c + 1) * D // COLS, qkv_step, 0)
        red.start()
    red_p.relay()
    red_d.finish()

    spread_n = lax.broadcasted_iota(jnp.int32, (32, D), 0)
    spread_c = lax.broadcasted_iota(jnp.int32, (32, D), 1)
    mine = (spread_c // 32) == spread_n
    pick_c = lax.broadcasted_iota(jnp.int32, (D, LANES), 0)
    pick_l = lax.broadcasted_iota(jnp.int32, (D, LANES), 1)
    table[...] = jnp.zeros_like(table)
    for k in range(2):
        rows = jnp.zeros((32, LANES), F32)
        for q in range(4):
            spread = jnp.where(mine, vec[4 * k + q : 4 * k + q + 1], 0.0)
            pick = jnp.where(pick_l == 32 * q + pick_c % 32, 1.0, 0.0)
            rows = rows + jnp.dot(spread, pick, preferred_element_type=F32, precision=lax.Precision.HIGHEST)
        for n in range(32):
            table[8 * n + k : 8 * n + k + 1] = rows[n : n + 1]
    for n in range(32):
        table[8 * n + 2 : 8 * n + 3] = ub[:, n * LANES : (n + 1) * LANES]
    table_slot = io.slots(1)[0]
    io.start(table_slot, lambda: table, lambda: table_sib, core)

    io.arrived(table_slot, lambda: table_sib)
    for j in range(4):
        rows = pl.ds(pl.multiple_of((dp ^ (2 * j)) * 32, 32), 32)
        s_s[j] = table[rows] + table_sib[rows]
    red_s.start()

    red_u.fold()
    red_q.relay()
    red_k.relay()
    red_v.relay()
    red_s.relay()
    red_u.cross()
    red_p.fold()
    red_q.fold()
    red_k.fold()
    red_p.cross()
    red_v.fold()
    red_s.fold()
    red_q.cross()
    red_k.cross()
    for red in (red_u, red_p, red_q, red_k):
        red.finish()
    back_in.wait()
    back_out.wait()
    red_v.finish()
    red_s.finish()
    io.finish()


def backward(*saved):
    t = saved[3].shape[0]
    any_ = pl.BlockSpec(memory_space=pl.ANY)
    vmem = pl.BlockSpec(memory_space=pltpu.VMEM)
    sh = jax.ShapeDtypeStruct
    ra, rd, rs = D // 32, FF // 32, 8
    outs = [
        (sh((ra, 3 * D), F32), vmem),
        (sh((ra, D), F32), vmem),
        (sh((ra, FF), F32), vmem),
        (sh((rd, D), F32), vmem),
        (sh((rs, LANES), F32), vmem),
        (sh((4, t // 4, D), BF), any_),
        (sh((4, t // 4, D), BF), any_),
    ]
    for count, k in ((6, 2), (3, 1)):
        outs += [
            (sh((4, count, k * ra, D), BF), any_),
            (sh((count, k * ra, FF), BF), any_),
            (sh((count, k * rd, D), BF), any_),
            (sh((count, k * rs, LANES), F32), any_),
        ]
    v = pltpu.VMEM
    results = pl.pallas_call(
        backward_kernel,
        out_shape=[o for o, _ in outs],
        in_specs=[any_] * 12 + [vmem, any_],
        out_specs=[o for _, o in outs],
        scratch_shapes=[
            v((t, D), BF),
            v((2 * t, FF), BF),
            v((2 * t, D), BF),
            v((2 * t, 3 * D), BF),
            v((2 * t, D // 2), BF),
            v((2 * t, D // 2), BF),
            v((2 * t, D // 2), BF),
            v((D // 2, 2 * t), BF),
            v((t, 3 * D), BF),
            v((t, D), BF),
            v((t, D), BF),
            v((t, D), BF),
            v((t, D), F32),
            v((2, 512, D), BF),
            v((2, 256, FF), BF),
            v((2, t, 512), BF),
            v((2, t, 512), BF),
            v((t, D), F32),
            v((4, 4 * rd, D), BF),
            v((4, 4 * ra, FF), BF),
            v((2, 2 * rd, D), BF),
            v((2, 2 * ra, FF), BF),
            v((2, 2 * ra, D), BF),
            v((32 * rs, LANES), F32),
            v((32 * rs, LANES), F32),
            v((4, 4 * rs, LANES), F32),
            v((2, 2 * rs, LANES), F32),
            v((8, D), F32),
            v((1, FF), F32),
            pltpu.SemaphoreType.DMA((N_BACK,)),
            pltpu.SemaphoreType.DMA((N_BACK,)),
            pltpu.SemaphoreType.DMA((N_LOCAL,)),
        ],
        compiler_params=pltpu.CompilerParams(
            collective_id=1, has_side_effects=True, vmem_limit_bytes=60 * 2**20
        ),
    )(*saved)
    return results[:7]


def norm_parts(v):
    center = v - jnp.mean(v, axis=-1, keepdims=True)
    r = lax.rsqrt(jnp.mean(center * center, axis=-1, keepdims=True) + EPSILON)
    return center * r, r


def norm_back(vhat, r, gain, e):
    t = e * gain
    grad = r * (
        t - jnp.mean(t, axis=-1, keepdims=True) - vhat * jnp.mean(t * vhat, axis=-1, keepdims=True)
    )
    return grad, jnp.sum(e * vhat, axis=0), jnp.sum(e, axis=0)


SMALL = (D, D, D, D, D, D, D, D, FF)


def per_device(
    n_dp,
    n_seq,
    clips,
    counts,
    out_cotangent,
    norm1_gain,
    norm1_shift,
    qkv_weight,
    query_bias,
    value_bias,
    proj_weight,
    proj_bias,
    norm2_gain,
    norm2_shift,
    up_weight,
    up_bias,
    down_weight,
    down_bias,
):
    links = Links(n_dp, n_seq)
    n = n_dp * n_seq
    slots = clips.shape[0]
    rows = D // n
    small = (
        norm1_gain,
        norm1_shift,
        query_bias,
        value_bias,
        proj_bias,
        norm2_gain,
        norm2_shift,
        down_bias,
        up_bias,
    )
    packed = jnp.concatenate(small)
    packed = jnp.pad(packed, (0, rows * LANES - packed.shape[0])).reshape(rows, LANES)

    living = (jnp.arange(slots) < counts[0]).astype(F32)[:, None, None]
    living_cot = living * out_cotangent
    if links.short:
        living_rows = jnp.broadcast_to(living.reshape(slots, 1), (slots, LANES))
        flat = lambda w: w.reshape(-1, LANES)
        saved = forward(
            flat(qkv_weight),
            flat(proj_weight),
            packed,
            flat(up_weight),
            flat(down_weight),
            clips,
            out_cotangent,
            living_rows,
        )
        qkv_grad, proj_grad, up_grad, down_grad, small_grad, out_back, in_back = backward(*saved)
        out_home, in_home = links.by_clip(out_back, slots), links.by_clip(in_back, slots)
        small_out = small_grad[:3].reshape(-1)
    else:
        shard_a = jnp.concatenate(
            [qkv_weight.reshape(rows, 3 * D), proj_weight.reshape(rows, D), packed], axis=1
        ).astype(BF)
        shard_u = up_weight.reshape(rows, FF).astype(BF)
        shard_d = down_weight.reshape(FF // n, D).astype(BF)
        a_mat, u_mat, d_mat = (links.gather(shard) for shard in (shard_a, shard_u, shard_d))
        x, out_grad = (links.collect(t.astype(BF)) for t in (clips, living_cot))
        x = x.astype(F32)

        table = a_mat[:, 4 * D :].reshape(n_dp, n_seq, rows * LANES)
        table = table.reshape(n, rows * LANES).astype(F32)
        vectors, at = [], 0
        for size in SMALL:
            vectors.append(table[:, at : at + size // n].reshape(size))
            at += size // n
        gain1, shift1, q_bias, v_bias, p_bias, gain2, shift2, d_bias, u_bias = vectors

        vhat1, r1 = norm_parts(x)
        normed1 = (vhat1 * gain1 + shift1).astype(BF)
        qkv_bias = jnp.concatenate([q_bias, jnp.zeros_like(q_bias), v_bias])
        qkv_mat, proj_mat = a_mat[:, : 3 * D], a_mat[:, 3 * D : 4 * D]
        qkv = (dot(normed1, qkv_mat) + qkv_bias).astype(BF)
        attended = attend(qkv)
        branch = dot(attended, proj_mat) + p_bias
        middle = x + branch
        vhat2, r2 = norm_parts(middle)
        normed2 = (vhat2 * gain2 + shift2).astype(BF)
        hidden, slope = gelu_both(dot(normed2, u_mat) + u_bias)
        hidden = hidden.astype(BF)
        slope = slope.astype(BF)
        out_part = branch + dot(hidden, d_mat) + d_bias
        out_home = links.hand_back(out_part.astype(BF), slots)
        down_grad = links.reduce(dot_tn(hidden, out_grad))
        upper_grad = (dot_nt(out_grad, d_mat) * slope).astype(BF)
        up_grad = links.reduce(dot_tn(normed2, upper_grad))
        part, gain2_grad, shift2_grad = norm_back(vhat2, r2, gain2, dot_nt(upper_grad, u_mat))
        branch_grad = (out_grad.astype(F32) + part).astype(BF)
        dq, dk, dv = attend_back(qkv, dot_nt(branch_grad, proj_mat).astype(BF))
        joined = jnp.concatenate([dq, dk, dv], axis=1)
        first_part, gain1_grad, shift1_grad = norm_back(vhat1, r1, gain1, dot_nt(joined, qkv_mat))
        in_home = links.hand_back((part + first_part).astype(BF), slots)
        total = lambda g: jnp.sum(g.astype(F32), axis=0)
        small_grads = (
            gain1_grad,
            shift1_grad,
            total(dq),
            total(dv),
            total(branch_grad),
            gain2_grad,
            shift2_grad,
            total(out_grad),
            total(upper_grad),
        )
        grad_table = jnp.concatenate([g.reshape(n, -1) for g in small_grads], axis=1)
        width = grad_table.shape[1]
        grad_table = jnp.pad(grad_table, ((0, 0), (0, rows * LANES - width)))
        d_a = [dot_tn(normed1, joined), dot_tn(attended, branch_grad), grad_table.reshape(n * rows, LANES)]
        a_grad = links.reduce(jnp.concatenate(d_a, axis=1))
        qkv_grad, proj_grad = a_grad[:, : 3 * D], a_grad[:, 3 * D : 4 * D]
        small_out = a_grad[:, 4 * D :].reshape(-1)
    block_out = living * (clips + out_home.astype(F32))
    input_grad = living_cot + in_home.astype(F32)
    pieces, at = [], 0
    for size in SMALL:
        pieces.append(small_out[at : at + size // n])
        at += size // n
    g1, s1, qb, vb, pb, g2, s2, db, ub = pieces
    return (
        block_out,
        input_grad,
        g1,
        s1,
        qkv_grad.reshape(-1),
        qb,
        vb,
        proj_grad.reshape(-1),
        pb,
        g2,
        s2,
        up_grad.reshape(-1),
        ub,
        down_grad.reshape(-1),
        db,
    )


def solution(mesh):
    flat = P(AXES)
    tokens = P("dp", "seq", None)
    return jax.shard_map(
        functools.partial(per_device, mesh.shape["dp"], mesh.shape["seq"]),
        mesh=mesh,
        in_specs=(tokens, P("dp"), tokens) + (flat,) * 13,
        out_specs=(tokens, tokens) + (flat,) * 13,
        check_vma=False,
    )
```
